32 devices in a mesh: rep: 8 (over y, x, core), fsdp: 4 (over z).
Axes of the slice: x: 2, y: 2, z: 4, core: 2. Of those that a mesh axis runs over, the one named last changes fastest.
Arguments:
- inputs: bfloat16 [16, 1024, 1024], P('rep', 'fsdp'), may hold values from -6 to 6
- cotangent: bfloat16 [16, 1024, 1024], P('rep', 'fsdp'), may hold values from -6 to 6
- lengths: int32 [16], P('rep'), may hold values from 256 to 1024, as said below
- norm_first: bfloat16 [1024], P('fsdp'), may hold values from 0.5 to 1.5
- w_qkv: bfloat16 [1024, 3072], P('fsdp'), may hold values from -0.1875 to 0.1875
- w_out: bfloat16 [1024, 1024], P('fsdp'), may hold values from -1.5 to 1.5
- norm_second: bfloat16 [1024], P('fsdp'), may hold values from 0.5 to 1.5
- w_in: bfloat16 [1024, 5248], P('fsdp'), may hold values from -0.1875 to 0.1875
- w_down: bfloat16 [2624, 1024], P('fsdp'), may hold values from -0.15625 to 0.15625
Outputs:
- output: bfloat16 [16, 1024, 1024], P('rep', 'fsdp')
- grad_inputs: bfloat16 [16, 1024, 1024], P('rep', 'fsdp')
- grad_norm_first: float32 [1024], P('fsdp')
- grad_w_qkv: float32 [1024, 3072], P('fsdp')
- grad_w_out: float32 [1024, 1024], P('fsdp')
- grad_norm_second: float32 [1024], P('fsdp')
- grad_w_in: float32 [1024, 5248], P('fsdp')
- grad_w_down: float32 [2624, 1024], P('fsdp')
The draws below stay inside these ranges and needn't reach their ends.
Inputs may be any that keep to these rules, and one draw needn't show every extreme that they name: `lengths`: in each aligned group of 2 sequences (those of one index of rep) at least one has length 1024.
All inputs are finite; a program needn't handle non-finite values.
Results may differ from the reference program's by a relative error of at most 0.022.
Values may be sent and summed in bfloat16 or wider, within the bound.
No kernel may reach another device: no remote copies, remote signals or barrier semaphores. Data moves between devices by JAX's collectives and lax.ppermute only.
A program may use at most 192 MiB of HBM per device.

```python
import jax
import jax.numpy as jnp
from jax import lax

D = 1024
HEAD_DIM = 64
FF = 2624
WIN = 64
SEQ_GRP = 2
SEQ_LEN = 1024
SEQS = 16


def draw_lengths(key, part):
    key = jax.random.fold_in(key, 11)
    key_slot, key_other = jax.random.split(key)
    groups = SEQS // SEQ_GRP
    full_slot = jax.random.randint(key_slot, (groups, 1), 0, SEQ_GRP)
    others = jax.random.randint(key_other, (groups, SEQ_GRP), SEQ_LEN // 4, SEQ_LEN + 1)
    slot_ids = jnp.arange(SEQ_GRP)[None, :]
    result = jnp.where(slot_ids == full_slot, SEQ_LEN, others)
    return result.reshape(SEQS).astype(jnp.int32)


def steps_of(stream_key, extent, cuts, low, top_value):
    level = 1.0
    for position, shards_of in cuts:
        draws = jax.random.uniform(jax.random.fold_in(jax.random.fold_in(stream_key, 6), position), (shards_of,), jnp.float32, low / len(cuts), top_value / len(cuts))
        level = level * jnp.repeat(jnp.exp(draws), extent[position] // shards_of).reshape((-1,) + (1,) * (len(extent) - 1 - position))
    return level


def bell_draw(stream_key, extent, spread, bound, pieces=(), kind=jnp.bfloat16):
    factor_of = steps_of(stream_key, extent, pieces, -0.22, 0.18) if pieces else 1.0
    values = jax.random.normal(stream_key, extent, jnp.float32) * spread * factor_of
    return jnp.minimum(jnp.maximum(values, -bound), bound).astype(kind)


def setup_inputs(seed: int = 0) -> dict:
    key_list = jax.random.split(jax.random.key(seed), 10)
    return {
        "inputs": bell_draw(key_list[0], (SEQS, SEQ_LEN, D), 1.0, 6.0, ((0, 8), (1, 4))),
        "cotangent": bell_draw(key_list[1], (SEQS, SEQ_LEN, D), 1.0, 6.0, ((0, 8), (1, 4))),
        "lengths": draw_lengths(jax.random.fold_in(key_list[9], 71), 0),
        "norm_first": jnp.clip(1.0 + 0.1 * jax.random.normal(key_list[3], (D,), jnp.float32), 0.5, 1.5).astype(jnp.bfloat16),
        "w_qkv": bell_draw(key_list[4], (D, 3 * D), D ** -0.5, 0.1875, ((0, 4),)),
        "w_out": bell_draw(key_list[5], (D, D), (D // 64) ** -0.5, 1.5, ((0, 4),)),
        "norm_second": jnp.clip(1.0 + 0.1 * jax.random.normal(key_list[6], (D,), jnp.float32), 0.5, 1.5).astype(jnp.bfloat16),
        "w_in": bell_draw(key_list[7], (D, 2 * FF), D ** -0.5, 0.1875, ((0, 4),)),
        "w_down": bell_draw(key_list[8], (FF, D), (FF // 2) ** -0.5, 0.15625, ((0, 4),)),
    }


@jax.custom_vjp
def low(v):
    return lax.optimization_barrier(v.astype(jnp.bfloat16)).astype(jnp.float32)

@jax.custom_vjp
def low_back(v):
    return v

def low_keep(v):
    return (low(v), None)

def low_pass(kept, grad):
    return (grad,)

def back_keep(v):
    return (v, None)

def back_low(kept, grad):
    return (low(grad),)
low.defvjp(low_keep, low_pass)
low_back.defvjp(back_keep, back_low)
highest = lax.Precision.HIGHEST
epsilon = 1e-05

def matmul(left, right):
    return jnp.dot(left, right, precision=highest, preferred_element_type=jnp.float32)

def layer_norm(values, gain):
    centred = values - lax.optimization_barrier(jnp.mean(values, axis=-1, keepdims=True))
    scaled = centred * lax.rsqrt(lax.optimization_barrier(jnp.mean(centred * centred, axis=-1, keepdims=True)) + epsilon)
    return scaled * gain

def rotary(values, positions):
    halfway = HEAD_DIM // 2
    frequency = 10000.0 ** (-(2.0 * jnp.arange(halfway, dtype=jnp.float32)) / HEAD_DIM)
    angles = positions.astype(jnp.float32)[:, None] * frequency[None, :]
    angles = jnp.concatenate([angles, angles], axis=-1)
    cosine = jnp.cos(angles)[:, None, :]
    sine_table = jnp.sin(angles)[:, None, :]
    rotated = jnp.concatenate([-values[..., halfway:], values[..., :halfway]], axis=-1)
    return values * cosine + rotated * sine_table

def attend(queries, keys, values, length):
    total_rows = queries.shape[0]
    block_rows = min(512, total_rows)
    block_count = total_rows // block_rows
    keys_pad = jnp.pad(keys, ((WIN, WIN), (0, 0), (0, 0)))
    values_pad = jnp.pad(values, ((WIN, WIN), (0, 0), (0, 0)))

    def one_block(block_index):
        block_start = block_index * block_rows
        query_blk = lax.dynamic_slice_in_dim(queries, block_start, block_rows, 0)
        key_blk = lax.dynamic_slice_in_dim(keys_pad, block_start, block_rows + 2 * WIN, 0)
        value_blk = lax.dynamic_slice_in_dim(values_pad, block_start, block_rows + 2 * WIN, 0)
        scores = jnp.einsum('qhd,khd->hqk', query_blk, key_blk, precision=highest) * HEAD_DIM ** (-0.5)
        scores = low_back(scores)
        query_pos = block_start + jnp.arange(block_rows, dtype=jnp.int32)
        key_pos = block_start - WIN + jnp.arange(block_rows + 2 * WIN, dtype=jnp.int32)
        key_live = (key_pos >= 0) & (key_pos < length)
        allowed = (jnp.abs(query_pos[:, None] - key_pos[None, :]) <= WIN) & (key_live[None, :] | (query_pos[:, None] == key_pos[None, :]))
        masked = jnp.where(allowed[None], scores, -1e+30)
        row_peak = lax.optimization_barrier(jnp.max(masked, axis=-1, keepdims=True))
        exponent = jnp.exp(masked - row_peak)
        softmax_out = exponent / lax.optimization_barrier(jnp.sum(exponent, axis=-1, keepdims=True))
        softmax_out = low(softmax_out)
        return jnp.einsum('hqk,khd->qhd', softmax_out, value_blk, precision=highest)
    outputs = lax.map(jax.checkpoint(one_block), jnp.arange(block_count, dtype=jnp.int32))
    return outputs.reshape(total_rows, D)

def layer_apply(params, inputs, length):
    norm_first, w_qkv, w_out, norm_second, w_in, w_down = params
    total_rows = inputs.shape[0]
    head_count = D // HEAD_DIM
    positions = jnp.arange(total_rows, dtype=jnp.int32)
    valid_rows = (positions < length).astype(jnp.float32)[:, None]
    normed = low(layer_norm(inputs, norm_first))
    joint_qkv = low_back(matmul(normed, w_qkv))
    queries = joint_qkv[:, :D].reshape(total_rows, head_count, HEAD_DIM)
    keys = joint_qkv[:, D:2 * D].reshape(total_rows, head_count, HEAD_DIM)
    values = joint_qkv[:, 2 * D:].reshape(total_rows, head_count, HEAD_DIM)
    queries = low(rotary(queries, positions))
    keys = low(rotary(keys, positions))
    values = low(values)
    attended = low(low_back(attend(queries, keys, values, length)))
    branch = low_back(matmul(attended, w_out))
    middle = inputs + valid_rows * branch
    normed_second = low(layer_norm(middle, norm_second))
    hidden = low_back(matmul(normed_second, w_in))
    mixed_low = low(jax.nn.gelu(hidden[:, :FF], approximate=False) * hidden[:, FF:])
    result = low_back(matmul(mixed_low, w_down))
    return middle + valid_rows * result

def reference(inputs, cotangent, lengths, norm_first, w_qkv, w_out, norm_second, w_in, w_down):
    params = tuple((weight.astype(jnp.float32) for weight in (norm_first, w_qkv, w_out, norm_second, w_in, w_down)))

    def sequence_step(totals, item):
        seq_inputs, seq_cotangent, seq_length = item

        def forward(weights_in, values_in):
            return layer_apply(weights_in, values_in, seq_length)
        outputs, pullback = jax.vjp(forward, params, seq_inputs.astype(jnp.float32))
        grads, grad_values = pullback(seq_cotangent.astype(jnp.float32))
        totals = jax.tree.map(lambda left, right: left + right, totals, grads)
        return (totals, (outputs.astype(jnp.bfloat16), grad_values.astype(jnp.bfloat16)))
    zero_grads = tuple((jnp.zeros_like(weight) for weight in params))
    totals, stacked = lax.scan(sequence_step, zero_grads, (inputs, cotangent, lengths))
    return (stacked[0], stacked[1], totals[0], totals[1], totals[2], totals[3], totals[4], totals[5])
```

```python
import functools

import jax
import jax.numpy as jnp
from jax import lax
from jax.experimental import pallas as pl
from jax.experimental.pallas import tpu as pltpu
from jax.sharding import PartitionSpec as P

HEAD_DIM = 64
WIN = 64
BLOCK_Q = 128
LANES = 128

epsilon = 1e-05
root_half = 0.7071067811865476
inv_root_two_pi = 0.3989422804014327
f32 = jnp.float32
bf16 = jnp.bfloat16
VMEM_LIMIT = 48 * 1024 * 1024


def bit_count():
    return lax.axis_size("rep").bit_length() - 1


def axis_of(bit):
    return 0 if bit == 0 else bit_count() - bit


def bit_value(bit):
    return (lax.axis_index("rep") >> bit) & 1


def piece_number():
    bits = bit_count()
    return sum(bit_value(bit) << (bits - 1 - axis_of(bit)) for bit in range(bits))


def flip(value, bit):
    size = lax.axis_size("rep")
    return lax.ppermute(value, "rep", [(i, i ^ (1 << bit)) for i in range(size)])


def turn(value, steps):
    size = lax.axis_size("fsdp")
    return lax.ppermute(value, "fsdp", [(i, (i + steps) % size) for i in range(size)])


def link_orders():
    bits = list(range(1, bit_count()))
    return bits, bits[::-1]


def widen(state, bit):
    axis = axis_of(bit)
    got = flip(state, bit)
    first = bit_value(bit) == 0
    return jnp.concatenate(
        [jnp.where(first, state, got), jnp.where(first, got, state)], axis=axis
    )


def spread(parts):
    results = []
    for part, order in zip(parts, link_orders()):
        state = part[(None,) * bit_count()]
        for bit in order + [0]:
            state = widen(state, bit)
        results.append(state)
    return results


def fold(state, first_axis, order):
    axes = {bit: first_axis + axis_of(bit) - 1 for bit in order}
    for bit in order:
        mine = bit_value(bit)
        keep = lax.dynamic_slice_in_dim(state, mine, 1, axes[bit])
        give = lax.dynamic_slice_in_dim(state, 1 - mine, 1, axes[bit])
        state = (keep.astype(f32) + flip(give, bit).astype(f32)).astype(bf16)
    return state


def to_owner(state):
    size = lax.axis_size("fsdp")
    me = lax.axis_index("fsdp")
    total = lax.dynamic_index_in_dim(state, me, 0, False).astype(f32)
    for steps in range(1, size):
        give = lax.dynamic_index_in_dim(state, lax.rem(me + steps, size), 0, False)
        total = total + turn(give, steps).astype(f32)
    return total.astype(bf16)


def half_columns(width):
    return width // 2 // LANES * LANES


def half_rows(rows):
    return -(-rows // 2 // 16) * 16


def place(shard, others, pad_rows=0):
    size = lax.axis_size("fsdp")
    me = lax.axis_index("fsdp")
    rows = shard.shape[0]
    whole = jnp.zeros((size * rows + pad_rows, shard.shape[1]), shard.dtype)
    whole = lax.dynamic_update_slice(whole, shard, (me * rows, 0))
    for steps in range(1, size):
        source = lax.rem(me - steps + size, size)
        whole = lax.dynamic_update_slice(whole, others[steps - 1], (source * rows, 0))
    return whole


def gather_rows(shard):
    pieces = lax.axis_size("rep")
    size = lax.axis_size("fsdp")
    rows = shard.shape[0] // pieces
    piece = lax.dynamic_slice_in_dim(shard, piece_number() * rows, rows, 0)
    came = jnp.stack([turn(piece, steps) for steps in range(1, size)])
    cut = half_columns(shard.shape[1])
    left, right = spread((came[:, :, :cut], came[:, :, cut:]))
    joined = jnp.concatenate([left, right], axis=-1)
    joined = jnp.moveaxis(joined, bit_count(), 0).reshape((size - 1,) + shard.shape)
    return place(shard, joined)


def gather_columns(shard, pad_rows):
    pieces = lax.axis_size("rep")
    size = lax.axis_size("fsdp")
    rows, width = shard.shape
    columns = width // pieces
    piece = lax.dynamic_slice_in_dim(shard, piece_number() * columns, columns, 1)
    came = jnp.stack([turn(piece, steps) for steps in range(1, size)])
    cut = half_rows(rows)
    upper, lower = spread((came[:, :cut], came[:, cut:]))
    joined = jnp.concatenate([upper, lower], axis=-2)
    joined = joined.reshape((pieces, size - 1, rows, columns))
    joined = jnp.transpose(joined, (1, 2, 0, 3)).reshape((size - 1, rows, width))
    return place(shard, joined, pad_rows)


def tokens_dot(left, right):
    return lax.dot_general(left, right, (((0,), (0,)), ((), ())), preferred_element_type=f32)


def pair_sum(left, right, split_left):
    size = lax.axis_size("fsdp")

    def half(which):
        if split_left:
            view = left.reshape(left.shape[0], size, 2, -1)
            part = lax.dynamic_index_in_dim(view, which, 2, False)
            return tokens_dot(part.reshape(left.shape[0], -1), right)
        width = right.shape[1] // 2
        return tokens_dot(left, lax.dynamic_slice_in_dim(right, which * width, width, 1))

    mine = bit_value(0)
    got = flip(half(1 - mine).astype(bf16), 0)
    return (half(mine) + got.astype(f32)).astype(bf16)


def reduce_rows(state):
    size = lax.axis_size("fsdp")
    links = bit_count() - 1
    width = state.shape[1]
    cut = half_columns(width)
    state = state.reshape((size,) + (2,) * links + (-1, width))
    parts = []
    for part, order in zip((state[..., :cut], state[..., cut:]), link_orders()):
        parts.append(fold(part, 1, order).reshape(size, -1, part.shape[-1]))
    owned = to_owner(jnp.concatenate(parts, axis=-1))
    left, right = spread((owned[:, :cut], owned[:, cut:]))
    return jnp.concatenate([left, right], axis=-1).reshape(-1, width).astype(f32)


def reduce_columns(state):
    size = lax.axis_size("fsdp")
    links = bit_count() - 1
    rows = state.shape[0] // size
    cut = half_rows(rows)
    columns = state.shape[1] // (1 << links)
    state = state.reshape((size, rows) + (2,) * links + (columns,))
    parts = []
    for part, order in zip((state[:, :cut], state[:, cut:]), link_orders()):
        parts.append(fold(part, 2, order).reshape(size, -1, columns))
    owned = to_owner(jnp.concatenate(parts, axis=1))
    upper, lower = spread((owned[:cut], owned[cut:]))
    joined = jnp.concatenate([upper, lower], axis=-2).reshape(-1, rows, columns)
    return jnp.transpose(joined, (1, 0, 2)).reshape(rows, -1).astype(f32)


def neighbours(up, down):
    size = lax.axis_size("fsdp")
    forward = [(i, i + 1) for i in range(size - 1)]
    backward = [(i + 1, i) for i in range(size - 1)]
    return lax.ppermute(up, "fsdp", backward), lax.ppermute(down, "fsdp", forward)


def params(*semantics):
    return pltpu.CompilerParams(
        dimension_semantics=semantics, vmem_limit_bytes=VMEM_LIMIT
    )


def cost(flops, nbytes):
    return pl.CostEstimate(flops=int(flops), bytes_accessed=int(nbytes), transcendentals=0)


def dot_nn(left, right):
    return jnp.dot(left, right, preferred_element_type=f32)


def dot_nt(left, right):
    return lax.dot_general(left, right, (((1,), (1,)), ((), ())), preferred_element_type=f32)


def normalized(values):
    centred = values - jnp.mean(values, axis=-1, keepdims=True)
    inverse = lax.rsqrt(jnp.mean(centred * centred, axis=-1, keepdims=True) + epsilon)
    return centred * inverse, inverse


def norm_back(grad_out, gain, scaled, inverse):
    grad_scaled = grad_out * gain
    return inverse * (
        grad_scaled
        - jnp.mean(grad_scaled, axis=-1, keepdims=True)
        - scaled * jnp.mean(grad_scaled * scaled, axis=-1, keepdims=True)
    )


def swapped_halves(values):
    width = values.shape[-1]
    lane = lax.broadcasted_iota(jnp.int32, values.shape, values.ndim - 1)
    ahead = pltpu.roll(values, width - HEAD_DIM // 2, values.ndim - 1)
    behind = pltpu.roll(values, HEAD_DIM // 2, values.ndim - 1)
    return jnp.where(lane % HEAD_DIM < HEAD_DIM // 2, ahead, behind)


def qkv_kernel(x_ref, gain_ref, w_ref, cos_ref, sin_ref, normed_ref, out_ref, *, rope_steps):
    step = pl.program_id(0)

    @pl.when(step == 0)
    def _():
        scaled, _inverse = normalized(x_ref[...].astype(f32))
        normed_ref[...] = (scaled * gain_ref[...]).astype(bf16)

    product = dot_nn(normed_ref[...], w_ref[...])

    @pl.when(step >= rope_steps)
    def _():
        out_ref[0] = product.astype(bf16)

    @pl.when(step < rope_steps)
    def _():
        seq_rows = cos_ref.shape[0]
        cosine, sine = cos_ref[...], sin_ref[...]
        for top in range(0, product.shape[0], seq_rows):
            for lane in range(0, product.shape[1], LANES):
                tile = product[top : top + seq_rows, lane : lane + LANES]
                out_ref[0, top : top + seq_rows, lane : lane + LANES] = (
                    tile * cosine + swapped_halves(tile) * sine
                ).astype(bf16)


def qkv_call(x, gain, weight, cosine, sine):
    rows, width = x.shape
    block = 512
    per_plane = width // block
    return pl.pallas_call(
        functools.partial(qkv_kernel, rope_steps=2 * per_plane),
        grid=(3 * per_plane,),
        in_specs=[
            pl.BlockSpec((rows, width), lambda i: (0, 0)),
            pl.BlockSpec((1, width), lambda i: (0, 0)),
            pl.BlockSpec((width, block), lambda i: (0, i)),
            pl.BlockSpec(cosine.shape, lambda i: (0, 0)),
            pl.BlockSpec(sine.shape, lambda i: (0, 0)),
        ],
        out_specs=[
            pl.BlockSpec((rows, width), lambda i: (0, 0)),
            pl.BlockSpec((1, rows, block), lambda i: (i // per_plane, 0, i % per_plane)),
        ],
        out_shape=[
            jax.ShapeDtypeStruct((rows, width), bf16),
            jax.ShapeDtypeStruct((3, rows, width), bf16),
        ],
        compiler_params=params("arbitrary"),
        cost_estimate=cost(6 * rows * width * width, 6 * width * width + 10 * rows * width),
        name="qkv",
    )(x, gain, weight, cosine, sine)


def head_masks():
    lane = lax.broadcasted_iota(jnp.int32, (1, LANES), 1)
    first = lane < HEAD_DIM
    return first, first.astype(f32).astype(bf16), (~first).astype(f32).astype(bf16)


def two_heads(tile, low_mask, high_mask):
    return jnp.concatenate([tile * low_mask, tile * high_mask], axis=0)


def score_bias(first_row, length):
    shape = (BLOCK_Q, BLOCK_Q + 2 * WIN)
    query = first_row + lax.broadcasted_iota(jnp.int32, shape, 0)
    key = first_row - WIN + lax.broadcasted_iota(jnp.int32, shape, 1)
    near = jnp.abs(query - key) <= WIN
    live = (key >= 0) & (key < length)
    bias = jnp.where(near & (live | (query == key)), 0.0, -1e30).astype(f32)
    return jnp.concatenate([bias, bias], axis=0)


def softmax_of(queries, keys, bias):
    scores = dot_nt(queries, keys) * (HEAD_DIM**-0.5) + bias
    exponent = jnp.exp(scores - jnp.max(scores, axis=-1, keepdims=True))
    return exponent / jnp.sum(exponent, axis=-1, keepdims=True)


def attend_kernel(
    meta_ref, q_ref, k_ref, v_ref, k_up_ref, v_up_ref, k_down_ref, v_down_ref, out_ref
):
    length = meta_ref[1 + pl.program_id(0)]
    rows, width = q_ref.shape[1:]
    first_head, low_mask, high_mask = head_masks()
    for lane in range(0, width, LANES):
        lanes = slice(lane, lane + LANES)
        keys = jnp.concatenate([k_up_ref[0, :, lanes], k_ref[0, :, lanes], k_down_ref[0, :, lanes]], 0)
        values = jnp.concatenate([v_up_ref[0, :, lanes], v_ref[0, :, lanes], v_down_ref[0, :, lanes]], 0)
        for top in range(0, rows, BLOCK_Q):
            bias = score_bias(meta_ref[0] + top, length)
            span = slice(top, top + BLOCK_Q + 2 * WIN)
            queries = two_heads(q_ref[0, top : top + BLOCK_Q, lanes], low_mask, high_mask)
            probs = softmax_of(queries, keys[span], bias).astype(bf16)
            result = dot_nn(probs, values[span])
            out_ref[top : top + BLOCK_Q, lanes] = jnp.where(
                first_head, result[:BLOCK_Q], result[BLOCK_Q:]
            ).astype(bf16)


def attention_specs(seqs, seq_rows, width, block):
    own = lambda plane: pl.BlockSpec((1, seq_rows, block), lambda s, h: (plane, s, h))
    rim = lambda plane: pl.BlockSpec((1, WIN, block), lambda s, h: (plane, s, h))
    flat = pl.BlockSpec((seq_rows, block), lambda s, h: (s, h))
    return own, rim, flat


def attend_call(meta, qkv, rim_up, rim_down, seqs):
    _, rows, width = qkv.shape
    seq_rows = rows // seqs
    block = 256
    own, rim, flat = attention_specs(seqs, seq_rows, width, block)
    return pl.pallas_call(
        attend_kernel,
        grid=(seqs, width // block),
        in_specs=[pl.BlockSpec(memory_space=pltpu.SMEM), own(0), own(1), own(2), rim(0), rim(1), rim(0), rim(1)],
        out_specs=flat,
        out_shape=jax.ShapeDtypeStruct((rows, width), bf16),
        compiler_params=params("arbitrary", "arbitrary"),
        cost_estimate=cost(8 * rows * width * (BLOCK_Q + 2 * WIN), 10 * rows * width),
        name="attend",
    )(meta, qkv, qkv, qkv, rim_up, rim_up, rim_down, rim_down)


def attend_back_kernel(
    meta_ref,
    q_ref,
    k_ref,
    v_ref,
    k_up_ref,
    v_up_ref,
    k_down_ref,
    v_down_ref,
    go_ref,
    cos_ref,
    sin_ref,
    gq_ref,
    gk_ref,
    gv_ref,
    up_ref,
    down_ref,
    gk_acc,
    gv_acc,
):
    length = meta_ref[1 + pl.program_id(0)]
    rows, width = q_ref.shape[1:]
    scale = HEAD_DIM**-0.5
    first_head, low_mask, high_mask = head_masks()

    def turned_back(tile, span):
        return tile * cos_ref[span, :] - swapped_halves(tile) * sin_ref[span, :]

    for lane in range(0, width, LANES):
        lanes = slice(lane, lane + LANES)
        keys = jnp.concatenate([k_up_ref[0, :, lanes], k_ref[0, :, lanes], k_down_ref[0, :, lanes]], 0)
        values = jnp.concatenate([v_up_ref[0, :, lanes], v_ref[0, :, lanes], v_down_ref[0, :, lanes]], 0)
        gk_acc[...] = jnp.zeros_like(gk_acc)
        gv_acc[...] = jnp.zeros_like(gv_acc)
        for top in range(0, rows, BLOCK_Q):
            bias = score_bias(meta_ref[0] + top, length)
            span = slice(top, top + BLOCK_Q + 2 * WIN)
            queries = two_heads(q_ref[0, top : top + BLOCK_Q, lanes], low_mask, high_mask)
            grads = two_heads(go_ref[top : top + BLOCK_Q, lanes], low_mask, high_mask)
            probs = softmax_of(queries, keys[span], bias)
            grad_probs = dot_nt(grads, values[span])
            delta = jnp.sum(probs * grad_probs, axis=-1, keepdims=True)
            grad_scores = (probs * (grad_probs - delta)).astype(bf16)
            result = dot_nn(grad_scores, keys[span])
            result = jnp.where(first_head, result[:BLOCK_Q], result[BLOCK_Q:]) * scale
            own = slice(WIN + top, WIN + top + BLOCK_Q)
            gq_ref[top : top + BLOCK_Q, lanes] = turned_back(result, own).astype(bf16)
            gk_acc[span, :] += tokens_dot(grad_scores, queries)
            gv_acc[span, :] += tokens_dot(probs.astype(bf16), grads)
        grad_keys = turned_back(gk_acc[...] * scale, slice(None))
        grad_values = gv_acc[...]
        up_ref[0, :, lanes] = grad_keys[:WIN].astype(bf16)
        up_ref[1, :, lanes] = grad_values[:WIN].astype(bf16)
        down_ref[0, :, lanes] = grad_keys[WIN + rows :].astype(bf16)
        down_ref[1, :, lanes] = grad_values[WIN + rows :].astype(bf16)
        gk_ref[:, lanes] = grad_keys[WIN : WIN + rows]
        gv_ref[:, lanes] = grad_values[WIN : WIN + rows]


def attend_back_call(meta, qkv, rim_up, rim_down, grad_out, cosine, sine, seqs):
    _, rows, width = qkv.shape
    seq_rows = rows // seqs
    block = 256
    own, rim, flat = attention_specs(seqs, seq_rows, width, block)
    table = pl.BlockSpec(cosine.shape, lambda s, h: (0, 0))
    edge = pl.BlockSpec((2, WIN, block), lambda s, h: (0, s, h))
    edge_shape = jax.ShapeDtypeStruct((2, seqs * WIN, width), bf16)
    return pl.pallas_call(
        attend_back_kernel,
        grid=(seqs, width // block),
        in_specs=[
            pl.BlockSpec(memory_space=pltpu.SMEM), own(0), own(1), own(2), rim(0), rim(1), rim(0), rim(1),
            flat, table, table,
        ],
        out_specs=[flat, flat, flat, edge, edge],
        out_shape=[
            jax.ShapeDtypeStruct((rows, width), bf16),
            jax.ShapeDtypeStruct((rows, width), f32),
            jax.ShapeDtypeStruct((rows, width), f32),
            edge_shape,
            edge_shape,
        ],
        scratch_shapes=[
            pltpu.VMEM((seq_rows + 2 * WIN, LANES), f32),
            pltpu.VMEM((seq_rows + 2 * WIN, LANES), f32),
        ],
        compiler_params=params("arbitrary", "arbitrary"),
        cost_estimate=cost(20 * rows * width * (BLOCK_Q + 2 * WIN), 20 * rows * width),
        name="attend_back",
    )(meta, qkv, qkv, qkv, rim_up, rim_up, rim_down, rim_down, grad_out, cosine, sine)


def out_kernel(o_ref, w_ref, x_ref, valid_ref, gain_ref, middle_ref, normed_ref):
    branch = dot_nn(o_ref[...], w_ref[...])
    middle = x_ref[...].astype(f32) + valid_ref[...] * branch
    middle_ref[...] = middle
    scaled, _inverse = normalized(middle)
    normed_ref[...] = (scaled * gain_ref[...]).astype(bf16)


def out_call(attended, weight, x, valid, gain):
    rows, width = x.shape
    block = 128
    tile = pl.BlockSpec((block, width), lambda i: (i, 0))
    return pl.pallas_call(
        out_kernel,
        grid=(rows // block,),
        in_specs=[
            tile,
            pl.BlockSpec((width, width), lambda i: (0, 0)),
            tile,
            pl.BlockSpec((block, 1), lambda i: (i, 0)),
            pl.BlockSpec((1, width), lambda i: (0, 0)),
        ],
        out_specs=[tile, tile],
        out_shape=[jax.ShapeDtypeStruct((rows, width), f32), jax.ShapeDtypeStruct((rows, width), bf16)],
        compiler_params=params("arbitrary"),
        cost_estimate=cost(2 * rows * width * width, 2 * width * width + 10 * rows * width),
        name="out_norm",
    )(attended, weight, x, valid, gain)


def gate_kernel(n_ref, w1_ref, w2_ref, mixed_ref, slope_ref, act_ref):
    gate_in = dot_nn(n_ref[...], w1_ref[...])
    gate_up = dot_nn(n_ref[...], w2_ref[...])
    normal_cdf = 0.5 * (1.0 + lax.erf(gate_in * root_half))
    density = jnp.exp(-0.5 * gate_in * gate_in) * inv_root_two_pi
    activated = gate_in * normal_cdf
    mixed_ref[...] = (activated * gate_up).astype(bf16)
    slope_ref[...] = (gate_up * (normal_cdf + gate_in * density)).astype(bf16)
    act_ref[...] = activated.astype(bf16)


def gate_call(normed, weight, block):
    rows, width = normed.shape
    hidden = weight.shape[1] // 2
    steps = hidden // block
    tile = pl.BlockSpec((rows, block), lambda i: (0, i))
    shape = jax.ShapeDtypeStruct((rows, hidden), bf16)
    return pl.pallas_call(
        gate_kernel,
        grid=(steps,),
        in_specs=[
            pl.BlockSpec((rows, width), lambda i: (0, 0)),
            pl.BlockSpec((width, block), lambda i: (0, i)),
            pl.BlockSpec((width, block), lambda i: (0, i + steps)),
        ],
        out_specs=[tile, tile, tile],
        out_shape=[shape, shape, shape],
        compiler_params=params("arbitrary"),
        cost_estimate=cost(4 * rows * width * hidden, 4 * width * hidden + 6 * rows * hidden),
        name="gate",
    )(normed, weight, weight)


def gate_back_kernel(g_ref, w_ref, slope_ref, act_ref, out_ref):
    grad_mixed = dot_nt(g_ref[...], w_ref[...])
    out_ref[0] = (grad_mixed * slope_ref[...].astype(f32)).astype(bf16)
    out_ref[1] = (grad_mixed * act_ref[...].astype(f32)).astype(bf16)


def gate_back_call(grad_result, weight, slope, act, block):
    rows, width = grad_result.shape
    hidden = weight.shape[0]
    tile = pl.BlockSpec((rows, block), lambda i: (0, i))
    return pl.pallas_call(
        gate_back_kernel,
        grid=(hidden // block,),
        in_specs=[
            pl.BlockSpec((rows, width), lambda i: (0, 0)),
            pl.BlockSpec((block, width), lambda i: (i, 0)),
            tile,
            tile,
        ],
        out_specs=pl.BlockSpec((2, rows, block), lambda i: (0, 0, i)),
        out_shape=jax.ShapeDtypeStruct((2, rows, hidden), bf16),
        compiler_params=params("arbitrary"),
        cost_estimate=cost(2 * rows * width * hidden, 2 * width * hidden + 8 * rows * hidden),
        name="gate_back",
    )(grad_result, weight, slope, act)


def middle_back_kernel(gu_ref, w_ref, middle_ref, upstream_ref, valid_ref, gain_ref, grad_ref, branch_ref, acc):
    step = pl.program_id(0) * pl.num_programs(1) + pl.program_id(1)

    @pl.when(step == 0)
    def _():
        acc[...] = jnp.zeros_like(acc)

    acc[...] += dot_nt(gu_ref[0], w_ref[...])

    @pl.when(step == pl.num_programs(0) * pl.num_programs(1) - 1)
    def _():
        for top in range(0, acc.shape[0], 128):
            rows = slice(top, top + 128)
            scaled, inverse = normalized(middle_ref[rows, :])
            grad = upstream_ref[rows, :].astype(f32) + norm_back(
                acc[rows, :], gain_ref[...], scaled, inverse
            )
            grad_ref[rows, :] = grad
            branch_ref[rows, :] = (grad * valid_ref[rows, :]).astype(bf16)


def middle_back_call(grad_hidden, weight, middle, upstream, valid, gain, block):
    rows, width = middle.shape
    hidden = grad_hidden.shape[2]
    steps = hidden // block
    whole = pl.BlockSpec((rows, width), lambda h, i: (0, 0))
    return pl.pallas_call(
        middle_back_kernel,
        grid=(2, steps),
        in_specs=[
            pl.BlockSpec((1, rows, block), lambda h, i: (h, 0, i)),
            pl.BlockSpec((width, block), lambda h, i: (0, h * steps + i)),
            whole,
            whole,
            pl.BlockSpec((rows, 1), lambda h, i: (0, 0)),
            pl.BlockSpec((1, width), lambda h, i: (0, 0)),
        ],
        out_specs=[whole, whole],
        out_shape=[jax.ShapeDtypeStruct((rows, width), f32), jax.ShapeDtypeStruct((rows, width), bf16)],
        scratch_shapes=[pltpu.VMEM((rows, width), f32)],
        compiler_params=params("arbitrary", "arbitrary"),
        cost_estimate=cost(4 * rows * width * hidden, 4 * width * hidden + 4 * rows * hidden + 12 * rows * width),
        name="middle_back",
    )(grad_hidden, weight, middle, upstream, valid, gain)


def input_back_kernel(gqkv_ref, w_ref, x_ref, grad_ref, gain_ref, out_ref, acc):
    step = pl.program_id(0)

    @pl.when(step == 0)
    def _():
        acc[...] = jnp.zeros_like(acc)

    acc[...] += dot_nt(gqkv_ref[...], w_ref[...])

    @pl.when(step == pl.num_programs(0) - 1)
    def _():
        for top in range(0, acc.shape[0], 128):
            rows = slice(top, top + 128)
            scaled, inverse = normalized(x_ref[rows, :].astype(f32))
            out_ref[rows, :] = (
                grad_ref[rows, :] + norm_back(acc[rows, :], gain_ref[...], scaled, inverse)
            ).astype(bf16)


def input_back_call(grad_joint, weight, x, grad_middle, gain):
    rows, width = x.shape
    block = width
    whole = pl.BlockSpec((rows, width), lambda i: (0, 0))
    return pl.pallas_call(
        input_back_kernel,
        grid=(3 * width // block,),
        in_specs=[
            pl.BlockSpec((rows, block), lambda i: (0, i)),
            pl.BlockSpec((width, block), lambda i: (0, i)),
            whole,
            whole,
            pl.BlockSpec((1, width), lambda i: (0, 0)),
        ],
        out_specs=whole,
        out_shape=jax.ShapeDtypeStruct((rows, width), bf16),
        scratch_shapes=[pltpu.VMEM((rows, width), f32)],
        compiler_params=params("arbitrary"),
        cost_estimate=cost(6 * rows * width * width, 6 * width * width + 14 * rows * width),
        name="input_back",
    )(grad_joint, weight, x, grad_middle, gain)


def rope_tables(positions):
    halfway = HEAD_DIM // 2
    frequency = 10000.0 ** (-(2.0 * jnp.arange(halfway, dtype=f32)) / HEAD_DIM)
    angles = positions.astype(f32)[:, None] * frequency[None, :]
    cosine, sine = jnp.cos(angles), jnp.sin(angles)
    return (
        jnp.concatenate([cosine] * (LANES // halfway), axis=1),
        jnp.concatenate([-sine, sine] * (LANES // HEAD_DIM), axis=1),
    )


def on_device(inputs, cotangent, lengths, norm_first, w_qkv, w_out, norm_second, w_in, w_down):
    seqs, shard_rows, width = inputs.shape
    rows = seqs * shard_rows
    hidden = w_in.shape[1] // 2
    hidden_pad = -(-hidden // 384) * 384
    pad = hidden_pad - hidden
    block = 896 if hidden_pad % 896 == 0 else 384
    first_row = lax.axis_index("fsdp") * shard_rows
    query_pos = first_row + jnp.arange(shard_rows, dtype=jnp.int32)
    rim_pos = first_row - WIN + jnp.arange(shard_rows + 2 * WIN, dtype=jnp.int32)
    cosine, sine = rope_tables(rim_pos)
    valid = (query_pos[None, :] < lengths[:, None]).astype(f32).reshape(rows, 1)
    meta = jnp.concatenate([first_row.astype(jnp.int32)[None], lengths.astype(jnp.int32)])
    x = inputs.reshape(rows, width)
    upstream = cotangent.reshape(rows, width)
    grad_result = (upstream.astype(f32) * valid).astype(bf16)

    gains = jnp.pad(jnp.stack([norm_first, norm_second], axis=1), ((0, 0), (0, LANES - 2)))
    whole_first = gather_rows(jnp.concatenate([w_qkv, gains], axis=1))
    in_shard = jnp.pad(w_in.reshape(-1, 2, hidden), ((0, 0), (0, 0), (0, pad))).reshape(-1, 2 * hidden_pad)
    whole_second = gather_rows(jnp.concatenate([w_out, in_shard], axis=1))
    whole_down = gather_columns(w_down, pad)
    gain_first = whole_first[:, 3 * width].astype(f32)[None, :]
    gain_second = whole_first[:, 3 * width + 1].astype(f32)[None, :]
    whole_qkv = whole_first[:, : 3 * width]
    whole_out = whole_second[:, :width]
    whole_in = whole_second[:, width:]

    own_rows = slice(WIN, WIN + shard_rows)
    normed_first, qkv = qkv_call(x, gain_first, whole_qkv, cosine[own_rows], sine[own_rows])
    by_seq = qkv.reshape(3, seqs, shard_rows, width)[1:]
    edge = (2, seqs * WIN, width)
    rim_down, rim_up = neighbours(
        by_seq[:, :, :WIN].reshape(edge), by_seq[:, :, shard_rows - WIN :].reshape(edge)
    )
    attended = attend_call(meta, qkv, rim_up, rim_down, seqs)
    middle, normed_second = out_call(attended, whole_out, x, valid, gain_second)
    mixed, slope, act = gate_call(normed_second, whole_in, block)
    result = jnp.dot(mixed, whole_down, preferred_element_type=f32)
    output = (middle + valid * result).astype(bf16)

    state_down = pair_sum(mixed[:, :hidden], grad_result, False)
    grad_hidden = gate_back_call(grad_result, whole_down, slope, act, block)
    state_in = [pair_sum(normed_second, grad_hidden[half], True) for half in range(2)]
    grad_middle, grad_branch = middle_back_call(
        grad_hidden, whole_in, middle, upstream, valid, gain_second, block
    )
    grad_att = dot_nt(grad_branch, whole_out).astype(bf16)
    state_out = pair_sum(attended, grad_branch, True)
    grad_q, grad_k, grad_v, edge_up, edge_down = attend_back_call(
        meta, qkv, rim_up, rim_down, grad_att, cosine, sine, seqs
    )
    from_next, from_before = neighbours(edge_up, edge_down)

    def with_edges(own, plane):
        own = own.reshape(seqs, shard_rows, width)
        before = from_before[plane].reshape(seqs, WIN, width).astype(f32)
        after = from_next[plane].reshape(seqs, WIN, width).astype(f32)
        rest = ((0, 0), (0, shard_rows - WIN), (0, 0))
        own = own + jnp.pad(before, rest) + jnp.pad(after, (rest[0], rest[1][::-1], rest[2]))
        return own.reshape(rows, width).astype(bf16)

    grad_joint = jnp.concatenate([grad_q, with_edges(grad_k, 0), with_edges(grad_v, 1)], axis=1)
    state_qkv = pair_sum(normed_first, grad_joint, True)
    grad_inputs = input_back_call(grad_joint, whole_qkv, x, grad_middle, gain_first)

    grad_down = reduce_columns(state_down)
    grad_in = reduce_rows(jnp.concatenate(state_in, axis=1))
    grad_in = jnp.concatenate([grad_in[:, :hidden], grad_in[:, hidden_pad : hidden_pad + hidden]], axis=1)
    grad_last = reduce_rows(jnp.concatenate([state_qkv, state_out], axis=1))
    grad_qkv = grad_last[:, : 3 * width]
    grad_out = grad_last[:, 3 * width :]
    grad_first = jnp.sum(grad_qkv * w_qkv.astype(f32), axis=1) / norm_first.astype(f32)
    grad_second = jnp.sum(grad_in * w_in.astype(f32), axis=1) / norm_second.astype(f32)
    return (
        output.reshape(inputs.shape),
        grad_inputs.reshape(inputs.shape),
        grad_first,
        grad_qkv,
        grad_out,
        grad_second,
        grad_in,
        grad_down,
    )


def solution(mesh):
    in_specs = (
        P("rep", "fsdp", None),
        P("rep", "fsdp", None),
        P("rep"),
        P("fsdp"),
        P("fsdp", None),
        P("fsdp", None),
        P("fsdp"),
        P("fsdp", None),
        P("fsdp", None),
    )
    out_specs = (
        P("rep", "fsdp", None),
        P("rep", "fsdp", None),
        P("fsdp"),
        P("fsdp", None),
        P("fsdp", None),
        P("fsdp"),
        P("fsdp", None),
        P("fsdp", None),
    )
    return jax.shard_map(
        on_device, mesh=mesh, in_specs=in_specs, out_specs=out_specs, check_vma=False
    )
```

```python
import functools

import jax
import jax.numpy as jnp
from jax import lax
from jax.experimental import pallas as pl
from jax.experimental.pallas import tpu as pltpu
from jax.sharding import PartitionSpec as P

HEAD_DIM = 64
WIN = 64
BLOCK_Q = 128
LANES = 128

epsilon = 1e-05
root_half = 0.7071067811865476
inv_root_two_pi = 0.3989422804014327
f32 = jnp.float32
bf16 = jnp.bfloat16
VMEM_LIMIT = 48 * 1024 * 1024


def after(value, *before):
    return lax.optimization_barrier((value, before))[0]


def bit_count():
    return lax.axis_size("rep").bit_length() - 1


def bit_value(bit):
    return (lax.axis_index("rep") >> bit) & 1


def link_count():
    return bit_count() - 1


def link_axis(bit):
    return bit_count() - 1 - bit


def flip(value, bit):
    size = lax.axis_size("rep")
    return lax.ppermute(value, "rep", [(i, i ^ (1 << bit)) for i in range(size)])


def turn(value, steps):
    size = lax.axis_size("fsdp")
    return lax.ppermute(value, "fsdp", [(i, (i + steps) % size) for i in range(size)])


def link_orders():
    bits = list(range(1, bit_count()))
    return list(zip(bits, bits[::-1]))


def in_order(mine, got, bit, axis):
    first = bit_value(bit) == 0
    return jnp.concatenate([jnp.where(first, mine, got), jnp.where(first, got, mine)], axis=axis)


def widen(states, bits, lead):
    return [
        in_order(state, flip(state, bit), bit, lead + link_axis(bit)) for state, bit in zip(states, bits)
    ]


def row_piece(shards):
    width = sum(shard.shape[1] for shard in shards)
    links = 1 << link_count()
    core, link = bit_value(0), lax.axis_index("rep") >> 1
    views = [shard.reshape(2, 2, links, -1, shard.shape[1]) for shard in shards]
    rows = views[0].shape[3]
    pieces = [
        lax.dynamic_slice(view, (core, 0, link, 0, 0), (1, 2, 1, rows, view.shape[4])) for view in views
    ]
    return jnp.concatenate(pieces, axis=-1).reshape(2, rows, width)


def row_states(came):
    ones = (1,) * link_count()
    return [
        jnp.stack([piece[part] for piece in came]).reshape((len(came),) + ones + came[0].shape[1:])
        for part in range(2)
    ]


def row_parts(states):
    mine = [state.reshape(state.shape[0], -1, state.shape[-1]) for state in states]
    return mine + [flip(state, 0) for state in mine]


def half_rows(rows):
    return -(-rows // 2 // 16) * 16


def column_piece(shard):
    columns = shard.shape[1] // lax.axis_size("rep")
    place = (bit_value(0) << link_count()) + (lax.axis_index("rep") >> 1)
    return lax.dynamic_slice_in_dim(shard, place * columns, columns, 1)


def column_states(came):
    cut = half_rows(came[0].shape[0])
    ones = (1,) * link_count()
    stacked = jnp.stack(came)
    return [
        part.reshape(part.shape[:1] + ones + part.shape[1:]) for part in (stacked[:, :cut], stacked[:, cut:])
    ]


def column_parts(states):
    mine = [state.reshape((state.shape[0], -1) + state.shape[-2:]) for state in states]
    return mine + [flip(state, 0) for state in mine]


def whole_columns(shard, parts, pad_rows):
    size = lax.axis_size("fsdp")
    me = lax.axis_index("fsdp")
    rows, width = shard.shape
    mine, got = [jnp.concatenate(pair, axis=2) for pair in (parts[:2], parts[2:])]
    joined = in_order(mine, got, 0, 1)
    joined = jnp.transpose(joined, (0, 2, 1, 3)).reshape(size - 1, rows, width)
    whole = jnp.zeros((size * rows + pad_rows, width), shard.dtype)
    whole = lax.dynamic_update_slice(whole, shard, (me * rows, 0))
    for steps in range(1, size):
        source = lax.rem(me - steps + size, size)
        whole = lax.dynamic_update_slice(whole, joined[steps - 1], (source * rows, 0))
    return whole


def turned_before(piece):
    return [turn(piece, steps) for steps in range(1, lax.axis_size("fsdp"))]


def tokens_dot(left, right):
    return lax.dot_general(left, right, (((0,), (0,)), ((), ())), preferred_element_type=f32)


def half_of(split, mine):
    index = bit_value(0) if mine else 1 - bit_value(0)
    return lax.dynamic_index_in_dim(split, index, 0, False)


def fold(blocks, lead, bit):
    axis = lead + link_axis(bit)
    mine = bit_value(bit)
    give = [lax.dynamic_slice_in_dim(block, 1 - mine, 1, axis) for block in blocks]
    got = flip(give[0] if len(give) == 1 else jnp.concatenate(give, axis=-1), bit)
    results, start = [], 0
    for block in blocks:
        keep = lax.dynamic_slice_in_dim(block, mine, 1, axis)
        width = block.shape[-1]
        add = lax.slice_in_dim(got, start, start + width, axis=got.ndim - 1)
        results.append((keep.astype(f32) + add.astype(f32)).astype(bf16))
        start += width
    return results


def scattered(state):
    flat = lax.psum_scatter(state.reshape(-1, state.shape[-1]), "fsdp", scatter_dimension=0, tiled=True)
    return flat.reshape(state.shape[1:])


def to_owner(state):
    size = lax.axis_size("fsdp")
    me = lax.axis_index("fsdp")
    came = [
        turn(lax.dynamic_index_in_dim(state, lax.rem(me + steps, size), 0, False), steps)
        for steps in range(1, size)
    ]
    total = lax.dynamic_index_in_dim(state, me, 0, False).astype(f32)
    for part in came:
        total = total + part.astype(f32)
    return total.astype(bf16)


def row_blocks(states):
    size = lax.axis_size("fsdp")
    views = [state.reshape((size, 2) + (2,) * link_count() + (-1, state.shape[1])) for state in states]
    return [[view[:, part] for view in views] for part in range(2)]


def neighbours(up, down):
    size = lax.axis_size("fsdp")
    forward = [(i, i + 1) for i in range(size - 1)]
    backward = [(i + 1, i) for i in range(size - 1)]
    return lax.ppermute(up, "fsdp", backward), lax.ppermute(down, "fsdp", forward)


def params(*semantics):
    return pltpu.CompilerParams(
        dimension_semantics=semantics, vmem_limit_bytes=VMEM_LIMIT
    )


def cost(flops, nbytes):
    return pl.CostEstimate(flops=int(flops), bytes_accessed=int(nbytes), transcendentals=0)


def dot_nn(left, right):
    return jnp.dot(left, right, preferred_element_type=f32)


def dot_nt(left, right):
    return lax.dot_general(left, right, (((1,), (1,)), ((), ())), preferred_element_type=f32)


def normalized(values):
    centred = values - jnp.mean(values, axis=-1, keepdims=True)
    inverse = lax.rsqrt(jnp.mean(centred * centred, axis=-1, keepdims=True) + epsilon)
    return centred * inverse, inverse


def norm_back(grad_out, gain, scaled, inverse):
    grad_scaled = grad_out * gain
    return inverse * (
        grad_scaled
        - jnp.mean(grad_scaled, axis=-1, keepdims=True)
        - scaled * jnp.mean(grad_scaled * scaled, axis=-1, keepdims=True)
    )


def swapped_halves(values):
    width = values.shape[-1]
    lane = lax.broadcasted_iota(jnp.int32, values.shape, values.ndim - 1)
    ahead = pltpu.roll(values, width - HEAD_DIM // 2, values.ndim - 1)
    behind = pltpu.roll(values, HEAD_DIM // 2, values.ndim - 1)
    return jnp.where(lane % HEAD_DIM < HEAD_DIM // 2, ahead, behind)


def assemble(meta_ref, whole_ref, own_ref, part_refs):
    rows = own_ref.shape[0]
    count, quarter = part_refs[0].shape[:2]
    size = count + 1
    me, core = meta_ref[1], meta_ref[2]
    whole_ref[pl.ds(pl.multiple_of(me * rows, quarter), rows), :] = own_ref[...]
    for steps in range(1, size):
        base = lax.rem(me - steps + size, size) * rows
        for number, part_ref in enumerate(part_refs):
            half = core if number < 2 else 1 - core
            start = base + half * (rows // 2) + (number % 2) * quarter
            whole_ref[pl.ds(pl.multiple_of(start, quarter), quarter), :] = part_ref[steps - 1]


def split_columns(values, split_ref, rows, size):
    half = values.shape[1] // size // 2
    for place in range(size):
        for core in range(2):
            start = (2 * place + core) * half
            split_ref[core, rows, place * half : (place + 1) * half] = values[:, start : start + half]


def joined_columns(split_ref, rows, size):
    half = split_ref.shape[2] // size
    return jnp.concatenate(
        [
            split_ref[core, rows, place * half : (place + 1) * half]
            for place in range(size)
            for core in range(2)
        ],
        axis=1,
    )


def part_specs(parts, block, place):
    count, quarter, _ = parts[0].shape
    return [pl.BlockSpec((count, quarter, block), lambda i: (0, 0, place(i)))] * 4


def qkv_kernel(
    meta_ref, x_ref, own_ref, p0, p1, p2, p3, gain_ref, g0, g1, g2, g3, cos_ref, sin_ref,
    split_ref, out_ref, gains_ref, whole_ref, normed_ref, column_ref, *, rope_steps, size,
):
    step = pl.program_id(0)

    @pl.when(step == 0)
    def _():
        assemble(meta_ref, column_ref, gain_ref, (g0, g1, g2, g3))
        row = lax.broadcasted_iota(jnp.int32, gains_ref.shape[:1] + (LANES,), 0)
        lane = lax.broadcasted_iota(jnp.int32, gains_ref.shape[:1] + (LANES,), 1)
        gains_ref[...] = dot_nt((row == lane).astype(f32).astype(bf16), column_ref[...])
        for top in range(0, x_ref.shape[0], 128):
            rows = slice(top, top + 128)
            scaled, _inverse = normalized(x_ref[rows, :].astype(f32))
            normed = (scaled * gains_ref[0:1, :]).astype(bf16)
            normed_ref[rows, :] = normed
            split_columns(normed, split_ref, rows, size)

    assemble(meta_ref, whole_ref, own_ref, (p0, p1, p2, p3))
    product = dot_nn(normed_ref[...], whole_ref[...])

    @pl.when(step >= rope_steps)
    def _():
        out_ref[0] = product.astype(bf16)

    @pl.when(step < rope_steps)
    def _():
        seq_rows = cos_ref.shape[0]
        cosine, sine = cos_ref[...], sin_ref[...]
        for top in range(0, product.shape[0], seq_rows):
            for lane in range(0, product.shape[1], LANES):
                tile = product[top : top + seq_rows, lane : lane + LANES]
                out_ref[0, top : top + seq_rows, lane : lane + LANES] = (
                    tile * cosine + swapped_halves(tile) * sine
                ).astype(bf16)


SMEM_SPEC = pl.BlockSpec(memory_space=pltpu.SMEM)


def fixed(*shape):
    return pl.BlockSpec(shape, lambda i: (0,) * len(shape))


def qkv_call(meta, x, own, parts, own_gains, cosine, sine):
    rows, width = x.shape
    slab = own.shape[0]
    size = width // slab
    block = 512
    per_plane = width // block
    return pl.pallas_call(
        functools.partial(qkv_kernel, rope_steps=2 * per_plane, size=size),
        grid=(3 * per_plane,),
        in_specs=[SMEM_SPEC, fixed(rows, width), pl.BlockSpec((slab, block), lambda i: (0, i))]
        + part_specs(parts, block, lambda i: i)
        + [fixed(slab, LANES)]
        + part_specs(parts, LANES, lambda i: 3 * width // LANES)
        + [fixed(*cosine.shape), fixed(*sine.shape)],
        out_specs=[
            fixed(2, rows, width // 2),
            pl.BlockSpec((1, rows, block), lambda i: (i // per_plane, 0, i % per_plane)),
            fixed(8, width),
        ],
        out_shape=[
            jax.ShapeDtypeStruct((2, rows, width // 2), bf16),
            jax.ShapeDtypeStruct((3, rows, width), bf16),
            jax.ShapeDtypeStruct((8, width), f32),
        ],
        scratch_shapes=[
            pltpu.VMEM((width, block), bf16),
            pltpu.VMEM((rows, width), bf16),
            pltpu.VMEM((width, LANES), bf16),
        ],
        compiler_params=params("arbitrary"),
        cost_estimate=cost(6 * rows * width * width, 6 * width * width + 10 * rows * width),
        name="qkv",
    )(meta, x, own, *parts, own_gains, *parts, cosine, sine)


def head_masks():
    lane = lax.broadcasted_iota(jnp.int32, (1, LANES), 1)
    first = lane < HEAD_DIM
    return first, first.astype(f32).astype(bf16), (~first).astype(f32).astype(bf16)


def two_heads(tile, low_mask, high_mask):
    return jnp.concatenate([tile * low_mask, tile * high_mask], axis=0)


def score_bias(first_row, length):
    shape = (BLOCK_Q, BLOCK_Q + 2 * WIN)
    query = first_row + lax.broadcasted_iota(jnp.int32, shape, 0)
    key = first_row - WIN + lax.broadcasted_iota(jnp.int32, shape, 1)
    near = jnp.abs(query - key) <= WIN
    live = (key >= 0) & (key < length)
    bias = jnp.where(near & (live | (query == key)), 0.0, -1e30).astype(f32)
    return jnp.concatenate([bias, bias], axis=0)


def softmax_of(queries, keys, bias):
    scores = dot_nt(queries, keys) * (HEAD_DIM**-0.5) + bias
    exponent = jnp.exp(scores - jnp.max(scores, axis=-1, keepdims=True))
    return exponent / jnp.sum(exponent, axis=-1, keepdims=True)


def attend_kernel(
    meta_ref, q_ref, k_ref, v_ref, k_up_ref, v_up_ref, k_down_ref, v_down_ref, out_ref, probs_ref
):
    length = meta_ref[3 + pl.program_id(0)]
    rows, width = q_ref.shape[1:]
    first_head, low_mask, high_mask = head_masks()
    for lane in range(0, width, LANES):
        lanes = slice(lane, lane + LANES)
        keys = jnp.concatenate([k_up_ref[0, :, lanes], k_ref[0, :, lanes], k_down_ref[0, :, lanes]], 0)
        values = jnp.concatenate([v_up_ref[0, :, lanes], v_ref[0, :, lanes], v_down_ref[0, :, lanes]], 0)
        for top in range(0, rows, BLOCK_Q):
            bias = score_bias(meta_ref[0] + top, length)
            span = slice(top, top + BLOCK_Q + 2 * WIN)
            queries = two_heads(q_ref[0, top : top + BLOCK_Q, lanes], low_mask, high_mask)
            probs = softmax_of(queries, keys[span], bias).astype(bf16)
            probs_ref[0, lane // LANES, top // BLOCK_Q] = probs
            result = dot_nn(probs, values[span])
            out_ref[top : top + BLOCK_Q, lanes] = jnp.where(
                first_head, result[:BLOCK_Q], result[BLOCK_Q:]
            ).astype(bf16)


def attention_specs(seqs, seq_rows, width, block):
    own = lambda plane: pl.BlockSpec((1, seq_rows, block), lambda s, h: (plane, s, h))
    rim = lambda plane: pl.BlockSpec((1, WIN, block), lambda s, h: (plane, s, h))
    flat = pl.BlockSpec((seq_rows, block), lambda s, h: (s, h))
    inner = (seq_rows // BLOCK_Q, 2 * BLOCK_Q, BLOCK_Q + 2 * WIN)
    probs = pl.BlockSpec((1, block // LANES) + inner, lambda s, h: (s, h, 0, 0, 0))
    probs_shape = jax.ShapeDtypeStruct((seqs, width // LANES) + inner, bf16)
    return own, rim, flat, probs, probs_shape


def attend_call(meta, qkv, rim_up, rim_down, seqs):
    _, rows, width = qkv.shape
    seq_rows = rows // seqs
    block = 256
    own, rim, flat, probs, probs_shape = attention_specs(seqs, seq_rows, width, block)
    return pl.pallas_call(
        attend_kernel,
        grid=(seqs, width // block),
        in_specs=[SMEM_SPEC, own(0), own(1), own(2), rim(0), rim(1), rim(0), rim(1)],
        out_specs=[flat, probs],
        out_shape=[jax.ShapeDtypeStruct((rows, width), bf16), probs_shape],
        compiler_params=params("arbitrary", "arbitrary"),
        cost_estimate=cost(8 * rows * width * (BLOCK_Q + 2 * WIN), 10 * rows * width),
        name="attend",
    )(meta, qkv, qkv, qkv, rim_up, rim_up, rim_down, rim_down)


def attend_back_kernel(
    q_ref,
    k_ref,
    v_ref,
    k_up_ref,
    v_up_ref,
    k_down_ref,
    v_down_ref,
    probs_ref,
    go_ref,
    cos_ref,
    sin_ref,
    gq_ref,
    gk_ref,
    gv_ref,
    up_ref,
    down_ref,
    gk_acc,
    gv_acc,
):
    rows, width = q_ref.shape[1:]
    scale = HEAD_DIM**-0.5
    first_head, low_mask, high_mask = head_masks()

    def turned_back(tile, span):
        return tile * cos_ref[span, :] - swapped_halves(tile) * sin_ref[span, :]

    for lane in range(0, width, LANES):
        lanes = slice(lane, lane + LANES)
        keys = jnp.concatenate([k_up_ref[0, :, lanes], k_ref[0, :, lanes], k_down_ref[0, :, lanes]], 0)
        values = jnp.concatenate([v_up_ref[0, :, lanes], v_ref[0, :, lanes], v_down_ref[0, :, lanes]], 0)
        gk_acc[...] = jnp.zeros_like(gk_acc)
        gv_acc[...] = jnp.zeros_like(gv_acc)
        for top in range(0, rows, BLOCK_Q):
            span = slice(top, top + BLOCK_Q + 2 * WIN)
            queries = two_heads(q_ref[0, top : top + BLOCK_Q, lanes], low_mask, high_mask)
            grads = two_heads(go_ref[top : top + BLOCK_Q, lanes], low_mask, high_mask)
            probs_low = probs_ref[0, lane // LANES, top // BLOCK_Q]
            probs = probs_low.astype(f32)
            grad_probs = dot_nt(grads, values[span])
            delta = jnp.sum(probs * grad_probs, axis=-1, keepdims=True)
            grad_scores = (probs * (grad_probs - delta)).astype(bf16)
            result = dot_nn(grad_scores, keys[span])
            result = jnp.where(first_head, result[:BLOCK_Q], result[BLOCK_Q:]) * scale
            own = slice(WIN + top, WIN + top + BLOCK_Q)
            gq_ref[top : top + BLOCK_Q, lanes] = turned_back(result, own).astype(bf16)
            gk_acc[span, :] += tokens_dot(grad_scores, queries)
            gv_acc[span, :] += tokens_dot(probs_low, grads)
        grad_keys = turned_back(gk_acc[...] * scale, slice(None))
        grad_values = gv_acc[...]
        up_ref[0, :, lanes] = grad_keys[:WIN].astype(bf16)
        up_ref[1, :, lanes] = grad_values[:WIN].astype(bf16)
        down_ref[0, :, lanes] = grad_keys[WIN + rows :].astype(bf16)
        down_ref[1, :, lanes] = grad_values[WIN + rows :].astype(bf16)
        gk_ref[:, lanes] = grad_keys[WIN : WIN + rows]
        gv_ref[:, lanes] = grad_values[WIN : WIN + rows]


def attend_back_call(qkv, rim_up, rim_down, saved, grad_out, cosine, sine, seqs):
    _, rows, width = qkv.shape
    seq_rows = rows // seqs
    block = 256
    own, rim, flat, probs, probs_shape = attention_specs(seqs, seq_rows, width, block)
    table = pl.BlockSpec(cosine.shape, lambda s, h: (0, 0))
    edge = pl.BlockSpec((2, WIN, block), lambda s, h: (0, s, h))
    edge_shape = jax.ShapeDtypeStruct((2, seqs * WIN, width), bf16)
    return pl.pallas_call(
        attend_back_kernel,
        grid=(seqs, width // block),
        in_specs=[
            own(0), own(1), own(2), rim(0), rim(1), rim(0), rim(1),
            probs, flat, table, table,
        ],
        out_specs=[flat, flat, flat, edge, edge],
        out_shape=[
            jax.ShapeDtypeStruct((rows, width), bf16),
            jax.ShapeDtypeStruct((rows, width), f32),
            jax.ShapeDtypeStruct((rows, width), f32),
            edge_shape,
            edge_shape,
        ],
        scratch_shapes=[
            pltpu.VMEM((seq_rows + 2 * WIN, LANES), f32),
            pltpu.VMEM((seq_rows + 2 * WIN, LANES), f32),
        ],
        compiler_params=params("arbitrary", "arbitrary"),
        cost_estimate=cost(20 * rows * width * (BLOCK_Q + 2 * WIN), 20 * rows * width),
        name="attend_back",
    )(qkv, qkv, qkv, rim_up, rim_up, rim_down, rim_down, saved, grad_out, cosine, sine)


def out_kernel(
    meta_ref, o_ref, own_ref, p0, p1, p2, p3, x_ref, valid_ref, gains_ref,
    middle_ref, n_split_ref, o_split_ref, whole_ref, *, size,
):
    @pl.when(pl.program_id(0) == 0)
    def _():
        assemble(meta_ref, whole_ref, own_ref, (p0, p1, p2, p3))

    values = o_ref[...]
    split_columns(values, o_split_ref, slice(None), size)
    middle = x_ref[...].astype(f32) + valid_ref[...] * dot_nn(values, whole_ref[...])
    middle_ref[...] = middle
    scaled, _inverse = normalized(middle)
    split_columns((scaled * gains_ref[1:2, :]).astype(bf16), n_split_ref, slice(None), size)


def out_call(meta, attended, own, parts, x, valid, gains):
    rows, width = x.shape
    slab = own.shape[0]
    size = width // slab
    block = 128
    tile = pl.BlockSpec((block, width), lambda i: (i, 0))
    split = pl.BlockSpec((2, block, width // 2), lambda i: (0, i, 0))
    split_shape = jax.ShapeDtypeStruct((2, rows, width // 2), bf16)
    return pl.pallas_call(
        functools.partial(out_kernel, size=size),
        grid=(rows // block,),
        in_specs=[SMEM_SPEC, tile, fixed(slab, width)]
        + part_specs(parts, width, lambda i: 0)
        + [tile, pl.BlockSpec((block, 1), lambda i: (i, 0)), fixed(8, width)],
        out_specs=[tile, split, split],
        out_shape=[jax.ShapeDtypeStruct((rows, width), f32), split_shape, split_shape],
        scratch_shapes=[pltpu.VMEM((width, width), bf16)],
        compiler_params=params("arbitrary"),
        cost_estimate=cost(2 * rows * width * width, 2 * width * width + 12 * rows * width),
        name="out_norm",
    )(meta, attended, own, *parts, x, valid, gains)


def gate_kernel(
    meta_ref, n_ref, own1_ref, p0, p1, p2, p3, own2_ref, q0, q1, q2, q3,
    mixed_ref, slope_ref, act_ref, normed_ref, first_ref, second_ref, *, size,
):
    @pl.when(pl.program_id(0) == 0)
    def _():
        for top in range(0, normed_ref.shape[0], 128):
            rows = slice(top, top + 128)
            normed_ref[rows, :] = joined_columns(n_ref, rows, size)

    assemble(meta_ref, first_ref, own1_ref, (p0, p1, p2, p3))
    assemble(meta_ref, second_ref, own2_ref, (q0, q1, q2, q3))
    gate_in = dot_nn(normed_ref[...], first_ref[...])
    gate_up = dot_nn(normed_ref[...], second_ref[...])
    normal_cdf = 0.5 * (1.0 + lax.erf(gate_in * root_half))
    density = jnp.exp(-0.5 * gate_in * gate_in) * inv_root_two_pi
    activated = gate_in * normal_cdf
    mixed_ref[...] = (activated * gate_up).astype(bf16)
    slope_ref[...] = (gate_up * (normal_cdf + gate_in * density)).astype(bf16)
    act_ref[...] = activated.astype(bf16)


def gate_call(meta, normed, own1, parts1, own2, parts2, block):
    _, rows, half = normed.shape
    width = 2 * half
    slab, hidden = own1.shape
    size = width // slab
    tile = pl.BlockSpec((rows, block), lambda i: (0, i))
    own = pl.BlockSpec((slab, block), lambda i: (0, i))
    shape = jax.ShapeDtypeStruct((rows, hidden), bf16)
    return pl.pallas_call(
        functools.partial(gate_kernel, size=size),
        grid=(hidden // block,),
        in_specs=[SMEM_SPEC, fixed(2, rows, half), own]
        + part_specs(parts1, block, lambda i: i)
        + [own]
        + part_specs(parts2, block, lambda i: i),
        out_specs=[tile, tile, tile],
        out_shape=[shape, shape, shape],
        scratch_shapes=[
            pltpu.VMEM((rows, width), bf16),
            pltpu.VMEM((width, block), bf16),
            pltpu.VMEM((width, block), bf16),
        ],
        compiler_params=params("arbitrary"),
        cost_estimate=cost(4 * rows * width * hidden, 4 * width * hidden + 6 * rows * hidden),
        name="gate",
    )(meta, normed, own1, *parts1, own2, *parts2)


def gate_back_kernel(
    meta_ref, g_ref, own_ref, p0, p1, p2, p3, slope_ref, act_ref, out_ref, whole_ref, *, block
):
    step = pl.program_id(0)

    @pl.when(step == 0)
    def _():
        rows = own_ref.shape[0]
        count, links, cut, columns = p0.shape
        size = count + 1
        me, core = meta_ref[1], meta_ref[2]
        whole_ref[size * rows :, :] = jnp.zeros_like(whole_ref[size * rows :, :])
        whole_ref[pl.ds(pl.multiple_of(me * rows, 16), rows), :] = own_ref[...]

        def put(halves):
            for steps in range(1, size):
                base = lax.rem(me - steps + size, size) * rows
                for half, parts in enumerate(halves):
                    for part, start in zip(parts, (0, cut)):
                        target = pl.ds(pl.multiple_of(base + start, 16), part.shape[2])
                        for link in range(links):
                            lane = (half * links + link) * columns
                            whole_ref[target, lane : lane + columns] = part[steps - 1, link]

        @pl.when(core == 0)
        def _():
            put(((p0, p1), (p2, p3)))

        @pl.when(core == 1)
        def _():
            put(((p2, p3), (p0, p1)))

    weight = whole_ref[pl.ds(pl.multiple_of(step * block, block), block), :]
    grad_mixed = dot_nt(g_ref[...], weight)
    out_ref[0] = (grad_mixed * slope_ref[...].astype(f32)).astype(bf16)
    out_ref[1] = (grad_mixed * act_ref[...].astype(f32)).astype(bf16)


def gate_back_plain_kernel(g_ref, w_ref, slope_ref, act_ref, out_ref):
    grad_mixed = dot_nt(g_ref[...], w_ref[...])
    out_ref[0] = (grad_mixed * slope_ref[...].astype(f32)).astype(bf16)
    out_ref[1] = (grad_mixed * act_ref[...].astype(f32)).astype(bf16)


def gate_back_call(meta, grad_result, own, parts, slope, act, block):
    rows, width = grad_result.shape
    hidden = slope.shape[1]
    tile = pl.BlockSpec((rows, block), lambda i: (0, i))
    out_spec = pl.BlockSpec((2, rows, block), lambda i: (0, 0, i))
    out_shape = jax.ShapeDtypeStruct((2, rows, hidden), bf16)
    settings = dict(
        grid=(hidden // block,),
        compiler_params=params("arbitrary"),
        cost_estimate=cost(2 * rows * width * hidden, 4 * width * hidden + 8 * rows * hidden),
        name="gate_back",
    )
    if own.shape[0] % 16:
        whole = whole_columns(own, parts, hidden - own.shape[0] * (parts[0].shape[0] + 1))
        out = pl.pallas_call(
            gate_back_plain_kernel,
            in_specs=[fixed(rows, width), pl.BlockSpec((block, width), lambda i: (i, 0)), tile, tile],
            out_specs=out_spec,
            out_shape=out_shape,
            **settings,
        )(grad_result, whole, slope, act)
        return out, whole
    return pl.pallas_call(
        functools.partial(gate_back_kernel, block=block),
        in_specs=[SMEM_SPEC, fixed(rows, width), fixed(*own.shape)]
        + [fixed(*part.shape) for part in parts]
        + [tile, tile],
        out_specs=[out_spec, fixed(hidden, width)],
        out_shape=[out_shape, jax.ShapeDtypeStruct((hidden, width), bf16)],
        **settings,
    )(meta, grad_result, own, *parts, slope, act)


def down_kernel(meta_ref, m_ref, g_ref, *rest, mine, size, links):
    add_ref = rest[0] if mine else None
    out_ref, sums_ref = rest[-2:]
    step = pl.program_id(0)
    block, half = m_ref.shape[1], sums_ref.shape[1]
    which = meta_ref[2] if mine else 1 - meta_ref[2]
    right = g_ref[:, pl.ds(pl.multiple_of(which * half, half), half)]
    sums_ref[pl.ds(pl.multiple_of(step * block, block), block), :] = tokens_dot(m_ref[...], right)

    @pl.when(step == pl.num_programs(0) - 1)
    def _():
        rows, columns = out_ref.shape[2:]
        for place in range(size):
            for link in range(links):
                value = sums_ref[place * rows : (place + 1) * rows, link * columns : (link + 1) * columns]
                if mine:
                    value = value + add_ref[place, link].astype(f32)
                out_ref[place, link] = value.astype(bf16)


def down_call(meta, mixed, grad_result, size, hidden, block, add=None):
    rows, hidden_pad = mixed.shape
    width = grad_result.shape[1]
    links = 1 << link_count()
    shape = (size, links, hidden // size, width // 2 // links)
    extra = [] if add is None else [add]
    return pl.pallas_call(
        functools.partial(down_kernel, mine=add is not None, size=size, links=links),
        grid=(hidden_pad // block,),
        in_specs=[SMEM_SPEC, pl.BlockSpec((rows, block), lambda i: (0, i)), fixed(rows, width)]
        + [fixed(*shape) for _ in extra],
        out_specs=fixed(*shape),
        out_shape=jax.ShapeDtypeStruct(shape, bf16),
        scratch_shapes=[pltpu.VMEM((hidden_pad, width // 2), f32)],
        compiler_params=params("arbitrary"),
        cost_estimate=cost(rows * width * hidden, width * hidden + 2 * rows * (hidden + width)),
        name="down_sum",
    )(meta, mixed, grad_result, *extra)


def middle_back_kernel(
    meta_ref, gu_ref, own1_ref, p0, p1, p2, p3, own2_ref, q0, q1, q2, q3, out_own_ref, r0, r1, r2, r3,
    middle_ref, upstream_ref, valid_ref, gains_ref, grad_ref, branch_ref, att_ref,
    acc, first_ref, second_ref, out_ref,
):
    step = pl.program_id(0)
    assemble(meta_ref, first_ref, own1_ref, (p0, p1, p2, p3))
    assemble(meta_ref, second_ref, own2_ref, (q0, q1, q2, q3))
    total = dot_nt(gu_ref[0], first_ref[...]) + dot_nt(gu_ref[1], second_ref[...])

    @pl.when(step == 0)
    def _():
        acc[...] = total
        assemble(meta_ref, out_ref, out_own_ref, (r0, r1, r2, r3))

    @pl.when(step > 0)
    def _():
        acc[...] += total

    @pl.when(step == pl.num_programs(0) - 1)
    def _():
        for top in range(0, acc.shape[0], 128):
            rows = slice(top, top + 128)
            scaled, inverse = normalized(middle_ref[rows, :])
            grad = upstream_ref[rows, :].astype(f32) + norm_back(
                acc[rows, :], gains_ref[1:2, :], scaled, inverse
            )
            grad_ref[rows, :] = grad
            branch = (grad * valid_ref[rows, :]).astype(bf16)
            branch_ref[rows, :] = branch
            att_ref[rows, :] = dot_nt(branch, out_ref[...]).astype(bf16)


def middle_back_call(
    meta, grad_hidden, own1, parts1, own2, parts2, out_own, out_parts, middle, upstream, valid, gains, block
):
    rows, width = middle.shape
    slab = own1.shape[0]
    hidden = grad_hidden.shape[2]
    whole = fixed(rows, width)
    own = pl.BlockSpec((slab, block), lambda i: (0, i))
    flat_low = jax.ShapeDtypeStruct((rows, width), bf16)
    return pl.pallas_call(
        middle_back_kernel,
        grid=(hidden // block,),
        in_specs=[SMEM_SPEC, pl.BlockSpec((2, rows, block), lambda i: (0, 0, i)), own]
        + part_specs(parts1, block, lambda i: i)
        + [own]
        + part_specs(parts2, block, lambda i: i)
        + [fixed(slab, width)]
        + part_specs(out_parts, width, lambda i: 0)
        + [whole, whole, fixed(rows, 1), fixed(8, width)],
        out_specs=[whole, whole, whole],
        out_shape=[jax.ShapeDtypeStruct((rows, width), f32), flat_low, flat_low],
        scratch_shapes=[
            pltpu.VMEM((rows, width), f32),
            pltpu.VMEM((width, block), bf16),
            pltpu.VMEM((width, block), bf16),
            pltpu.VMEM((width, width), bf16),
        ],
        compiler_params=params("arbitrary"),
        cost_estimate=cost(4 * rows * width * hidden, 4 * width * hidden + 4 * rows * hidden + 12 * rows * width),
        name="middle_back",
    )(meta, grad_hidden, own1, *parts1, own2, *parts2, out_own, *out_parts, middle, upstream, valid, gains)


def input_back_kernel(
    meta_ref, gqkv_ref, own_ref, p0, p1, p2, p3, x_ref, grad_ref, gains_ref, out_ref, acc, whole_ref
):
    step = pl.program_id(0)
    assemble(meta_ref, whole_ref, own_ref, (p0, p1, p2, p3))
    total = dot_nt(gqkv_ref[...], whole_ref[...])

    @pl.when(step == 0)
    def _():
        acc[...] = total

    @pl.when(step > 0)
    def _():
        acc[...] += total

    @pl.when(step == pl.num_programs(0) - 1)
    def _():
        for top in range(0, acc.shape[0], 128):
            rows = slice(top, top + 128)
            scaled, inverse = normalized(x_ref[rows, :].astype(f32))
            out_ref[rows, :] = (
                grad_ref[rows, :] + norm_back(acc[rows, :], gains_ref[0:1, :], scaled, inverse)
            ).astype(bf16)


def input_back_call(meta, grad_joint, own, parts, x, grad_middle, gains):
    rows, width = x.shape
    slab = own.shape[0]
    block = width
    whole = fixed(rows, width)
    return pl.pallas_call(
        input_back_kernel,
        grid=(3 * width // block,),
        in_specs=[
            SMEM_SPEC,
            pl.BlockSpec((rows, block), lambda i: (0, i)),
            pl.BlockSpec((slab, block), lambda i: (0, i)),
        ]
        + part_specs(parts, block, lambda i: i)
        + [whole, whole, fixed(8, width)],
        out_specs=whole,
        out_shape=jax.ShapeDtypeStruct((rows, width), bf16),
        scratch_shapes=[pltpu.VMEM((rows, width), f32), pltpu.VMEM((width, block), bf16)],
        compiler_params=params("arbitrary"),
        cost_estimate=cost(6 * rows * width * width, 6 * width * width + 14 * rows * width),
        name="input_back",
    )(meta, grad_joint, own, *parts, x, grad_middle, gains)


def rope_tables(positions):
    halfway = HEAD_DIM // 2
    frequency = 10000.0 ** (-(2.0 * jnp.arange(halfway, dtype=f32)) / HEAD_DIM)
    angles = positions.astype(f32)[:, None] * frequency[None, :]
    cosine, sine = jnp.cos(angles), jnp.sin(angles)
    return (
        jnp.concatenate([cosine] * (LANES // halfway), axis=1),
        jnp.concatenate([-sine, sine] * (LANES // HEAD_DIM), axis=1),
    )


def on_device(inputs, cotangent, lengths, norm_first, w_qkv, w_out, norm_second, w_in, w_down):
    seqs, shard_rows, width = inputs.shape
    rows = seqs * shard_rows
    size = lax.axis_size("fsdp")
    me = lax.axis_index("fsdp")
    hidden = w_in.shape[1] // 2
    hidden_pad = -(-hidden // 384) * 384
    pad = hidden_pad - hidden
    block = 896 if hidden_pad % 896 == 0 else 384
    steps = link_orders()

    gains = jnp.pad(jnp.stack([norm_first, norm_second], axis=1), ((0, 0), (0, LANES - 2)))
    came_one = turned_before(row_piece([w_qkv, gains]))
    own_in = [jnp.pad(w_in[:, half * hidden :][:, :hidden], ((0, 0), (0, pad))) for half in range(2)]
    piece_two = row_piece([own_in[0], w_out])
    piece_three = row_piece([own_in[1]])
    piece_four = column_piece(w_down)

    first_row = me * shard_rows
    query_pos = first_row + jnp.arange(shard_rows, dtype=jnp.int32)
    rim_pos = first_row - WIN + jnp.arange(shard_rows + 2 * WIN, dtype=jnp.int32)
    cosine, sine = rope_tables(rim_pos)
    valid = (query_pos[None, :] < lengths[:, None]).astype(f32).reshape(rows, 1)
    meta = jnp.concatenate([jnp.stack([first_row, me, bit_value(0)]).astype(jnp.int32), lengths.astype(jnp.int32)])
    x = inputs.reshape(rows, width)
    upstream = cotangent.reshape(rows, width)
    grad_result = (upstream.astype(f32) * valid).astype(bf16)

    came_one, piece_two, piece_three, piece_four, own_in, cosine, sine, grad_result = after(
        (came_one, piece_two, piece_three, piece_four, own_in, cosine, sine, grad_result)
    )
    came_two = turned_before(piece_two)
    one = row_states(came_one)
    for bits in steps:
        one = after(widen(one, bits, 1))
    one, came_two = after((one, came_two))
    parts_one = row_parts(one)
    two = widen(row_states(came_two), steps[0], 1)
    parts_one, piece_three = after((parts_one, piece_three))
    came_three = turned_before(piece_three)

    own_rows = slice(WIN, WIN + shard_rows)
    normed_first, qkv, gains_all = qkv_call(meta, x, w_qkv, parts_one, gains, cosine[own_rows], sine[own_rows])
    two, qkv = after((two, qkv))
    by_seq = qkv.reshape(3, seqs, shard_rows, width)[1:]
    edge = (2, seqs * WIN, width)
    edge_up, edge_down, came_three = after(
        (by_seq[:, :, :WIN].reshape(edge), by_seq[:, :, shard_rows - WIN :].reshape(edge), came_three)
    )
    rim_down, rim_up = neighbours(edge_up, edge_down)
    for bits in steps[1:]:
        two = widen(two, bits, 1)
    rim_down, rim_up, piece_four = after((rim_down, rim_up, piece_four))
    came_four = turned_before(piece_four)
    attended, saved = attend_call(meta, qkv, rim_up, rim_down, seqs)
    two, attended = after((two, attended))
    parts_two = after(row_parts(two))
    parts_in_one = [part[:, :, :hidden_pad] for part in parts_two]
    parts_out = [part[:, :, hidden_pad:] for part in parts_two]
    three = widen(row_states(after(came_three, parts_two)), steps[0], 1)
    middle, normed_second, attended_split = out_call(meta, attended, w_out, parts_out, x, valid, gains_all)
    three, middle, normed_second = after((three, middle, normed_second))
    for bits in steps[1:]:
        three = widen(three, bits, 1)
    three, came_four = after((three, came_four))
    parts_three = after(row_parts(three))
    four = widen(column_states(came_four), steps[0], 1)
    mixed, slope, act = gate_call(meta, normed_second, own_in[0], parts_in_one, own_in[1], parts_three, block)
    four, mixed = after((four, mixed))
    for bits in steps[1:]:
        four = widen(four, bits, 1)

    down_give = down_call(meta, mixed, grad_result, size, hidden, block)
    down_got = flip(down_give, 0)
    four, down_got = after((four, down_got))
    parts_four = column_parts(four)
    down = down_call(meta, mixed, grad_result, size, hidden, block, down_got)
    parts_four, down = after((parts_four, down))
    down = down.reshape((size,) + (2,) * link_count() + down.shape[2:])
    cut = half_rows(hidden // size)
    down = [[down[..., :cut, :]], [down[..., cut:, :]]]
    down = [fold(part, 1, bit) for part, bit in zip(down, steps[0])]
    grad_hidden, whole_down = gate_back_call(meta, grad_result, w_down, parts_four, slope, act, block)

    give_left = half_of(normed_second, False)
    in_give = [tokens_dot(give_left, grad_hidden[half]).astype(bf16) for half in range(2)]
    down, in_give, grad_hidden = after((down, in_give, grad_hidden))
    in_got = [flip(give, 0) for give in in_give]
    for bits in steps[1:]:
        down = [fold(part, 1, bit) for part, bit in zip(down, bits)]
    keep_left = half_of(normed_second, True)
    in_state = [
        (tokens_dot(keep_left, grad_hidden[half]) + in_got[half].astype(f32)).astype(bf16)
        for half in range(2)
    ]
    down, in_state, grad_hidden = after((down, in_state, grad_hidden))
    ins = [fold(part, 1, bit) for part, bit in zip(row_blocks(in_state), steps[0])]
    owned_down = scattered(
        jnp.concatenate([part[0].reshape((size,) + part[0].shape[-2:]) for part in down], axis=1)
    )
    grad_middle, grad_branch, grad_att = middle_back_call(
        meta, grad_hidden, own_in[0], parts_in_one, own_in[1], parts_three, w_out, parts_out,
        middle, upstream, valid, gains_all, block,
    )
    out_give = tokens_dot(half_of(attended_split, False), grad_branch).astype(bf16)
    out_got, grad_branch, grad_att = after((flip(out_give, 0), grad_branch, grad_att))
    out_state = (tokens_dot(half_of(attended_split, True), grad_branch) + out_got.astype(f32)).astype(bf16)
    grad_att, out_state, owned_down = after((grad_att, out_state, owned_down))
    all_down = lax.all_gather(owned_down, "rep", axis=0)
    grad_q, grad_k, grad_v, edge_up, edge_down = attend_back_call(
        qkv, rim_up, rim_down, saved, grad_att, cosine, sine, seqs
    )
    ins, edge_up, edge_down = after((ins, edge_up, edge_down))
    from_next, from_before = neighbours(edge_up, edge_down)
    for bits in steps[1:]:
        ins = [fold(part, 1, bit) for part, bit in zip(ins, bits)]

    def with_edges(own, plane):
        own = own.reshape(seqs, shard_rows, width)
        before = from_before[plane].reshape(seqs, WIN, width).astype(f32)
        later = from_next[plane].reshape(seqs, WIN, width).astype(f32)
        rest = ((0, 0), (0, shard_rows - WIN), (0, 0))
        own = own + jnp.pad(before, rest) + jnp.pad(later, (rest[0], rest[1][::-1], rest[2]))
        return own.reshape(rows, width).astype(bf16)

    grad_joint = jnp.concatenate([grad_q, with_edges(grad_k, 0), with_edges(grad_v, 1)], axis=1)
    give_left = half_of(normed_first, False)
    qkv_give = tokens_dot(give_left, grad_joint).astype(bf16)
    qkv_got, grad_last = after((flip(qkv_give, 0), grad_joint))
    keep_left = half_of(normed_first, True)
    qkv_state = (tokens_dot(keep_left, grad_last) + qkv_got.astype(f32)).astype(bf16)
    ins, out_state, qkv_state, grad_last, mixed = after((ins, out_state, qkv_state, grad_last, mixed))
    last = [fold(part, 1, bit) for part, bit in zip(row_blocks([qkv_state, out_state]), steps[0])]

    def slots(parts):
        return jnp.stack(
            [
                jnp.concatenate([piece.reshape(size, -1, piece.shape[-1]) for piece in part], axis=-1)
                for part in parts
            ],
            axis=1,
        )

    owned_in = scattered(slots(ins))
    grad_inputs = input_back_call(meta, grad_last, w_qkv, parts_one, x, grad_middle, gains_all)
    last, grad_inputs, mixed = after((last, grad_inputs, mixed))
    for bits in steps[1:]:
        last = [fold(part, 1, bit) for part, bit in zip(last, bits)]
    result = jnp.dot(mixed, whole_down, preferred_element_type=f32)
    output = (middle + valid * result).astype(bf16)
    last, output, owned_in, all_down = after((last, output, owned_in, all_down))
    owned_last = to_owner(slots(last))

    links = 1 << link_count()

    def spread(owned):
        ones = (1,) * link_count()
        states = [owned[part].reshape(ones + owned.shape[1:]) for part in range(2)]
        for bits in steps:
            states = widen(states, bits, 0)
        mine = jnp.stack([state.reshape((-1,) + owned.shape[1:]) for state in states])
        return in_order(mine[None], flip(mine, 0)[None], 0, 0).reshape(-1, owned.shape[-1])

    grad_down = all_down.reshape(links, 2, hidden // size, -1)
    grad_down = jnp.transpose(grad_down, (2, 1, 0, 3)).reshape(hidden // size, width).astype(f32)
    grad_mid = spread(owned_in)
    grad_in = jnp.concatenate(
        [grad_mid[:, :hidden], grad_mid[:, hidden_pad : hidden_pad + hidden]], axis=1
    ).astype(f32)
    grad_second = jnp.sum(grad_in * w_in.astype(f32), axis=1) / norm_second.astype(f32)
    owned_last, grad_in, grad_down, grad_second = after((owned_last, grad_in, grad_down, grad_second))
    grad_last = spread(owned_last)
    grad_qkv = grad_last[:, : 3 * width].astype(f32)
    grad_out = grad_last[:, 3 * width :].astype(f32)
    grad_first = jnp.sum(grad_qkv * w_qkv.astype(f32), axis=1) / norm_first.astype(f32)
    return (
        output.reshape(inputs.shape),
        grad_inputs.reshape(inputs.shape),
        grad_first,
        grad_qkv,
        grad_out,
        grad_second,
        grad_in,
        grad_down,
    )


def solution(mesh):
    in_specs = (
        P("rep", "fsdp", None),
        P("rep", "fsdp", None),
        P("rep"),
        P("fsdp"),
        P("fsdp", None),
        P("fsdp", None),
        P("fsdp"),
        P("fsdp", None),
        P("fsdp", None),
    )
    out_specs = (
        P("rep", "fsdp", None),
        P("rep", "fsdp", None),
        P("fsdp"),
        P("fsdp", None),
        P("fsdp", None),
        P("fsdp"),
        P("fsdp", None),
        P("fsdp", None),
    )
    return jax.shard_map(
        on_device, mesh=mesh, in_specs=in_specs, out_specs=out_specs, check_vma=False
    )
```

```python
import functools

import jax
import jax.numpy as jnp
from jax import lax
from jax.experimental import pallas as pl
from jax.experimental.pallas import tpu as pltpu
from jax.sharding import PartitionSpec as P

HEAD_DIM = 64
WIN = 64
BLOCK_Q = 128
LANES = 128

epsilon = 1e-05
root_half = 0.7071067811865476
inv_root_two_pi = 0.3989422804014327
f32 = jnp.float32
bf16 = jnp.bfloat16
COST_SCALE = 1.0


def after(value, *before):
    return lax.optimization_barrier((value, before))[0]


def bit_count():
    return lax.axis_size("rep").bit_length() - 1


def bit_value(bit):
    return (lax.axis_index("rep") >> bit) & 1


def link_count():
    return bit_count() - 1


def link_axis(bit):
    return bit_count() - 1 - bit


def flip(value, bit):
    size = lax.axis_size("rep")
    return lax.ppermute(value, "rep", [(i, i ^ (1 << bit)) for i in range(size)])


def turn(value, steps):
    size = lax.axis_size("fsdp")
    return lax.ppermute(value, "fsdp", [(i, (i + steps) % size) for i in range(size)])


def link_orders():
    bits = list(range(1, bit_count()))
    return list(zip(bits, bits[::-1]))


def in_order(mine, got, bit, axis):
    first = bit_value(bit) == 0
    return jnp.concatenate([jnp.where(first, mine, got), jnp.where(first, got, mine)], axis=axis)


def widen(states, bits, lead):
    return [
        in_order(state, flip(state, bit), bit, lead + link_axis(bit)) for state, bit in zip(states, bits)
    ]


def row_piece(shards):
    width = sum(shard.shape[1] for shard in shards)
    links = 1 << link_count()
    core, link = bit_value(0), lax.axis_index("rep") >> 1
    views = [shard.reshape(2, 2, links, -1, shard.shape[1]) for shard in shards]
    rows = views[0].shape[3]
    pieces = [
        lax.dynamic_slice(view, (core, 0, link, 0, 0), (1, 2, 1, rows, view.shape[4])) for view in views
    ]
    return jnp.concatenate(pieces, axis=-1).reshape(2, rows, width)


def row_states(came):
    ones = (1,) * link_count()
    return [
        jnp.stack([piece[part] for piece in came]).reshape((len(came),) + ones + came[0].shape[1:])
        for part in range(2)
    ]


def row_parts(states):
    mine = [state.reshape(state.shape[0], -1, state.shape[-1]) for state in states]
    return mine + [flip(state, 0) for state in mine]


def half_rows(rows):
    return -(-rows // 2 // 16) * 16


def column_piece(shard):
    columns = shard.shape[1] // lax.axis_size("rep")
    place = (bit_value(0) << link_count()) + (lax.axis_index("rep") >> 1)
    return lax.dynamic_slice_in_dim(shard, place * columns, columns, 1)


def column_states(came):
    cut = half_rows(came[0].shape[0])
    ones = (1,) * link_count()
    stacked = jnp.stack(came)
    return [
        part.reshape(part.shape[:1] + ones + part.shape[1:]) for part in (stacked[:, :cut], stacked[:, cut:])
    ]


def column_parts(states):
    mine = [state.reshape((state.shape[0], -1) + state.shape[-2:]) for state in states]
    return mine + [flip(state, 0) for state in mine]


def whole_columns(shard, parts, pad_rows):
    size = lax.axis_size("fsdp")
    me = lax.axis_index("fsdp")
    rows, width = shard.shape
    mine, got = [jnp.concatenate(pair, axis=2) for pair in (parts[:2], parts[2:])]
    joined = in_order(mine, got, 0, 1)
    joined = jnp.transpose(joined, (0, 2, 1, 3)).reshape(size - 1, rows, width)
    whole = jnp.zeros((size * rows + pad_rows, width), shard.dtype)
    whole = lax.dynamic_update_slice(whole, shard, (me * rows, 0))
    for steps in range(1, size):
        source = lax.rem(me - steps + size, size)
        whole = lax.dynamic_update_slice(whole, joined[steps - 1], (source * rows, 0))
    return whole


def turned_before(piece, steps):
    return [turn(piece, step) for step in steps]


def runs():
    size = lax.axis_size("fsdp")
    order = sorted(range(1, size), key=lambda step: (min(step, size - step), step))
    cuts = [(size - 1) * part // 3 for part in range(4)]
    return [order[first:last] for first, last in zip(cuts, cuts[1:])]


def in_turn(states, came):
    order = [step for run in runs() for step in run]
    return states([came[order.index(step)] for step in range(1, lax.axis_size("fsdp"))])


def tokens_dot(left, right):
    return lax.dot_general(left, right, (((0,), (0,)), ((), ())), preferred_element_type=f32)


def half_of(split, mine):
    index = bit_value(0) if mine else 1 - bit_value(0)
    return lax.dynamic_index_in_dim(split, index, 0, False)


def turned_slots(slots, steps):
    size = lax.axis_size("fsdp")
    me = lax.axis_index("fsdp")
    return [
        turn(lax.dynamic_index_in_dim(slots, lax.rem(me + step, size), 0, False), step) for step in steps
    ]


def slot_sum(slots, came):
    total = lax.dynamic_index_in_dim(slots, lax.axis_index("fsdp"), 0, False).astype(f32)
    for part in came:
        total = total + part.astype(f32)
    return total.astype(bf16)


def bits_left(done):
    orders = zip(*link_orders())
    return [sorted(order[done:]) for order in orders]


def split_index(number, place):
    low = number & ((1 << place) - 1)
    return ((number >> place) << (place + 1)) | low


def halves(state, done, part):
    bit = link_orders()[done][part]
    place = bits_left(done)[part].index(bit)
    size, links = state.shape[:2]
    view = state.reshape((size, links >> (place + 1), 2, 1 << place) + state.shape[2:])
    shape = (size, links // 2) + state.shape[2:]
    keep, give = [
        lax.dynamic_index_in_dim(view, index, 2, False).reshape(shape)
        for index in (bit_value(bit), 1 - bit_value(bit))
    ]
    return keep, give


def swap(parts, done):
    return [(keep, flip(give, bit)) for (keep, give), bit in zip(parts, link_orders()[done])]


def added(keep, got):
    return (keep.astype(f32) + got.astype(f32)).astype(bf16)


def neighbours(up, down):
    size = lax.axis_size("fsdp")
    forward = [(i, i + 1) for i in range(size - 1)]
    backward = [(i + 1, i) for i in range(size - 1)]
    return lax.ppermute(up, "fsdp", backward), lax.ppermute(down, "fsdp", forward)


def params(megabytes, *semantics):
    return pltpu.CompilerParams(dimension_semantics=semantics, vmem_limit_bytes=megabytes << 20)


def cost(flops, nbytes):
    return pl.CostEstimate(flops=int(flops * COST_SCALE), bytes_accessed=int(nbytes * COST_SCALE), transcendentals=0)


def dot_nn(left, right):
    return jnp.dot(left, right, preferred_element_type=f32)


def dot_nt(left, right):
    return lax.dot_general(left, right, (((1,), (1,)), ((), ())), preferred_element_type=f32)


def normalized(values):
    centred = values - jnp.mean(values, axis=-1, keepdims=True)
    inverse = lax.rsqrt(jnp.mean(centred * centred, axis=-1, keepdims=True) + epsilon)
    return centred * inverse, inverse


def norm_back(grad_out, gain, scaled, inverse):
    grad_scaled = grad_out * gain
    return inverse * (
        grad_scaled
        - jnp.mean(grad_scaled, axis=-1, keepdims=True)
        - scaled * jnp.mean(grad_scaled * scaled, axis=-1, keepdims=True)
    )


def swapped_halves(values):
    width = values.shape[-1]
    lane = lax.broadcasted_iota(jnp.int32, values.shape, values.ndim - 1)
    ahead = pltpu.roll(values, width - HEAD_DIM // 2, values.ndim - 1)
    behind = pltpu.roll(values, HEAD_DIM // 2, values.ndim - 1)
    return jnp.where(lane % HEAD_DIM < HEAD_DIM // 2, ahead, behind)


def assemble(meta_ref, whole_ref, own_ref, part_refs):
    rows = own_ref.shape[0]
    count, quarter = part_refs[0].shape[:2]
    size = count + 1
    me, core = meta_ref[1], meta_ref[2]
    whole_ref[pl.ds(pl.multiple_of(me * rows, quarter), rows), :] = own_ref[...]
    for steps in range(1, size):
        base = lax.rem(me - steps + size, size) * rows
        for number, part_ref in enumerate(part_refs):
            half = core if number < 2 else 1 - core
            start = base + half * (rows // 2) + (number % 2) * quarter
            whole_ref[pl.ds(pl.multiple_of(start, quarter), quarter), :] = part_ref[steps - 1]


def split_columns(values, split_ref, rows, size):
    half = values.shape[1] // size // 2
    for place in range(size):
        for core in range(2):
            start = (2 * place + core) * half
            split_ref[core, rows, place * half : (place + 1) * half] = values[:, start : start + half]


def joined_columns(split_ref, rows, size):
    half = split_ref.shape[2] // size
    return jnp.concatenate(
        [
            split_ref[core, rows, place * half : (place + 1) * half]
            for place in range(size)
            for core in range(2)
        ],
        axis=1,
    )


def assemble_two(meta_ref, whole_ref, own_ref, wide_refs, narrow_refs):
    cut = wide_refs[0].shape[2]
    assemble(meta_ref, whole_ref.at[:, :cut], own_ref.at[:, :cut], wide_refs)
    assemble(meta_ref, whole_ref.at[:, cut:], own_ref.at[:, cut:], narrow_refs)


def stretch_specs(parts, start, block):
    rest = parts[0].shape[2] - start - block
    wide = part_specs(parts, block, lambda i: start // block)
    return wide + part_specs(parts, rest, lambda i: (start + block) // rest)


def part_specs(parts, block, place):
    count, quarter, _ = parts[0].shape
    return [pl.BlockSpec((count, quarter, block), lambda i: (0, 0, place(i)))] * 4


def qkv_kernel(
    meta_ref, x_ref, own_ref, p0, p1, p2, p3, gain_ref, g0, g1, g2, g3, cos_ref, sin_ref,
    split_ref, out_ref, gains_ref, whole_ref, normed_ref, column_ref, *, rope_steps, size,
):
    step = pl.program_id(0)

    @pl.when(step == 0)
    def _():
        assemble(meta_ref, column_ref, gain_ref, (g0, g1, g2, g3))
        row = lax.broadcasted_iota(jnp.int32, gains_ref.shape[:1] + (LANES,), 0)
        lane = lax.broadcasted_iota(jnp.int32, gains_ref.shape[:1] + (LANES,), 1)
        gains_ref[...] = dot_nt((row == lane).astype(f32).astype(bf16), column_ref[...])
        for top in range(0, x_ref.shape[0], 128):
            rows = slice(top, top + 128)
            scaled, _inverse = normalized(x_ref[rows, :].astype(f32))
            normed = (scaled * gains_ref[0:1, :]).astype(bf16)
            normed_ref[rows, :] = normed
            split_columns(normed, split_ref, rows, size)

    assemble(meta_ref, whole_ref, own_ref, (p0, p1, p2, p3))
    product = dot_nn(normed_ref[...], whole_ref[...])

    @pl.when(step >= rope_steps)
    def _():
        out_ref[0] = product.astype(bf16)

    @pl.when(step < rope_steps)
    def _():
        seq_rows = cos_ref.shape[0]
        cosine, sine = cos_ref[...], sin_ref[...]
        for top in range(0, product.shape[0], seq_rows):
            for lane in range(0, product.shape[1], LANES):
                tile = product[top : top + seq_rows, lane : lane + LANES]
                out_ref[0, top : top + seq_rows, lane : lane + LANES] = (
                    tile * cosine + swapped_halves(tile) * sine
                ).astype(bf16)


SMEM_SPEC = pl.BlockSpec(memory_space=pltpu.SMEM)


def fixed(*shape):
    return pl.BlockSpec(shape, lambda i: (0,) * len(shape))


def once(*shape):
    return pl.BlockSpec(shape, lambda i: (0,) * len(shape), pipeline_mode=pl.Buffered(1))


def qkv_call(meta, x, own, parts, own_gains, cosine, sine):
    rows, width = x.shape
    slab = own.shape[0]
    size = width // slab
    block = 512
    per_plane = width // block
    return pl.pallas_call(
        functools.partial(qkv_kernel, rope_steps=2 * per_plane, size=size),
        grid=(3 * per_plane,),
        in_specs=[SMEM_SPEC, once(rows, width), pl.BlockSpec((slab, block), lambda i: (0, i))]
        + part_specs(parts, block, lambda i: i)
        + [once(slab, LANES)]
        + part_specs(parts, LANES, lambda i: 3 * width // LANES)
        + [once(*cosine.shape), once(*sine.shape)],
        out_specs=[
            fixed(2, rows, width // 2),
            pl.BlockSpec((1, rows, block), lambda i: (i // per_plane, 0, i % per_plane)),
            fixed(8, width),
        ],
        out_shape=[
            jax.ShapeDtypeStruct((2, rows, width // 2), bf16),
            jax.ShapeDtypeStruct((3, rows, width), bf16),
            jax.ShapeDtypeStruct((8, width), f32),
        ],
        scratch_shapes=[
            pltpu.VMEM((width, block), bf16),
            pltpu.VMEM((rows, width), bf16),
            pltpu.VMEM((width, LANES), bf16),
        ],
        compiler_params=params(48, "arbitrary"),
        cost_estimate=cost(6 * rows * width * width, 6 * width * width + 10 * rows * width),
        name="qkv",
    )(meta, x, own, *parts, own_gains, *parts, cosine, sine)


def head_masks():
    lane = lax.broadcasted_iota(jnp.int32, (1, LANES), 1)
    first = lane < HEAD_DIM
    return first, first.astype(f32).astype(bf16), (~first).astype(f32).astype(bf16)


def two_heads(tile, low_mask, high_mask):
    return jnp.concatenate([tile * low_mask, tile * high_mask], axis=0)


def score_bias(first_row, length):
    shape = (BLOCK_Q, BLOCK_Q + 2 * WIN)
    query = first_row + lax.broadcasted_iota(jnp.int32, shape, 0)
    key = first_row - WIN + lax.broadcasted_iota(jnp.int32, shape, 1)
    near = jnp.abs(query - key) <= WIN
    live = (key >= 0) & (key < length)
    bias = jnp.where(near & (live | (query == key)), 0.0, -1e30).astype(f32)
    return jnp.concatenate([bias, bias], axis=0)


def softmax_of(queries, keys, bias):
    scores = dot_nt(queries, keys) * (HEAD_DIM**-0.5) + bias
    exponent = jnp.exp(scores - jnp.max(scores, axis=-1, keepdims=True))
    return exponent / jnp.sum(exponent, axis=-1, keepdims=True)


def attend_kernel(
    meta_ref, q_ref, k_ref, v_ref, k_up_ref, v_up_ref, k_down_ref, v_down_ref, out_ref, probs_ref
):
    length = meta_ref[1 + pl.program_id(0)]
    rows, width = q_ref.shape[1:]
    first_head, low_mask, high_mask = head_masks()
    for lane in range(0, width, LANES):
        lanes = slice(lane, lane + LANES)
        keys = jnp.concatenate([k_up_ref[0, :, lanes], k_ref[0, :, lanes], k_down_ref[0, :, lanes]], 0)
        values = jnp.concatenate([v_up_ref[0, :, lanes], v_ref[0, :, lanes], v_down_ref[0, :, lanes]], 0)
        for top in range(0, rows, BLOCK_Q):
            bias = score_bias(meta_ref[0] + top, length)
            span = slice(top, top + BLOCK_Q + 2 * WIN)
            queries = two_heads(q_ref[0, top : top + BLOCK_Q, lanes], low_mask, high_mask)
            probs = softmax_of(queries, keys[span], bias).astype(bf16)
            probs_ref[0, lane // LANES, top // BLOCK_Q] = probs
            result = dot_nn(probs, values[span])
            out_ref[top : top + BLOCK_Q, lanes] = jnp.where(
                first_head, result[:BLOCK_Q], result[BLOCK_Q:]
            ).astype(bf16)


def attention_specs(seqs, seq_rows, width, block):
    own = lambda plane: pl.BlockSpec((1, seq_rows, block), lambda s, h: (plane, s, h))
    rim = lambda plane: pl.BlockSpec((1, WIN, block), lambda s, h: (plane, s, h))
    flat = pl.BlockSpec((seq_rows, block), lambda s, h: (s, h))
    inner = (seq_rows // BLOCK_Q, 2 * BLOCK_Q, BLOCK_Q + 2 * WIN)
    probs = pl.BlockSpec((1, block // LANES) + inner, lambda s, h: (s, h, 0, 0, 0))
    probs_shape = jax.ShapeDtypeStruct((seqs, width // LANES) + inner, bf16)
    return own, rim, flat, probs, probs_shape


def attend_call(meta, qkv, rim_up, rim_down, seqs):
    _, rows, width = qkv.shape
    seq_rows = rows // seqs
    block = 256
    own, rim, flat, probs, probs_shape = attention_specs(seqs, seq_rows, width, block)
    return pl.pallas_call(
        attend_kernel,
        grid=(seqs, width // block),
        in_specs=[SMEM_SPEC, own(0), own(1), own(2), rim(0), rim(1), rim(0), rim(1)],
        out_specs=[flat, probs],
        out_shape=[jax.ShapeDtypeStruct((rows, width), bf16), probs_shape],
        compiler_params=params(48, "arbitrary", "arbitrary"),
        cost_estimate=cost(8 * rows * width * (BLOCK_Q + 2 * WIN), 10 * rows * width),
        name="attend",
    )(meta, qkv, qkv, qkv, rim_up, rim_up, rim_down, rim_down)


def attend_back_kernel(
    q_ref,
    k_ref,
    v_ref,
    k_up_ref,
    v_up_ref,
    k_down_ref,
    v_down_ref,
    probs_ref,
    go_ref,
    cos_ref,
    sin_ref,
    gq_ref,
    gk_ref,
    gv_ref,
    up_ref,
    down_ref,
    gk_acc,
    gv_acc,
):
    rows, width = q_ref.shape[1:]
    scale = HEAD_DIM**-0.5
    first_head, low_mask, high_mask = head_masks()

    def turned_back(tile, span):
        return tile * cos_ref[span, :] - swapped_halves(tile) * sin_ref[span, :]

    for lane in range(0, width, LANES):
        lanes = slice(lane, lane + LANES)
        keys = jnp.concatenate([k_up_ref[0, :, lanes], k_ref[0, :, lanes], k_down_ref[0, :, lanes]], 0)
        values = jnp.concatenate([v_up_ref[0, :, lanes], v_ref[0, :, lanes], v_down_ref[0, :, lanes]], 0)
        gk_acc[...] = jnp.zeros_like(gk_acc)
        gv_acc[...] = jnp.zeros_like(gv_acc)
        for top in range(0, rows, BLOCK_Q):
            span = slice(top, top + BLOCK_Q + 2 * WIN)
            queries = two_heads(q_ref[0, top : top + BLOCK_Q, lanes], low_mask, high_mask)
            grads = two_heads(go_ref[top : top + BLOCK_Q, lanes], low_mask, high_mask)
            probs_low = probs_ref[0, lane // LANES, top // BLOCK_Q]
            probs = probs_low.astype(f32)
            grad_probs = dot_nt(grads, values[span])
            delta = jnp.sum(probs * grad_probs, axis=-1, keepdims=True)
            grad_scores = (probs * (grad_probs - delta)).astype(bf16)
            result = dot_nn(grad_scores, keys[span])
            result = jnp.where(first_head, result[:BLOCK_Q], result[BLOCK_Q:]) * scale
            own = slice(WIN + top, WIN + top + BLOCK_Q)
            gq_ref[top : top + BLOCK_Q, lanes] = turned_back(result, own).astype(bf16)
            gk_acc[span, :] += tokens_dot(grad_scores, queries)
            gv_acc[span, :] += tokens_dot(probs_low, grads)
        grad_keys = turned_back(gk_acc[...] * scale, slice(None))
        grad_values = gv_acc[...]
        up_ref[0, :, lanes] = grad_keys[:WIN].astype(bf16)
        up_ref[1, :, lanes] = grad_values[:WIN].astype(bf16)
        down_ref[0, :, lanes] = grad_keys[WIN + rows :].astype(bf16)
        down_ref[1, :, lanes] = grad_values[WIN + rows :].astype(bf16)
        gk_ref[:, lanes] = grad_keys[WIN : WIN + rows]
        gv_ref[:, lanes] = grad_values[WIN : WIN + rows]


def attend_back_call(qkv, rim_up, rim_down, saved, grad_out, cosine, sine, seqs):
    _, rows, width = qkv.shape
    seq_rows = rows // seqs
    block = 256
    own, rim, flat, probs, probs_shape = attention_specs(seqs, seq_rows, width, block)
    table = pl.BlockSpec(cosine.shape, lambda s, h: (0, 0))
    edge = pl.BlockSpec((2, WIN, block), lambda s, h: (0, s, h))
    edge_shape = jax.ShapeDtypeStruct((2, seqs * WIN, width), bf16)
    return pl.pallas_call(
        attend_back_kernel,
        grid=(seqs, width // block),
        in_specs=[
            own(0), own(1), own(2), rim(0), rim(1), rim(0), rim(1),
            probs, flat, table, table,
        ],
        out_specs=[flat, flat, flat, edge, edge],
        out_shape=[
            jax.ShapeDtypeStruct((rows, width), bf16),
            jax.ShapeDtypeStruct((rows, width), f32),
            jax.ShapeDtypeStruct((rows, width), f32),
            edge_shape,
            edge_shape,
        ],
        scratch_shapes=[
            pltpu.VMEM((seq_rows + 2 * WIN, LANES), f32),
            pltpu.VMEM((seq_rows + 2 * WIN, LANES), f32),
        ],
        compiler_params=params(48, "arbitrary", "arbitrary"),
        cost_estimate=cost(20 * rows * width * (BLOCK_Q + 2 * WIN), 20 * rows * width),
        name="attend_back",
    )(qkv, qkv, qkv, rim_up, rim_up, rim_down, rim_down, saved, grad_out, cosine, sine)


def out_kernel(
    meta_ref, o_ref, own_ref, p0, p1, p2, p3, q0, q1, q2, q3, x_ref, valid_ref, gains_ref,
    middle_ref, n_split_ref, o_split_ref, whole_ref, *, size,
):
    @pl.when(pl.program_id(0) == 0)
    def _():
        assemble_two(meta_ref, whole_ref, own_ref, (p0, p1, p2, p3), (q0, q1, q2, q3))

    values = o_ref[...]
    split_columns(values, o_split_ref, slice(None), size)
    middle = x_ref[...].astype(f32) + valid_ref[...] * dot_nn(values, whole_ref[...])
    middle_ref[...] = middle
    scaled, _inverse = normalized(middle)
    split_columns((scaled * gains_ref[1:2, :]).astype(bf16), n_split_ref, slice(None), size)


def out_call(meta, attended, own, parts, start, stretch, x, valid, gains):
    rows, width = x.shape
    slab = own.shape[0]
    size = width // slab
    block = 128
    tile = pl.BlockSpec((block, width), lambda i: (i, 0))
    split = pl.BlockSpec((2, block, width // 2), lambda i: (0, i, 0))
    split_shape = jax.ShapeDtypeStruct((2, rows, width // 2), bf16)
    return pl.pallas_call(
        functools.partial(out_kernel, size=size),
        grid=(rows // block,),
        in_specs=[SMEM_SPEC, tile, once(slab, width)]
        + stretch_specs(parts, start, stretch)
        + [tile, pl.BlockSpec((block, 1), lambda i: (i, 0)), once(8, width)],
        out_specs=[tile, split, split],
        out_shape=[jax.ShapeDtypeStruct((rows, width), f32), split_shape, split_shape],
        scratch_shapes=[pltpu.VMEM((width, width), bf16)],
        compiler_params=params(48, "arbitrary"),
        cost_estimate=cost(2 * rows * width * width, 2 * width * width + 12 * rows * width),
        name="out_norm",
    )(meta, attended, own, *parts, *parts, x, valid, gains)


def gate_kernel(
    meta_ref, n_ref, own1_ref, p0, p1, p2, p3, own2_ref, q0, q1, q2, q3,
    mixed_ref, slope_ref, act_ref, normed_ref, first_ref, second_ref, *, size,
):
    @pl.when(pl.program_id(0) == 0)
    def _():
        for top in range(0, normed_ref.shape[0], 128):
            rows = slice(top, top + 128)
            normed_ref[rows, :] = joined_columns(n_ref, rows, size)

    assemble(meta_ref, first_ref, own1_ref, (p0, p1, p2, p3))
    assemble(meta_ref, second_ref, own2_ref, (q0, q1, q2, q3))
    gate_in = dot_nn(normed_ref[...], first_ref[...])
    gate_up = dot_nn(normed_ref[...], second_ref[...])
    normal_cdf = 0.5 * (1.0 + lax.erf(gate_in * root_half))
    density = jnp.exp(-0.5 * gate_in * gate_in) * inv_root_two_pi
    activated = gate_in * normal_cdf
    mixed_ref[...] = (activated * gate_up).astype(bf16)
    slope_ref[...] = (gate_up * (normal_cdf + gate_in * density)).astype(bf16)
    act_ref[...] = activated.astype(bf16)


def gate_call(meta, normed, owns, parts, block):
    _, rows, half = normed.shape
    width = 2 * half
    slab, hidden = owns[0].shape
    steps = hidden // block
    size = width // slab
    tile = pl.BlockSpec((rows, block), lambda i: (0, i))
    own = pl.BlockSpec((slab, block), lambda i: (0, i))
    shape = jax.ShapeDtypeStruct((rows, hidden), bf16)
    return pl.pallas_call(
        functools.partial(gate_kernel, size=size),
        grid=(hidden // block,),
        in_specs=[SMEM_SPEC, once(2, rows, half), own]
        + part_specs(parts, block, lambda i: i)
        + [own]
        + part_specs(parts, block, lambda i: i + steps),
        out_specs=[tile, tile, tile],
        out_shape=[shape, shape, shape],
        scratch_shapes=[
            pltpu.VMEM((rows, width), bf16),
            pltpu.VMEM((width, block), bf16),
            pltpu.VMEM((width, block), bf16),
        ],
        compiler_params=params(48, "arbitrary"),
        cost_estimate=cost(4 * rows * width * hidden, 4 * width * hidden + 6 * rows * hidden),
        name="gate",
    )(meta, normed, owns[0], *parts, owns[1], *parts)


def gate_back_kernel(
    meta_ref, g_ref, own_ref, p0, p1, p2, p3, slope_ref, act_ref, out_ref, whole_ref, *, block
):
    step = pl.program_id(0)

    @pl.when(step == 0)
    def _():
        rows = own_ref.shape[0]
        count, links, cut, columns = p0.shape
        size = count + 1
        me, core = meta_ref[1], meta_ref[2]
        whole_ref[size * rows :, :] = jnp.zeros_like(whole_ref[size * rows :, :])
        whole_ref[pl.ds(pl.multiple_of(me * rows, 16), rows), :] = own_ref[...]

        def put(halves):
            for steps in range(1, size):
                base = lax.rem(me - steps + size, size) * rows
                for half, parts in enumerate(halves):
                    for part, start in zip(parts, (0, cut)):
                        target = pl.ds(pl.multiple_of(base + start, 16), part.shape[2])
                        for link in range(links):
                            lane = (half * links + link) * columns
                            whole_ref[target, lane : lane + columns] = part[steps - 1, link]

        @pl.when(core == 0)
        def _():
            put(((p0, p1), (p2, p3)))

        @pl.when(core == 1)
        def _():
            put(((p2, p3), (p0, p1)))

    weight = whole_ref[pl.ds(pl.multiple_of(step * block, block), block), :]
    grad_mixed = dot_nt(g_ref[...], weight)
    out_ref[0] = (grad_mixed * slope_ref[...].astype(f32)).astype(bf16)
    out_ref[1] = (grad_mixed * act_ref[...].astype(f32)).astype(bf16)


def gate_back_plain_kernel(g_ref, w_ref, slope_ref, act_ref, out_ref):
    grad_mixed = dot_nt(g_ref[...], w_ref[...])
    out_ref[0] = (grad_mixed * slope_ref[...].astype(f32)).astype(bf16)
    out_ref[1] = (grad_mixed * act_ref[...].astype(f32)).astype(bf16)


def gate_back_call(meta, grad_result, own, parts, slope, act, block):
    rows, width = grad_result.shape
    hidden = slope.shape[1]
    tile = pl.BlockSpec((rows, block), lambda i: (0, i))
    out_spec = pl.BlockSpec((2, rows, block), lambda i: (0, 0, i))
    out_shape = jax.ShapeDtypeStruct((2, rows, hidden), bf16)
    settings = dict(
        grid=(hidden // block,),
        compiler_params=params(48, "arbitrary"),
        cost_estimate=cost(2 * rows * width * hidden, 4 * width * hidden + 8 * rows * hidden),
        name="gate_back",
    )
    if own.shape[0] % 16:
        whole = whole_columns(own, parts, hidden - own.shape[0] * (parts[0].shape[0] + 1))
        out = pl.pallas_call(
            gate_back_plain_kernel,
            in_specs=[once(rows, width), pl.BlockSpec((block, width), lambda i: (i, 0)), tile, tile],
            out_specs=out_spec,
            out_shape=out_shape,
            **settings,
        )(grad_result, whole, slope, act)
        return out, whole
    return pl.pallas_call(
        functools.partial(gate_back_kernel, block=block),
        in_specs=[SMEM_SPEC, once(rows, width), once(*own.shape)]
        + [once(*part.shape) for part in parts]
        + [tile, tile],
        out_specs=[out_spec, fixed(hidden, width)],
        out_shape=[out_shape, jax.ShapeDtypeStruct((hidden, width), bf16)],
        **settings,
    )(meta, grad_result, own, *parts, slope, act)


def down_kernel(meta_ref, m_ref, g_ref, *rest, mine, size, links, hidden, cut, places):
    step = pl.program_id(0)
    block, half = m_ref.shape[1], g_ref.shape[1] // 2
    which = meta_ref[2] if mine else 1 - meta_ref[2]
    right = g_ref[:, pl.ds(pl.multiple_of(which * half, half), half)]
    sums = tokens_dot(m_ref[...], right)
    rows, columns = hidden // size, half // links

    def put(first):
        for place in range(size):
            top, end = max(place * rows, first), min((place + 1) * rows, first + block)
            if top >= end:
                continue
            for link in range(links):
                value = sums[top - first : end - first, link * columns : (link + 1) * columns]
                rest[-1][place, link, top - place * rows : end - place * rows, :] = value.astype(bf16)

    for number in range(-(-hidden // block)):
        pl.when(step == number)(functools.partial(put, number * block))

    if mine:
        add_ref, keep0, give0, keep1, give1, state_ref = rest

        @pl.when(step == pl.num_programs(0) - 1)
        def _():
            for part, (keep_ref, give_ref) in enumerate(((keep0, give0), (keep1, give1))):
                span = slice(0, cut) if part == 0 else slice(cut, rows)
                own = meta_ref[3 + part]
                for place in range(size):
                    for number in range(links // 2):
                        base = split_index(number, places[part])
                        for ref, value in ((keep_ref, own), (give_ref, 1 - own)):
                            link = base + value * (1 << places[part])
                            ref[place, number] = added(
                                state_ref[place, link, span, :], add_ref[place, link, span, :]
                            )


def first_places():
    return [left.index(bit) for left, bit in zip(bits_left(0), link_orders()[0])]


def down_call(meta, mixed, grad_result, size, hidden, block, add=None):
    rows, hidden_pad = mixed.shape
    width = grad_result.shape[1]
    links = 1 << link_count()
    shard = hidden // size
    cut = half_rows(shard)
    columns = width // 2 // links
    shape = (size, links, shard, columns)
    mine = add is not None
    parts = [(size, links // 2, height, columns) for height in (cut, cut, shard - cut, shard - cut)]
    out = pl.pallas_call(
        functools.partial(
            down_kernel, mine=mine, size=size, links=links, hidden=hidden, cut=cut, places=first_places()
        ),
        grid=(hidden_pad // block,),
        in_specs=[SMEM_SPEC, pl.BlockSpec((rows, block), lambda i: (0, i)), once(rows, width)]
        + ([once(*shape)] if mine else []),
        out_specs=[fixed(*part) for part in parts] if mine else fixed(*shape),
        out_shape=[jax.ShapeDtypeStruct(part, bf16) for part in parts]
        if mine
        else jax.ShapeDtypeStruct(shape, bf16),
        scratch_shapes=[pltpu.VMEM(shape, bf16)] if mine else [],
        compiler_params=params(24, "arbitrary"),
        cost_estimate=cost(rows * width * hidden, width * hidden + 2 * rows * (hidden + width)),
        name="down_sum",
    )(meta, mixed, grad_result, *([add] if mine else []))
    return [(out[0], out[1]), (out[2], out[3])] if mine else out


def sum_kernel(meta_ref, left_ref, right_ref, add_ref, keep0, give0, keep1, give1, state_ref, *, size, links, places):
    state_ref[...] = (tokens_dot(left_ref[meta_ref[2]], right_ref[...]) + add_ref[...].astype(f32)).astype(bf16)
    rows = state_ref.shape[0] // (2 * size * links)
    for part, (keep_ref, give_ref) in enumerate(((keep0, give0), (keep1, give1))):
        own = meta_ref[3 + part]
        for place in range(size):
            for number in range(links // 2):
                base = (2 * place + part) * links + split_index(number, places[part])
                for ref, value in ((keep_ref, own), (give_ref, 1 - own)):
                    start = (base + value * (1 << places[part])) * rows
                    ref[place, number] = state_ref[pl.ds(pl.multiple_of(start, rows), rows), :]


def sum_call(meta, left, right, add, block):
    _, tokens, height = left.shape
    width = right.shape[1]
    size = lax.axis_size("fsdp")
    links = 1 << link_count()
    rows = height // (2 * size * links)
    if rows % 16:
        state = (tokens_dot(half_of(left, True), right) + add.astype(f32)).astype(bf16)
        state = state.reshape(size, 2, links, rows, width)
        return [halves(state[:, part], 0, part) for part in range(2)]
    shape = (size, links // 2, rows, width)
    out = pl.pallas_call(
        functools.partial(sum_kernel, size=size, links=links, places=first_places()),
        grid=(width // block,),
        in_specs=[
            SMEM_SPEC,
            once(2, tokens, height),
            pl.BlockSpec((tokens, block), lambda i: (0, i)),
            pl.BlockSpec((height, block), lambda i: (0, i)),
        ],
        out_specs=[pl.BlockSpec((size, links // 2, rows, block), lambda i: (0, 0, 0, i))] * 4,
        out_shape=[jax.ShapeDtypeStruct(shape, bf16)] * 4,
        scratch_shapes=[pltpu.VMEM((height, block), bf16)],
        compiler_params=params(12, "arbitrary"),
        cost_estimate=cost(2 * tokens * height * width, 4 * height * width + 4 * tokens * width),
        name="sum_rows",
    )(meta, left, right, add)
    return [(out[0], out[1]), (out[2], out[3])]


def fold_kernel(meta_ref, *refs, count, done, places):
    ins, outs = refs[: 4 * count], refs[4 * count :]
    for part in range(2):
        own = meta_ref[3 + 2 * done + part]
        start = 0
        for number in range(count):
            keep_ref, got_ref = ins[4 * number + 2 * part], ins[4 * number + 2 * part + 1]
            width = keep_ref.shape[3]
            for index in range(keep_ref.shape[1] // 2):
                base = split_index(index, places[part])
                for ref, value in ((outs[2 * part], own), (outs[2 * part + 1], 1 - own)):
                    link = base + value * (1 << places[part])
                    ref[0, index, :, start : start + width] = added(keep_ref[0, link], got_ref[0, link])
            start += width


def fold_next(meta, blocks, done):
    size = blocks[0][0][0].shape[0]
    places = [left.index(bit) for left, bit in zip(bits_left(done), link_orders()[done])]
    flat = [array for block in blocks for pair in block for array in pair]
    shapes = []
    for part in range(2):
        _, links, rows, _ = blocks[0][part][0].shape
        width = sum(block[part][0].shape[3] for block in blocks)
        shapes += [(size, links // 2, rows, width)] * 2
    if any(shape[2] % 16 for shape in shapes):
        result = []
        for part in range(2):
            state = jnp.concatenate([added(*block[part]) for block in blocks], axis=3)
            result.append(halves(state, done, part))
        return result
    spec = lambda shape: pl.BlockSpec((1,) + tuple(shape[1:]), lambda i: (i, 0, 0, 0))
    out = pl.pallas_call(
        functools.partial(fold_kernel, count=len(blocks), done=done, places=places),
        grid=(size,),
        in_specs=[SMEM_SPEC] + [spec(array.shape) for array in flat],
        out_specs=[spec(shape) for shape in shapes],
        out_shape=[jax.ShapeDtypeStruct(shape, bf16) for shape in shapes],
        compiler_params=params(6, "arbitrary"),
        cost_estimate=cost(0, 3 * sum(array.size for array in flat)),
        name="fold",
    )(meta, *flat)
    return [(out[0], out[1]), (out[2], out[3])]


def last_kernel(*refs):
    k0, g0, k1, g1, out_ref = refs
    cut = k0.shape[2]
    out_ref[0, :cut, :] = added(k0[0, 0], g0[0, 0])
    out_ref[0, cut:, :] = added(k1[0, 0], g1[0, 0])


def fold_last(parts):
    (k0, g0), (k1, g1) = parts
    size, _, cut, width = k0.shape
    rows = cut + k1.shape[2]
    if cut % 16 or k1.shape[2] % 16:
        return jnp.concatenate([added(k0, g0)[:, 0], added(k1, g1)[:, 0]], axis=1)
    spec = lambda array: pl.BlockSpec((1,) + array.shape[1:], lambda i: (i, 0, 0, 0))
    return pl.pallas_call(
        last_kernel,
        grid=(size,),
        in_specs=[spec(array) for array in (k0, g0, k1, g1)],
        out_specs=pl.BlockSpec((1, rows, width), lambda i: (i, 0, 0)),
        out_shape=jax.ShapeDtypeStruct((size, rows, width), bf16),
        compiler_params=params(6, "arbitrary"),
        cost_estimate=cost(0, 6 * size * rows * width),
        name="fold_last",
    )(k0, g0, k1, g1)


def middle_back_kernel(
    meta_ref, gu_ref, own1_ref, p0, p1, p2, p3, own2_ref, q0, q1, q2, q3, out_own_ref, r0, r1, r2, r3,
    s0, s1, s2, s3, middle_ref, upstream_ref, valid_ref, gains_ref, grad_ref, branch_ref, att_ref,
    acc, first_ref, second_ref, out_ref,
):
    step = pl.program_id(0)
    assemble(meta_ref, first_ref, own1_ref, (p0, p1, p2, p3))
    assemble(meta_ref, second_ref, own2_ref, (q0, q1, q2, q3))
    total = dot_nt(gu_ref[0], first_ref[...]) + dot_nt(gu_ref[1], second_ref[...])

    @pl.when(step == 0)
    def _():
        acc[...] = total
        assemble_two(meta_ref, out_ref, out_own_ref, (r0, r1, r2, r3), (s0, s1, s2, s3))

    @pl.when(step > 0)
    def _():
        acc[...] += total

    @pl.when(step == pl.num_programs(0) - 1)
    def _():
        for top in range(0, acc.shape[0], 128):
            rows = slice(top, top + 128)
            scaled, inverse = normalized(middle_ref[rows, :])
            grad = upstream_ref[rows, :].astype(f32) + norm_back(
                acc[rows, :], gains_ref[1:2, :], scaled, inverse
            )
            grad_ref[rows, :] = grad
            branch = (grad * valid_ref[rows, :]).astype(bf16)
            branch_ref[rows, :] = branch
            att_ref[rows, :] = dot_nt(branch, out_ref[...]).astype(bf16)


def middle_back_call(
    meta, grad_hidden, owns, parts, out_own, middle, upstream, valid, gains, block
):
    rows, width = middle.shape
    slab = owns[0].shape[0]
    hidden = grad_hidden.shape[2]
    steps = hidden // block
    whole = fixed(rows, width)
    own = pl.BlockSpec((slab, block), lambda i: (0, i))
    flat_low = jax.ShapeDtypeStruct((rows, width), bf16)
    return pl.pallas_call(
        middle_back_kernel,
        grid=(hidden // block,),
        in_specs=[SMEM_SPEC, pl.BlockSpec((2, rows, block), lambda i: (0, 0, i)), own]
        + part_specs(parts, block, lambda i: i)
        + [own]
        + part_specs(parts, block, lambda i: i + steps)
        + [once(slab, width)]
        + stretch_specs(parts, 2 * hidden, block)
        + [whole, whole, once(rows, 1), once(8, width)],
        out_specs=[whole, whole, whole],
        out_shape=[jax.ShapeDtypeStruct((rows, width), f32), flat_low, flat_low],
        scratch_shapes=[
            pltpu.VMEM((rows, width), f32),
            pltpu.VMEM((width, block), bf16),
            pltpu.VMEM((width, block), bf16),
            pltpu.VMEM((width, width), bf16),
        ],
        compiler_params=params(40, "arbitrary"),
        cost_estimate=cost(4 * rows * width * hidden, 4 * width * hidden + 4 * rows * hidden + 12 * rows * width),
        name="middle_back",
    )(meta, grad_hidden, owns[0], *parts, owns[1], *parts, out_own, *parts, *parts, middle, upstream, valid, gains)


def input_back_kernel(
    meta_ref, gqkv_ref, own_ref, p0, p1, p2, p3, x_ref, grad_ref, gains_ref, out_ref, acc, whole_ref
):
    step = pl.program_id(0)
    assemble(meta_ref, whole_ref, own_ref, (p0, p1, p2, p3))
    total = dot_nt(gqkv_ref[...], whole_ref[...])

    @pl.when(step == 0)
    def _():
        acc[...] = total

    @pl.when(step > 0)
    def _():
        acc[...] += total

    @pl.when(step == pl.num_programs(0) - 1)
    def _():
        for top in range(0, acc.shape[0], 128):
            rows = slice(top, top + 128)
            scaled, inverse = normalized(x_ref[rows, :].astype(f32))
            out_ref[rows, :] = (
                grad_ref[rows, :] + norm_back(acc[rows, :], gains_ref[0:1, :], scaled, inverse)
            ).astype(bf16)


def input_back_call(meta, grad_joint, own, parts, x, grad_middle, gains):
    rows, width = x.shape
    slab = own.shape[0]
    block = width
    whole = fixed(rows, width)
    return pl.pallas_call(
        input_back_kernel,
        grid=(3 * width // block,),
        in_specs=[
            SMEM_SPEC,
            pl.BlockSpec((rows, block), lambda i: (0, i)),
            pl.BlockSpec((slab, block), lambda i: (0, i)),
        ]
        + part_specs(parts, block, lambda i: i)
        + [whole, whole, once(8, width)],
        out_specs=whole,
        out_shape=jax.ShapeDtypeStruct((rows, width), bf16),
        scratch_shapes=[pltpu.VMEM((rows, width), f32), pltpu.VMEM((width, block), bf16)],
        compiler_params=params(48, "arbitrary"),
        cost_estimate=cost(6 * rows * width * width, 6 * width * width + 14 * rows * width),
        name="input_back",
    )(meta, grad_joint, own, *parts, x, grad_middle, gains)


def rope_tables(positions):
    halfway = HEAD_DIM // 2
    frequency = 10000.0 ** (-(2.0 * jnp.arange(halfway, dtype=f32)) / HEAD_DIM)
    angles = positions.astype(f32)[:, None] * frequency[None, :]
    cosine, sine = jnp.cos(angles), jnp.sin(angles)
    return (
        jnp.concatenate([cosine] * (LANES // halfway), axis=1),
        jnp.concatenate([-sine, sine] * (LANES // HEAD_DIM), axis=1),
    )


def on_device(inputs, cotangent, lengths, norm_first, w_qkv, w_out, norm_second, w_in, w_down):
    seqs, shard_rows, width = inputs.shape
    rows = seqs * shard_rows
    size = lax.axis_size("fsdp")
    me = lax.axis_index("fsdp")
    hidden = w_in.shape[1] // 2
    block = 896
    hidden_pad = -(-hidden // block) * block
    pad = hidden_pad - hidden
    steps = link_orders()
    near, far, middle_way = runs()

    gains = jnp.pad(jnp.stack([norm_first, norm_second], axis=1), ((0, 0), (0, LANES - 2)))
    came_one = turned_before(row_piece([w_qkv, gains]), range(1, size))
    own_in = [jnp.pad(w_in[:, half * hidden :][:, :hidden], ((0, 0), (0, pad))) for half in range(2)]
    piece_two = row_piece([own_in[0], own_in[1], w_out])
    piece_three = column_piece(w_down)
    first_row = me * shard_rows
    query_pos = first_row + jnp.arange(shard_rows, dtype=jnp.int32)
    rim_pos = first_row - WIN + jnp.arange(shard_rows + 2 * WIN, dtype=jnp.int32)
    cosine, sine = rope_tables(rim_pos)
    valid = (query_pos[None, :] < lengths[:, None]).astype(f32).reshape(rows, 1)
    bits = [bit_value(bit) for pair in steps for bit in pair]
    meta = jnp.stack([first_row, me, bit_value(0)] + bits).astype(jnp.int32)
    meta_rows = jnp.concatenate([first_row.astype(jnp.int32)[None], lengths.astype(jnp.int32)])
    x = inputs.reshape(rows, width)
    upstream = cotangent.reshape(rows, width)
    grad_result = (upstream.astype(f32) * valid).astype(bf16)
    own_rows = slice(WIN, WIN + shard_rows)
    own_cosine, own_sine = cosine[own_rows], sine[own_rows]
    came_one, piece_two, piece_three, own_in, gains, cosine, sine, own_cosine, own_sine, grad_result, valid = after(
        (came_one, piece_two, piece_three, own_in, gains, cosine, sine, own_cosine, own_sine, grad_result, valid)
    )

    one = widen(row_states(came_one), steps[0], 1)
    came_two = turned_before(piece_two, near)
    one, came_two, piece_two = after((one, came_two, piece_two))

    for bits in steps[1:]:
        one = widen(one, bits, 1)
    came_two = came_two + turned_before(piece_two, far)
    one, came_two, piece_two = after((one, came_two, piece_two))

    parts_one = row_parts(one)
    came_two = came_two + turned_before(piece_two, middle_way)
    normed_first, qkv, gains_all = qkv_call(meta, x, w_qkv, parts_one, gains, own_cosine, own_sine)
    by_seq = qkv.reshape(3, seqs, shard_rows, width)[1:]
    edge = (2, seqs * WIN, width)
    edge_up, edge_down = by_seq[:, :, :WIN].reshape(edge), by_seq[:, :, shard_rows - WIN :].reshape(edge)
    qkv, edge_up, edge_down, came_two, piece_three = after((qkv, edge_up, edge_down, came_two, piece_three))

    rim_down, rim_up = neighbours(edge_up, edge_down)
    two = widen(in_turn(row_states, came_two), steps[0], 1)
    rim_down, rim_up, two, piece_three = after((rim_down, rim_up, two, piece_three))

    for bits in steps[1:]:
        two = widen(two, bits, 1)
    came_three = turned_before(piece_three, range(1, size))
    attended, saved = attend_call(meta_rows, qkv, rim_up, rim_down, seqs)
    two, came_three, attended = after((two, came_three, attended))

    parts_two = row_parts(two)
    three = widen(column_states(came_three), steps[0], 1)
    parts_two, three, attended = after((parts_two, three, attended))

    for bits in steps[1:]:
        three = widen(three, bits, 1)
    middle, normed_second, attended_split = out_call(
        meta, attended, w_out, parts_two, 2 * hidden_pad, block, x, valid, gains_all
    )
    mixed, slope, act = gate_call(meta, normed_second, own_in, parts_two, block)
    three, mixed, slope, act, normed_second = after((three, mixed, slope, act, normed_second))

    parts_three = column_parts(three)
    down_give = down_call(meta, mixed, grad_result, size, hidden, block)
    down_got = flip(down_give, 0)
    parts_three, down_got, slope, mixed = after((parts_three, down_got, slope, mixed))

    down = down_call(meta, mixed, grad_result, size, hidden, block, down_got)
    down, slope, mixed = after((down, slope, mixed))

    down = swap(down, 0)
    grad_hidden, whole_down = gate_back_call(meta, grad_result, w_down, parts_three, slope, act, block)
    give_left = half_of(normed_second, False)
    in_give = [tokens_dot(give_left, grad_hidden[half]).astype(bf16) for half in range(2)]
    down, in_give, grad_hidden, whole_down, mixed, normed_second = after(
        (down, in_give, grad_hidden, whole_down, mixed, normed_second)
    )

    in_got = [flip(give, 0) for give in in_give]
    for done in range(1, len(steps)):
        down = swap(fold_next(meta, [down], done), done)
    result = jnp.dot(mixed, whole_down, preferred_element_type=f32)
    output = (middle + valid * result).astype(bf16)
    in_got, output, grad_hidden, normed_second, down = after((in_got, output, grad_hidden, normed_second, down))

    one, two = [sum_call(meta, normed_second, grad_hidden[half], in_got[half], block) for half in range(2)]
    one, two, grad_hidden = after((one, two, grad_hidden))

    one = swap(one, 0)
    down_slots = fold_last(down)
    down_came = turned_slots(down_slots, range(1, size))
    grad_middle, grad_branch, grad_att = middle_back_call(
        meta, grad_hidden, own_in, parts_two, w_out, middle, upstream, valid, gains_all, block
    )
    one, two, down_came, grad_branch, grad_att = after((one, two, down_came, grad_branch, grad_att))

    two = swap(two, 0)
    for done in range(1, len(steps)):
        one = swap(fold_next(meta, [one], done), done)
    out_give = tokens_dot(half_of(attended_split, False), grad_branch).astype(bf16)
    out_got, grad_branch, grad_att = after((flip(out_give, 0), grad_branch, grad_att))
    outs = sum_call(meta, attended_split, grad_branch, out_got, width // 2)
    grad_att, outs = after((grad_att, outs))
    grad_q, grad_k, grad_v, edge_up, edge_down = attend_back_call(
        qkv, rim_up, rim_down, saved, grad_att, cosine, sine, seqs
    )
    one, two, outs, edge_up, edge_down, grad_q = after((one, two, outs, edge_up, edge_down, grad_q))

    for done in range(1, len(steps)):
        two = swap(fold_next(meta, [two], done), done)
    from_next, from_before = neighbours(edge_up, edge_down)
    one_slots = fold_last(one)
    from_next, from_before, two, one_slots, outs = after((from_next, from_before, two, one_slots, outs))

    def with_edges(own, plane):
        own = own.reshape(seqs, shard_rows, width)
        before = from_before[plane].reshape(seqs, WIN, width).astype(f32)
        later = from_next[plane].reshape(seqs, WIN, width).astype(f32)
        rest = ((0, 0), (0, shard_rows - WIN), (0, 0))
        own = own + jnp.pad(before, rest) + jnp.pad(later, (rest[0], rest[1][::-1], rest[2]))
        return own.reshape(rows, width).astype(bf16)

    outs = swap(outs, 0)
    one_came = turned_slots(one_slots, near) + turned_slots(one_slots, far)
    grad_joint = jnp.concatenate([grad_q, with_edges(grad_k, 0), with_edges(grad_v, 1)], axis=1)
    give_left = half_of(normed_first, False)
    qkv_give = tokens_dot(give_left, grad_joint).astype(bf16)
    qkv_got, grad_last = after((flip(qkv_give, 0), grad_joint))
    last = sum_call(meta, normed_first, grad_last, qkv_got, width)
    two_slots = fold_last(two)
    last, grad_last, outs, one_came, two_slots, one_slots = after(
        (last, grad_last, outs, one_came, two_slots, one_slots)
    )

    last = swap(last, 0)
    one_came = one_came + turned_slots(one_slots, middle_way)
    two_came = turned_slots(two_slots, near) + turned_slots(two_slots, far)
    grad_inputs = input_back_call(meta, grad_last, w_qkv, parts_one, x, grad_middle, gains_all)
    last, grad_inputs, one_came, two_came, one_slots, two_slots = after(
        (last, grad_inputs, one_came, two_came, one_slots, two_slots)
    )

    def spread_start(owned, cut):
        ones = (1,) * link_count()
        return [part.reshape(ones + part.shape) for part in (owned[:cut], owned[cut:])]

    def spread_end(states):
        mine = jnp.stack([state.reshape((-1,) + state.shape[-2:]) for state in states])
        whole = in_order(mine[None], flip(mine, 0)[None], 0, 0)
        return whole.reshape(-1, mine.shape[-1])

    last = [last, outs]
    for done in range(1, len(steps)):
        last = [swap(fold_next(meta, last, done), done)]
    two_came = two_came + turned_slots(two_slots, middle_way)
    owned_down = slot_sum(down_slots, down_came)
    spread_down = widen(spread_start(owned_down, half_rows(hidden // size)), steps[0], 0)
    owned_one = slot_sum(one_slots, one_came)
    last, two_came, owned_one, spread_down = after((last, two_came, owned_one, spread_down))

    last_slots = fold_last(last[0])
    last_came = turned_slots(last_slots, near) + turned_slots(last_slots, far)
    owned_in = jnp.concatenate([owned_one, slot_sum(two_slots, two_came)], axis=1)
    spread_in = widen(spread_start(owned_in, owned_in.shape[0] // 2), steps[0], 0)
    last_came, spread_in, last_slots, spread_down = after((last_came, spread_in, last_slots, spread_down))

    last_came = last_came + turned_slots(last_slots, middle_way)
    for bits in steps[1:]:
        spread_in = widen(spread_in, bits, 0)
        spread_down = widen(spread_down, bits, 0)
    last_came, spread_in, last_slots, spread_down = after((last_came, spread_in, last_slots, spread_down))

    owned_last = slot_sum(last_slots, last_came)
    spread_last = widen(spread_start(owned_last, owned_last.shape[0] // 2), steps[0], 0)
    down_mine = jnp.concatenate([state.reshape((-1,) + state.shape[-2:]) for state in spread_down], axis=1)
    grad_down = in_order(down_mine, flip(down_mine, 0), 0, 0)
    grad_in = spread_end(spread_in)
    spread_last, grad_in, grad_down = after((spread_last, grad_in, grad_down))

    for bits in steps[1:]:
        spread_last = widen(spread_last, bits, 0)
    spread_last, grad_in, grad_down = after((spread_last, grad_in, grad_down))

    grad_last = spread_end(spread_last)
    grad_in = jnp.concatenate(
        [grad_in[:, :hidden], grad_in[:, hidden_pad : hidden_pad + hidden]], axis=1
    ).astype(f32)
    grad_second = jnp.sum(grad_in * w_in.astype(f32), axis=1) / norm_second.astype(f32)
    grad_down = jnp.transpose(grad_down, (1, 0, 2)).reshape(hidden // size, width).astype(f32)
    grad_qkv = grad_last[:, : 3 * width].astype(f32)
    grad_out = grad_last[:, 3 * width :].astype(f32)
    grad_first = jnp.sum(grad_qkv * w_qkv.astype(f32), axis=1) / norm_first.astype(f32)
    return (
        output.reshape(inputs.shape),
        grad_inputs.reshape(inputs.shape),
        grad_first,
        grad_qkv,
        grad_out,
        grad_second,
        grad_in,
        grad_down,
    )


def solution(mesh):
    in_specs = (
        P("rep", "fsdp", None),
        P("rep", "fsdp", None),
        P("rep"),
        P("fsdp"),
        P("fsdp", None),
        P("fsdp", None),
        P("fsdp"),
        P("fsdp", None),
        P("fsdp", None),
    )
    out_specs = (
        P("rep", "fsdp", None),
        P("rep", "fsdp", None),
        P("fsdp"),
        P("fsdp", None),
        P("fsdp", None),
        P("fsdp"),
        P("fsdp", None),
        P("fsdp", None),
    )
    return jax.shard_map(
        on_device, mesh=mesh, in_specs=in_specs, out_specs=out_specs, check_vma=False
    )
```

```python
import functools

import jax
import jax.numpy as jnp
from jax import lax
from jax.experimental import pallas as pl
from jax.experimental.pallas import tpu as pltpu
from jax.sharding import PartitionSpec as P

HEAD_DIM = 64
WIN = 64
BLOCK_Q = 128
LANES = 128

epsilon = 1e-05
root_half = 0.7071067811865476
inv_root_two_pi = 0.3989422804014327
f32 = jnp.float32
bf16 = jnp.bfloat16
COST_SCALE = 1.0


def after(value, *before):
    return lax.optimization_barrier((value, before))[0]


def bit_count():
    return lax.axis_size("rep").bit_length() - 1


def bit_value(bit):
    return (lax.axis_index("rep") >> bit) & 1


def link_count():
    return bit_count() - 1


def link_axis(bit):
    return bit_count() - 1 - bit


def flip(value, bit):
    size = lax.axis_size("rep")
    return lax.ppermute(value, "rep", [(i, i ^ (1 << bit)) for i in range(size)])


def turn(value, steps):
    size = lax.axis_size("fsdp")
    return lax.ppermute(value, "fsdp", [(i, (i + steps) % size) for i in range(size)])


def link_orders():
    bits = list(range(1, bit_count()))
    return list(zip(bits, bits[::-1]))


def in_order(mine, got, bit, axis):
    first = bit_value(bit) == 0
    return jnp.concatenate([jnp.where(first, mine, got), jnp.where(first, got, mine)], axis=axis)


def widen(states, bits, lead):
    return [
        in_order(state, flip(state, bit), bit, lead + link_axis(bit)) for state, bit in zip(states, bits)
    ]


def row_piece(shards):
    width = sum(shard.shape[1] for shard in shards)
    links = 1 << link_count()
    core, link = bit_value(0), lax.axis_index("rep") >> 1
    views = [shard.reshape(2, 2, links, -1, shard.shape[1]) for shard in shards]
    rows = views[0].shape[3]
    pieces = [
        lax.dynamic_slice(view, (core, 0, link, 0, 0), (1, 2, 1, rows, view.shape[4])) for view in views
    ]
    return jnp.concatenate(pieces, axis=-1).reshape(2, rows, width)


def row_states(came):
    ones = (1,) * link_count()
    return [
        jnp.stack([piece[part] for piece in came]).reshape((len(came),) + ones + came[0].shape[1:])
        for part in range(2)
    ]


def row_parts(states):
    mine = [state.reshape(state.shape[0], -1, state.shape[-1]) for state in states]
    return mine + [flip(state, 0) for state in mine]


def half_rows(rows):
    return -(-rows // 2 // 16) * 16


def column_piece(shard):
    columns = shard.shape[1] // lax.axis_size("rep")
    place = (bit_value(0) << link_count()) + (lax.axis_index("rep") >> 1)
    return lax.dynamic_slice_in_dim(shard, place * columns, columns, 1)


def column_states(came):
    cut = half_rows(came[0].shape[0])
    ones = (1,) * link_count()
    stacked = jnp.stack(came)
    return [
        part.reshape(part.shape[:1] + ones + part.shape[1:]) for part in (stacked[:, :cut], stacked[:, cut:])
    ]


def column_parts(states):
    mine = [state.reshape((state.shape[0], -1) + state.shape[-2:]) for state in states]
    return mine + [flip(state, 0) for state in mine]


def whole_columns(shard, parts, pad_rows):
    size = lax.axis_size("fsdp")
    me = lax.axis_index("fsdp")
    rows, width = shard.shape
    mine, got = [jnp.concatenate(pair, axis=2) for pair in (parts[:2], parts[2:])]
    joined = in_order(mine, got, 0, 1)
    joined = jnp.transpose(joined, (0, 2, 1, 3)).reshape(size - 1, rows, width)
    whole = jnp.zeros((size * rows + pad_rows, width), shard.dtype)
    whole = lax.dynamic_update_slice(whole, shard, (me * rows, 0))
    for steps in range(1, size):
        source = lax.rem(me - steps + size, size)
        whole = lax.dynamic_update_slice(whole, joined[steps - 1], (source * rows, 0))
    return whole


def turned_before(piece, steps):
    return [turn(piece, step) for step in steps]


def runs():
    size = lax.axis_size("fsdp")
    order = sorted(range(1, size), key=lambda step: (min(step, size - step), step))
    cuts = [(size - 1) * part // 3 for part in range(4)]
    return [order[first:last] for first, last in zip(cuts, cuts[1:])]


def in_turn(states, came):
    order = [step for run in runs() for step in run]
    return states([came[order.index(step)] for step in range(1, lax.axis_size("fsdp"))])


def tokens_dot(left, right):
    return lax.dot_general(left, right, (((0,), (0,)), ((), ())), preferred_element_type=f32)


def half_of(split, mine):
    index = bit_value(0) if mine else 1 - bit_value(0)
    return lax.dynamic_index_in_dim(split, index, 0, False)


def turned_slots(slots, steps):
    size = lax.axis_size("fsdp")
    me = lax.axis_index("fsdp")
    return [
        turn(lax.dynamic_index_in_dim(slots, lax.rem(me + step, size), 0, False), step) for step in steps
    ]


def slot_sum(slots, came):
    total = lax.dynamic_index_in_dim(slots, lax.axis_index("fsdp"), 0, False).astype(f32)
    for part in came:
        total = total + part.astype(f32)
    return total.astype(bf16)


def bits_left(done):
    orders = zip(*link_orders())
    return [sorted(order[done:]) for order in orders]


def split_index(number, place):
    low = number & ((1 << place) - 1)
    return ((number >> place) << (place + 1)) | low


def halves(state, done, part):
    bit = link_orders()[done][part]
    place = bits_left(done)[part].index(bit)
    size, links = state.shape[:2]
    view = state.reshape((size, links >> (place + 1), 2, 1 << place) + state.shape[2:])
    shape = (size, links // 2) + state.shape[2:]
    keep, give = [
        lax.dynamic_index_in_dim(view, index, 2, False).reshape(shape)
        for index in (bit_value(bit), 1 - bit_value(bit))
    ]
    return keep, give


def swap(parts, done):
    return [(keep, flip(give, bit)) for (keep, give), bit in zip(parts, link_orders()[done])]


def added(keep, got):
    return (keep.astype(f32) + got.astype(f32)).astype(bf16)


def neighbours(up, down):
    size = lax.axis_size("fsdp")
    forward = [(i, i + 1) for i in range(size - 1)]
    backward = [(i + 1, i) for i in range(size - 1)]
    return lax.ppermute(up, "fsdp", backward), lax.ppermute(down, "fsdp", forward)


def params(megabytes, *semantics):
    return pltpu.CompilerParams(dimension_semantics=semantics, vmem_limit_bytes=megabytes << 20)


def cost(flops, nbytes):
    return pl.CostEstimate(flops=int(flops * COST_SCALE), bytes_accessed=int(nbytes * COST_SCALE), transcendentals=0)


def far(*arrays):
    return [pltpu.with_memory_space_constraint(array, pltpu.HBM) for array in arrays]


def dot_nn(left, right):
    return jnp.dot(left, right, preferred_element_type=f32)


def dot_nt(left, right):
    return lax.dot_general(left, right, (((1,), (1,)), ((), ())), preferred_element_type=f32)


def normalized(values):
    centred = values - jnp.mean(values, axis=-1, keepdims=True)
    inverse = lax.rsqrt(jnp.mean(centred * centred, axis=-1, keepdims=True) + epsilon)
    return centred * inverse, inverse


def norm_back(grad_out, gain, scaled, inverse):
    grad_scaled = grad_out * gain
    return inverse * (
        grad_scaled
        - jnp.mean(grad_scaled, axis=-1, keepdims=True)
        - scaled * jnp.mean(grad_scaled * scaled, axis=-1, keepdims=True)
    )


def swapped_halves(values):
    width = values.shape[-1]
    lane = lax.broadcasted_iota(jnp.int32, values.shape, values.ndim - 1)
    ahead = pltpu.roll(values, width - HEAD_DIM // 2, values.ndim - 1)
    behind = pltpu.roll(values, HEAD_DIM // 2, values.ndim - 1)
    return jnp.where(lane % HEAD_DIM < HEAD_DIM // 2, ahead, behind)


def assemble(meta_ref, whole_ref, own_ref, part_refs):
    rows = own_ref.shape[0]
    count, quarter = part_refs[0].shape[:2]
    size = count + 1
    me, core = meta_ref[1], meta_ref[2]
    whole_ref[pl.ds(pl.multiple_of(me * rows, quarter), rows), :] = own_ref[...]
    for steps in range(1, size):
        base = lax.rem(me - steps + size, size) * rows
        for number, part_ref in enumerate(part_refs):
            half = core if number < 2 else 1 - core
            start = base + half * (rows // 2) + (number % 2) * quarter
            whole_ref[pl.ds(pl.multiple_of(start, quarter), quarter), :] = part_ref[steps - 1]


def split_columns(values, split_ref, rows, size):
    half = values.shape[1] // size // 2
    for place in range(size):
        for core in range(2):
            start = (2 * place + core) * half
            split_ref[core, rows, place * half : (place + 1) * half] = values[:, start : start + half]


def joined_columns(split_ref, rows, size):
    half = split_ref.shape[2] // size
    return jnp.concatenate(
        [
            split_ref[core, rows, place * half : (place + 1) * half]
            for place in range(size)
            for core in range(2)
        ],
        axis=1,
    )


def assemble_two(meta_ref, whole_ref, own_ref, wide_refs, narrow_refs):
    cut = wide_refs[0].shape[2]
    assemble(meta_ref, whole_ref.at[:, :cut], own_ref.at[:, :cut], wide_refs)
    assemble(meta_ref, whole_ref.at[:, cut:], own_ref.at[:, cut:], narrow_refs)


def stretch_specs(parts, start, block):
    rest = parts[0].shape[2] - start - block
    wide = part_specs(parts, block, lambda i: start // block)
    return wide + part_specs(parts, rest, lambda i: (start + block) // rest)


def part_specs(parts, block, place):
    count, quarter, _ = parts[0].shape
    return [pl.BlockSpec((count, quarter, block), lambda i: (0, 0, place(i)))] * 4


def qkv_kernel(
    meta_ref, x_ref, own_ref, p0, p1, p2, p3, gain_ref, g0, g1, g2, g3, cos_ref, sin_ref,
    split_ref, out_ref, gains_ref, whole_ref, normed_ref, column_ref, *, rope_steps, size,
):
    step = pl.program_id(0)

    @pl.when(step == 0)
    def _():
        assemble(meta_ref, column_ref, gain_ref, (g0, g1, g2, g3))
        row = lax.broadcasted_iota(jnp.int32, gains_ref.shape[:1] + (LANES,), 0)
        lane = lax.broadcasted_iota(jnp.int32, gains_ref.shape[:1] + (LANES,), 1)
        gains_ref[...] = dot_nt((row == lane).astype(f32).astype(bf16), column_ref[...])
        for top in range(0, x_ref.shape[0], 128):
            rows = slice(top, top + 128)
            scaled, _inverse = normalized(x_ref[rows, :].astype(f32))
            normed = (scaled * gains_ref[0:1, :]).astype(bf16)
            normed_ref[rows, :] = normed
            split_columns(normed, split_ref, rows, size)

    assemble(meta_ref, whole_ref, own_ref, (p0, p1, p2, p3))
    product = dot_nn(normed_ref[...], whole_ref[...])

    @pl.when(step >= rope_steps)
    def _():
        out_ref[0] = product.astype(bf16)

    @pl.when(step < rope_steps)
    def _():
        seq_rows = cos_ref.shape[0]
        cosine, sine = cos_ref[...], sin_ref[...]
        for top in range(0, product.shape[0], seq_rows):
            for lane in range(0, product.shape[1], LANES):
                tile = product[top : top + seq_rows, lane : lane + LANES]
                out_ref[0, top : top + seq_rows, lane : lane + LANES] = (
                    tile * cosine + swapped_halves(tile) * sine
                ).astype(bf16)


SMEM_SPEC = pl.BlockSpec(memory_space=pltpu.SMEM)


def fixed(*shape):
    return pl.BlockSpec(shape, lambda i: (0,) * len(shape))


def once(*shape):
    return pl.BlockSpec(shape, lambda i: (0,) * len(shape), pipeline_mode=pl.Buffered(1))


def qkv_call(meta, x, own, parts, own_gains, cosine, sine):
    rows, width = x.shape
    slab = own.shape[0]
    size = width // slab
    block = 512
    per_plane = width // block
    return pl.pallas_call(
        functools.partial(qkv_kernel, rope_steps=2 * per_plane, size=size),
        grid=(3 * per_plane,),
        in_specs=[SMEM_SPEC, once(rows, width), pl.BlockSpec((slab, block), lambda i: (0, i))]
        + part_specs(parts, block, lambda i: i)
        + [once(slab, LANES)]
        + part_specs(parts, LANES, lambda i: 3 * width // LANES)
        + [once(*cosine.shape), once(*sine.shape)],
        out_specs=[
            fixed(2, rows, width // 2),
            pl.BlockSpec((1, rows, block), lambda i: (i // per_plane, 0, i % per_plane)),
            fixed(8, width),
        ],
        out_shape=[
            jax.ShapeDtypeStruct((2, rows, width // 2), bf16),
            jax.ShapeDtypeStruct((3, rows, width), bf16),
            jax.ShapeDtypeStruct((8, width), f32),
        ],
        scratch_shapes=[
            pltpu.VMEM((width, block), bf16),
            pltpu.VMEM((rows, width), bf16),
            pltpu.VMEM((width, LANES), bf16),
        ],
        compiler_params=params(20, "arbitrary"),
        cost_estimate=cost(6 * rows * width * width, 6 * width * width + 10 * rows * width),
        name="qkv",
    )(meta, *far(x, own, *parts), own_gains, *far(*parts), cosine, sine)


def head_masks():
    lane = lax.broadcasted_iota(jnp.int32, (1, LANES), 1)
    first = lane < HEAD_DIM
    return first, first.astype(f32).astype(bf16), (~first).astype(f32).astype(bf16)


def two_heads(tile, low_mask, high_mask):
    return jnp.concatenate([tile * low_mask, tile * high_mask], axis=0)


def score_bias(first_row, length):
    shape = (BLOCK_Q, BLOCK_Q + 2 * WIN)
    query = first_row + lax.broadcasted_iota(jnp.int32, shape, 0)
    key = first_row - WIN + lax.broadcasted_iota(jnp.int32, shape, 1)
    near = jnp.abs(query - key) <= WIN
    live = (key >= 0) & (key < length)
    bias = jnp.where(near & (live | (query == key)), 0.0, -1e30).astype(f32)
    return jnp.concatenate([bias, bias], axis=0)


def softmax_of(queries, keys, bias):
    scores = dot_nt(queries, keys) * (HEAD_DIM**-0.5) + bias
    exponent = jnp.exp(scores - jnp.max(scores, axis=-1, keepdims=True))
    return exponent / jnp.sum(exponent, axis=-1, keepdims=True)


def attend_kernel(
    meta_ref, q_ref, k_ref, v_ref, k_up_ref, v_up_ref, k_down_ref, v_down_ref, out_ref, probs_ref
):
    length = meta_ref[1 + pl.program_id(0)]
    rows, width = q_ref.shape[1:]
    first_head, low_mask, high_mask = head_masks()
    for lane in range(0, width, LANES):
        lanes = slice(lane, lane + LANES)
        keys = jnp.concatenate([k_up_ref[0, :, lanes], k_ref[0, :, lanes], k_down_ref[0, :, lanes]], 0)
        values = jnp.concatenate([v_up_ref[0, :, lanes], v_ref[0, :, lanes], v_down_ref[0, :, lanes]], 0)
        for top in range(0, rows, BLOCK_Q):
            bias = score_bias(meta_ref[0] + top, length)
            span = slice(top, top + BLOCK_Q + 2 * WIN)
            queries = two_heads(q_ref[0, top : top + BLOCK_Q, lanes], low_mask, high_mask)
            probs = softmax_of(queries, keys[span], bias).astype(bf16)
            probs_ref[0, lane // LANES, top // BLOCK_Q] = probs
            result = dot_nn(probs, values[span])
            out_ref[top : top + BLOCK_Q, lanes] = jnp.where(
                first_head, result[:BLOCK_Q], result[BLOCK_Q:]
            ).astype(bf16)


def attention_specs(seqs, seq_rows, width, block):
    own = lambda plane: pl.BlockSpec((1, seq_rows, block), lambda s, h: (plane, s, h))
    rim = lambda plane: pl.BlockSpec((1, WIN, block), lambda s, h: (plane, s, h))
    flat = pl.BlockSpec((seq_rows, block), lambda s, h: (s, h))
    inner = (seq_rows // BLOCK_Q, 2 * BLOCK_Q, BLOCK_Q + 2 * WIN)
    probs = pl.BlockSpec((1, block // LANES) + inner, lambda s, h: (s, h, 0, 0, 0))
    probs_shape = pltpu.HBM((seqs, width // LANES) + inner, bf16)
    return own, rim, flat, probs, probs_shape


def attend_call(meta, qkv, rim_up, rim_down, seqs):
    _, rows, width = qkv.shape
    seq_rows = rows // seqs
    block = 256
    own, rim, flat, probs, probs_shape = attention_specs(seqs, seq_rows, width, block)
    return pl.pallas_call(
        attend_kernel,
        grid=(seqs, width // block),
        in_specs=[SMEM_SPEC, own(0), own(1), own(2), rim(0), rim(1), rim(0), rim(1)],
        out_specs=[flat, probs],
        out_shape=[jax.ShapeDtypeStruct((rows, width), bf16), probs_shape],
        compiler_params=params(16, "arbitrary", "arbitrary"),
        cost_estimate=cost(8 * rows * width * (BLOCK_Q + 2 * WIN), 10 * rows * width),
        name="attend",
    )(meta, qkv, qkv, qkv, rim_up, rim_up, rim_down, rim_down)


def attend_back_kernel(
    q_ref,
    k_ref,
    v_ref,
    k_up_ref,
    v_up_ref,
    k_down_ref,
    v_down_ref,
    probs_ref,
    go_ref,
    cos_ref,
    sin_ref,
    gq_ref,
    gk_ref,
    gv_ref,
    up_ref,
    down_ref,
    gk_acc,
    gv_acc,
):
    rows, width = q_ref.shape[1:]
    scale = HEAD_DIM**-0.5
    first_head, low_mask, high_mask = head_masks()

    def turned_back(tile, span):
        return tile * cos_ref[span, :] - swapped_halves(tile) * sin_ref[span, :]

    for lane in range(0, width, LANES):
        lanes = slice(lane, lane + LANES)
        keys = jnp.concatenate([k_up_ref[0, :, lanes], k_ref[0, :, lanes], k_down_ref[0, :, lanes]], 0)
        values = jnp.concatenate([v_up_ref[0, :, lanes], v_ref[0, :, lanes], v_down_ref[0, :, lanes]], 0)
        gk_acc[...] = jnp.zeros_like(gk_acc)
        gv_acc[...] = jnp.zeros_like(gv_acc)
        for top in range(0, rows, BLOCK_Q):
            span = slice(top, top + BLOCK_Q + 2 * WIN)
            queries = two_heads(q_ref[0, top : top + BLOCK_Q, lanes], low_mask, high_mask)
            grads = two_heads(go_ref[top : top + BLOCK_Q, lanes], low_mask, high_mask)
            probs_low = probs_ref[0, lane // LANES, top // BLOCK_Q]
            probs = probs_low.astype(f32)
            grad_probs = dot_nt(grads, values[span])
            delta = jnp.sum(probs * grad_probs, axis=-1, keepdims=True)
            grad_scores = (probs * (grad_probs - delta)).astype(bf16)
            result = dot_nn(grad_scores, keys[span])
            result = jnp.where(first_head, result[:BLOCK_Q], result[BLOCK_Q:]) * scale
            own = slice(WIN + top, WIN + top + BLOCK_Q)
            gq_ref[top : top + BLOCK_Q, lanes] = turned_back(result, own).astype(bf16)
            gk_acc[span, :] += tokens_dot(grad_scores, queries)
            gv_acc[span, :] += tokens_dot(probs_low, grads)
        grad_keys = turned_back(gk_acc[...] * scale, slice(None))
        grad_values = gv_acc[...]
        up_ref[0, :, lanes] = grad_keys[:WIN].astype(bf16)
        up_ref[1, :, lanes] = grad_values[:WIN].astype(bf16)
        down_ref[0, :, lanes] = grad_keys[WIN + rows :].astype(bf16)
        down_ref[1, :, lanes] = grad_values[WIN + rows :].astype(bf16)
        gk_ref[:, lanes] = grad_keys[WIN : WIN + rows]
        gv_ref[:, lanes] = grad_values[WIN : WIN + rows]


def attend_back_call(qkv, rim_up, rim_down, saved, grad_out, cosine, sine, seqs):
    _, rows, width = qkv.shape
    seq_rows = rows // seqs
    block = 256
    own, rim, flat, probs, probs_shape = attention_specs(seqs, seq_rows, width, block)
    table = pl.BlockSpec(cosine.shape, lambda s, h: (0, 0))
    edge = pl.BlockSpec((2, WIN, block), lambda s, h: (0, s, h))
    edge_shape = jax.ShapeDtypeStruct((2, seqs * WIN, width), bf16)
    return pl.pallas_call(
        attend_back_kernel,
        grid=(seqs, width // block),
        in_specs=[
            own(0), own(1), own(2), rim(0), rim(1), rim(0), rim(1),
            probs, flat, table, table,
        ],
        out_specs=[flat, flat, flat, edge, edge],
        out_shape=[
            jax.ShapeDtypeStruct((rows, width), bf16),
            jax.ShapeDtypeStruct((rows, width), f32),
            jax.ShapeDtypeStruct((rows, width), f32),
            edge_shape,
            edge_shape,
        ],
        scratch_shapes=[
            pltpu.VMEM((seq_rows + 2 * WIN, LANES), f32),
            pltpu.VMEM((seq_rows + 2 * WIN, LANES), f32),
        ],
        compiler_params=params(16, "arbitrary", "arbitrary"),
        cost_estimate=cost(20 * rows * width * (BLOCK_Q + 2 * WIN), 20 * rows * width),
        name="attend_back",
    )(qkv, qkv, qkv, rim_up, rim_up, rim_down, rim_down, *far(saved), grad_out, cosine, sine)


def out_kernel(
    meta_ref, o_ref, own_ref, p0, p1, p2, p3, q0, q1, q2, q3, x_ref, valid_ref, gains_ref,
    middle_ref, n_split_ref, o_split_ref, whole_ref, *, size,
):
    @pl.when(pl.program_id(0) == 0)
    def _():
        assemble_two(meta_ref, whole_ref, own_ref, (p0, p1, p2, p3), (q0, q1, q2, q3))

    values = o_ref[...]
    split_columns(values, o_split_ref, slice(None), size)
    middle = x_ref[...].astype(f32) + valid_ref[...] * dot_nn(values, whole_ref[...])
    middle_ref[...] = middle
    scaled, _inverse = normalized(middle)
    split_columns((scaled * gains_ref[1:2, :]).astype(bf16), n_split_ref, slice(None), size)


def out_call(meta, attended, own, parts, start, stretch, x, valid, gains):
    rows, width = x.shape
    slab = own.shape[0]
    size = width // slab
    block = 128
    tile = pl.BlockSpec((block, width), lambda i: (i, 0))
    split = pl.BlockSpec((2, block, width // 2), lambda i: (0, i, 0))
    split_shape = jax.ShapeDtypeStruct((2, rows, width // 2), bf16)
    return pl.pallas_call(
        functools.partial(out_kernel, size=size),
        grid=(rows // block,),
        in_specs=[SMEM_SPEC, tile, once(slab, width)]
        + stretch_specs(parts, start, stretch)
        + [tile, pl.BlockSpec((block, 1), lambda i: (i, 0)), once(8, width)],
        out_specs=[tile, split, split],
        out_shape=[pltpu.HBM((rows, width), f32), split_shape, split_shape],
        scratch_shapes=[pltpu.VMEM((width, width), bf16)],
        compiler_params=params(16, "arbitrary"),
        cost_estimate=cost(2 * rows * width * width, 2 * width * width + 12 * rows * width),
        name="out_norm",
    )(meta, attended, *far(own, *parts, *parts, x), valid, gains)


def gate_kernel(
    meta_ref, n_ref, own1_ref, p0, p1, p2, p3, own2_ref, q0, q1, q2, q3,
    mixed_ref, slope_ref, act_ref, normed_ref, first_ref, second_ref, *, size,
):
    @pl.when(pl.program_id(0) == 0)
    def _():
        for top in range(0, normed_ref.shape[0], 128):
            rows = slice(top, top + 128)
            normed_ref[rows, :] = joined_columns(n_ref, rows, size)

    assemble(meta_ref, first_ref, own1_ref, (p0, p1, p2, p3))
    assemble(meta_ref, second_ref, own2_ref, (q0, q1, q2, q3))
    gate_in = dot_nn(normed_ref[...], first_ref[...])
    gate_up = dot_nn(normed_ref[...], second_ref[...])
    normal_cdf = 0.5 * (1.0 + lax.erf(gate_in * root_half))
    density = jnp.exp(-0.5 * gate_in * gate_in) * inv_root_two_pi
    activated = gate_in * normal_cdf
    mixed_ref[...] = (activated * gate_up).astype(bf16)
    slope_ref[...] = (gate_up * (normal_cdf + gate_in * density)).astype(bf16)
    act_ref[...] = activated.astype(bf16)


def gate_call(meta, normed, owns, parts, block):
    _, rows, half = normed.shape
    width = 2 * half
    slab, hidden = owns[0].shape
    steps = hidden // block
    size = width // slab
    tile = pl.BlockSpec((rows, block), lambda i: (0, i))
    own = pl.BlockSpec((slab, block), lambda i: (0, i))
    return pl.pallas_call(
        functools.partial(gate_kernel, size=size),
        grid=(hidden // block,),
        in_specs=[SMEM_SPEC, once(2, rows, half), own]
        + part_specs(parts, block, lambda i: i)
        + [own]
        + part_specs(parts, block, lambda i: i + steps),
        out_specs=[tile, tile, tile],
        out_shape=[pltpu.HBM((rows, hidden), bf16)] * 3,
        scratch_shapes=[
            pltpu.VMEM((rows, width), bf16),
            pltpu.VMEM((width, block), bf16),
            pltpu.VMEM((width, block), bf16),
        ],
        compiler_params=params(32, "arbitrary"),
        cost_estimate=cost(4 * rows * width * hidden, 4 * width * hidden + 6 * rows * hidden),
        name="gate",
    )(meta, normed, *far(owns[0], *parts, owns[1], *parts))


def gate_back_kernel(
    meta_ref, g_ref, own_ref, p0, p1, p2, p3, slope_ref, act_ref, out_ref, whole_ref, *, block
):
    step = pl.program_id(0)

    @pl.when(step == 0)
    def _():
        rows = own_ref.shape[0]
        count, links, cut, columns = p0.shape
        size = count + 1
        me, core = meta_ref[1], meta_ref[2]
        whole_ref[size * rows :, :] = jnp.zeros_like(whole_ref[size * rows :, :])
        whole_ref[pl.ds(pl.multiple_of(me * rows, 16), rows), :] = own_ref[...]

        def put(halves):
            for steps in range(1, size):
                base = lax.rem(me - steps + size, size) * rows
                for half, parts in enumerate(halves):
                    for part, start in zip(parts, (0, cut)):
                        target = pl.ds(pl.multiple_of(base + start, 16), part.shape[2])
                        for link in range(links):
                            lane = (half * links + link) * columns
                            whole_ref[target, lane : lane + columns] = part[steps - 1, link]

        @pl.when(core == 0)
        def _():
            put(((p0, p1), (p2, p3)))

        @pl.when(core == 1)
        def _():
            put(((p2, p3), (p0, p1)))

    weight = whole_ref[pl.ds(pl.multiple_of(step * block, block), block), :]
    grad_mixed = dot_nt(g_ref[...], weight)
    out_ref[0] = (grad_mixed * slope_ref[...].astype(f32)).astype(bf16)
    out_ref[1] = (grad_mixed * act_ref[...].astype(f32)).astype(bf16)


def gate_back_plain_kernel(g_ref, w_ref, slope_ref, act_ref, out_ref):
    grad_mixed = dot_nt(g_ref[...], w_ref[...])
    out_ref[0] = (grad_mixed * slope_ref[...].astype(f32)).astype(bf16)
    out_ref[1] = (grad_mixed * act_ref[...].astype(f32)).astype(bf16)


def gate_back_call(meta, grad_result, own, parts, slope, act, block):
    rows, width = grad_result.shape
    hidden = slope.shape[1]
    tile = pl.BlockSpec((rows, block), lambda i: (0, i))
    out_spec = pl.BlockSpec((2, rows, block), lambda i: (0, 0, i))
    out_shape = jax.ShapeDtypeStruct((2, rows, hidden), bf16)
    settings = dict(
        grid=(hidden // block,),
        compiler_params=params(28, "arbitrary"),
        cost_estimate=cost(2 * rows * width * hidden, 4 * width * hidden + 8 * rows * hidden),
        name="gate_back",
    )
    if own.shape[0] % 16:
        whole = whole_columns(own, parts, hidden - own.shape[0] * (parts[0].shape[0] + 1))
        out = pl.pallas_call(
            gate_back_plain_kernel,
            in_specs=[once(rows, width), pl.BlockSpec((block, width), lambda i: (i, 0)), tile, tile],
            out_specs=out_spec,
            out_shape=out_shape,
            **settings,
        )(grad_result, whole, slope, act)
        return out, whole
    return pl.pallas_call(
        functools.partial(gate_back_kernel, block=block),
        in_specs=[SMEM_SPEC, once(rows, width), once(*own.shape)]
        + [once(*part.shape) for part in parts]
        + [tile, tile],
        out_specs=[out_spec, fixed(hidden, width)],
        out_shape=[out_shape, jax.ShapeDtypeStruct((hidden, width), bf16)],
        **settings,
    )(meta, *far(grad_result, own, *parts, slope, act))


def down_kernel(
    meta_ref, m_ref, n_ref, g_ref, h_ref, keep0, give0, keep1, give1, state_ref, *, hidden, places
):
    step = pl.program_id(0)
    block, half = m_ref.shape[1], h_ref.shape[1]
    size, links, rows, columns = state_ref.shape
    right = g_ref[:, pl.ds(pl.multiple_of(meta_ref[2] * half, half), half)]
    sums = tokens_dot(m_ref[...], right) + tokens_dot(n_ref[...], h_ref[...])

    def put(first):
        for place in range(size):
            top, end = max(place * rows, first), min((place + 1) * rows, first + block)
            if top >= end:
                continue
            for link in range(links):
                value = sums[top - first : end - first, link * columns : (link + 1) * columns]
                state_ref[place, link, top - place * rows : end - place * rows, :] = value.astype(bf16)

    for number in range(-(-hidden // block)):
        pl.when(step == number)(functools.partial(put, number * block))

    @pl.when(step == pl.num_programs(0) - 1)
    def _():
        height, width = keep0.shape[2:]
        tiles = rows // height
        for part, (keep_ref, give_ref) in enumerate(((keep0, give0), (keep1, give1))):
            own = meta_ref[3 + part]
            span = range(part * (width // columns), min((part + 1) * (width // columns), tiles))
            for place in range(size):
                for number in range(links // 2):
                    base = split_index(number, places[part])
                    for ref, value in ((keep_ref, own), (give_ref, 1 - own)):
                        link = base + value * (1 << places[part])
                        for lane, tile in enumerate(span):
                            ref[place, number, :, lane * columns : (lane + 1) * columns] = state_ref[
                                place, link, tile * height : (tile + 1) * height, :
                            ]
                        if len(span) * columns < width:
                            ref[place, number, :, len(span) * columns :] = jnp.zeros(
                                (height, width - len(span) * columns), bf16
                            )


def first_places():
    return [left.index(bit) for left, bit in zip(bits_left(0), link_orders()[0])]


def piece_rows(width):
    return width // lax.axis_size("fsdp") // (4 << link_count())


def fits(shard, columns, height):
    return shard % 16 == 0 and columns == LANES and height == 16


def down_call(meta, mixed, mixed_other, grad_result, grad_other, hidden, block):
    rows, hidden_pad = mixed.shape
    width = grad_result.shape[1]
    size = lax.axis_size("fsdp")
    links = 1 << link_count()
    shard, columns, height = hidden // size, width // 2 // links, piece_rows(width)
    if not fits(shard, columns, height):
        own = lax.dynamic_slice_in_dim(grad_result, bit_value(0) * (width // 2), width // 2, 1)
        sums = tokens_dot(mixed, own) + tokens_dot(mixed_other, grad_other)
        state = sums[:hidden].astype(bf16).reshape(size, shard, links, columns)
        state = jnp.moveaxis(state, 2, 1).reshape(size, links, 2, height, -1)
        return [halves(state[:, :, part], 0, part) for part in range(2)]
    tiles = -(-shard // height // 2)
    shape = (size, links // 2, height, tiles * columns)
    out = pl.pallas_call(
        functools.partial(down_kernel, hidden=hidden, places=first_places()),
        grid=(hidden_pad // block,),
        in_specs=[SMEM_SPEC]
        + [pl.BlockSpec((rows, block), lambda i: (0, i))] * 2
        + [once(rows, width), once(rows, width // 2)],
        out_specs=[fixed(*shape)] * 4,
        out_shape=[pltpu.HBM(shape, bf16)] * 4,
        scratch_shapes=[pltpu.VMEM((size, links, shard, columns), bf16)],
        compiler_params=params(24, "arbitrary"),
        cost_estimate=cost(2 * rows * width * hidden, width * hidden + 4 * rows * (hidden + width)),
        name="down_sum",
    )(meta, *far(mixed, mixed_other, grad_result, grad_other))
    return [(out[0], out[1]), (out[2], out[3])]


def sum_kernel(meta_ref, left_ref, left_other_ref, right_ref, right_other_ref, *rest, size, links, places, steps):
    state_ref = rest[-1]
    state_ref[...] = (
        tokens_dot(left_ref[meta_ref[2]], right_ref[0]) + tokens_dot(left_other_ref[...], right_other_ref[0])
    ).astype(bf16)
    rows = state_ref.shape[0] // (2 * size * links)

    def put(outs):
        for part in range(2):
            own = meta_ref[3 + part]
            for place in range(size):
                for number in range(links // 2):
                    base = (2 * place + part) * links + split_index(number, places[part])
                    for ref, value in ((outs[2 * part], own), (outs[2 * part + 1], 1 - own)):
                        start = (base + value * (1 << places[part])) * rows
                        ref[place, number] = state_ref[pl.ds(pl.multiple_of(start, rows), rows), :]

    planes = (len(rest) - 1) // 4
    for plane in range(planes):
        pl.when(pl.program_id(0) // steps == plane)(functools.partial(put, rest[4 * plane : 4 * plane + 4]))


def sum_call(meta, left, left_other, right, right_other, block):
    _, tokens, height = left.shape
    planes, _, width = right.shape
    size = lax.axis_size("fsdp")
    links = 1 << link_count()
    rows = height // (2 * size * links)
    steps = width // block
    if rows % 16:
        result = []
        for plane in range(planes):
            state = tokens_dot(half_of(left, True), right[plane]) + tokens_dot(left_other, right_other[plane])
            state = state.astype(bf16).reshape(size, 2, links, rows, width)
            result.append([halves(state[:, part], 0, part) for part in range(2)])
        return result
    shape = (size, links // 2, rows, width)
    right_spec = pl.BlockSpec((1, tokens, block), lambda i: (i // steps, 0, i % steps))

    def out_spec(plane):
        return pl.BlockSpec(
            shape[:3] + (block,), lambda i: (0, 0, 0, jnp.clip(i - plane * steps, 0, steps - 1))
        )

    out = pl.pallas_call(
        functools.partial(sum_kernel, size=size, links=links, places=first_places(), steps=steps),
        grid=(planes * steps,),
        in_specs=[SMEM_SPEC, once(2, tokens, height), once(tokens, height), right_spec, right_spec],
        out_specs=[out_spec(plane) for plane in range(planes) for _ in range(4)],
        out_shape=[pltpu.HBM(shape, bf16)] * (4 * planes),
        scratch_shapes=[pltpu.VMEM((height, block), bf16)],
        compiler_params=params(22, "arbitrary"),
        cost_estimate=cost(4 * tokens * height * width * planes, 4 * planes * (height + tokens) * width),
        name="sum_rows",
    )(meta, left, left_other, right, right_other)
    return [[(out[k], out[k + 1]), (out[k + 2], out[k + 3])] for k in range(0, 4 * planes, 4)]


def fold_kernel(meta_ref, *refs, count, done, places):
    ins, outs = refs[: 4 * count], refs[4 * count :]
    for part in range(2):
        own = meta_ref[3 + 2 * done + part]
        start = 0
        for number in range(count):
            keep_ref, got_ref = ins[4 * number + 2 * part], ins[4 * number + 2 * part + 1]
            size, links, _, width = keep_ref.shape
            for place in range(size):
                for index in range(links // 2):
                    base = split_index(index, places[part])
                    for ref, value in ((outs[2 * part], own), (outs[2 * part + 1], 1 - own)):
                        link = base + value * (1 << places[part])
                        ref[place, index, :, start : start + width] = added(
                            keep_ref[place, link], got_ref[place, link]
                        )
            start += width


def fold_next(meta, blocks, done):
    size = blocks[0][0][0].shape[0]
    places = [left.index(bit) for left, bit in zip(bits_left(done), link_orders()[done])]
    flat = [array for block in blocks for pair in block for array in pair]
    shapes = []
    for part in range(2):
        _, links, rows, _ = blocks[0][part][0].shape
        width = sum(block[part][0].shape[3] for block in blocks)
        shapes += [(size, links // 2, rows, width)] * 2
    if any(shape[2] % 16 for shape in shapes):
        result = []
        for part in range(2):
            state = jnp.concatenate([added(*block[part]) for block in blocks], axis=3)
            result.append(halves(state, done, part))
        return result
    out = pl.pallas_call(
        functools.partial(fold_kernel, count=len(blocks), done=done, places=places),
        grid=(1,),
        in_specs=[SMEM_SPEC] + [once(*array.shape) for array in flat],
        out_specs=[fixed(*shape) for shape in shapes],
        out_shape=[pltpu.HBM(shape, bf16) for shape in shapes],
        compiler_params=params(16, "arbitrary"),
        cost_estimate=cost(0, 3 * sum(array.size for array in flat)),
        name="fold",
    )(meta, *far(*flat))
    return [(out[0], out[1]), (out[2], out[3])]


def finish_kernel(meta_ref, m0, m1, g0, g1, w_ref, out_ref, norm_ref, *down_refs, padded, links):
    step = pl.program_id(0)
    mine = (step < 2) == (meta_ref[2] == 0)
    first = step % 2 == 0
    own = jnp.where(first, m0[...].astype(f32), m1[...].astype(f32))
    got = jnp.where(first, g0[...].astype(f32), g1[...].astype(f32))
    value = jnp.where(mine, own, got)
    hidden = out_ref.shape[1] // 2
    out_ref[:, :hidden] = value[:, :hidden]
    out_ref[:, hidden:] = value[:, padded : padded + hidden]
    sums = jnp.sum(out_ref[...] * w_ref[...].astype(f32), axis=1, keepdims=True)
    norm_ref[0] = jnp.broadcast_to(sums, (sums.shape[0], LANES)).T[:1]
    if down_refs:
        (down_ref,) = down_refs
        height = value.shape[0] // links
        tiles = (value.shape[1] - 2 * padded) // LANES

        def put(core, part):
            for link in range(links):
                for tile in range(tiles):
                    top = (part * tiles + tile) * height
                    if top < down_ref.shape[0]:
                        lane = (core * links + link) * LANES
                        start = 2 * padded + tile * LANES
                        down_ref[top : top + height, lane : lane + LANES] = value[
                            link * height : (link + 1) * height, start : start + LANES
                        ]

        for number in range(4):
            pl.when(step == number)(functools.partial(put, number // 2, number % 2))


def finish_call(meta, parts, w_in, padded, shard, model):
    rows, columns = w_in.shape
    quarter, width = parts[0].shape
    links = 1 << link_count()
    height = quarter // links
    fast = fits(shard, model // 2 // links, height)
    out = pl.pallas_call(
        functools.partial(finish_kernel, padded=padded, links=links),
        grid=(4,),
        in_specs=[SMEM_SPEC]
        + [once(quarter, width)] * 4
        + [pl.BlockSpec((quarter, columns), lambda i: (i, 0))],
        out_specs=[
            pl.BlockSpec((quarter, columns), lambda i: (i, 0)),
            pl.BlockSpec((1, 1, quarter), lambda i: (i, 0, 0)),
        ]
        + [fixed(shard, model)] * fast,
        out_shape=[jax.ShapeDtypeStruct((rows, columns), f32), jax.ShapeDtypeStruct((4, 1, quarter), f32)]
        + [jax.ShapeDtypeStruct((shard, model), f32)] * fast,
        compiler_params=params(30, "arbitrary"),
        cost_estimate=cost(4 * rows * columns, 10 * rows * columns),
        name="finish",
    )(meta, *far(*parts, w_in))
    if fast:
        return out
    mine, got = [
        jnp.stack([part[:, 2 * padded :] for part in pair]).reshape(1, 2, links, height, -1)
        for pair in (parts[:2], parts[2:])
    ]
    whole = jnp.moveaxis(in_order(mine, got, 0, 0), 2, 1).reshape(2 * links, shard, -1)
    return out[0], out[1], jnp.transpose(whole, (1, 0, 2)).reshape(shard, model).astype(f32)


def last_kernel(*refs):
    k0, g0, k1, g1, out_ref = refs
    cut = k0.shape[2]
    for place in range(k0.shape[0]):
        out_ref[place, :cut, :] = added(k0[place, 0], g0[place, 0])
        out_ref[place, cut:, :] = added(k1[place, 0], g1[place, 0])


def fold_last(parts):
    (k0, g0), (k1, g1) = parts
    size, _, cut, width = k0.shape
    rows = cut + k1.shape[2]
    if cut % 16 or k1.shape[2] % 16:
        return jnp.concatenate([added(k0, g0)[:, 0], added(k1, g1)[:, 0]], axis=1)
    return pl.pallas_call(
        last_kernel,
        grid=(1,),
        in_specs=[once(*array.shape) for array in (k0, g0, k1, g1)],
        out_specs=fixed(size, rows, width),
        out_shape=jax.ShapeDtypeStruct((size, rows, width), bf16),
        compiler_params=params(16, "arbitrary"),
        cost_estimate=cost(0, 6 * size * rows * width),
        name="fold_last",
    )(*far(k0, g0, k1, g1))


def middle_back_kernel(
    meta_ref, gu_ref, own1_ref, p0, p1, p2, p3, own2_ref, q0, q1, q2, q3, out_own_ref, r0, r1, r2, r3,
    s0, s1, s2, s3, middle_ref, upstream_ref, valid_ref, gains_ref, grad_ref, branch_ref, att_ref,
    acc, first_ref, second_ref, out_ref,
):
    step = pl.program_id(0)
    assemble(meta_ref, first_ref, own1_ref, (p0, p1, p2, p3))
    assemble(meta_ref, second_ref, own2_ref, (q0, q1, q2, q3))
    total = dot_nt(gu_ref[0], first_ref[...]) + dot_nt(gu_ref[1], second_ref[...])

    @pl.when(step == 0)
    def _():
        acc[...] = total
        assemble_two(meta_ref, out_ref, out_own_ref, (r0, r1, r2, r3), (s0, s1, s2, s3))

    @pl.when(step > 0)
    def _():
        acc[...] += total

    @pl.when(step == pl.num_programs(0) - 1)
    def _():
        for top in range(0, acc.shape[0], 128):
            rows = slice(top, top + 128)
            scaled, inverse = normalized(middle_ref[rows, :])
            grad = upstream_ref[rows, :].astype(f32) + norm_back(
                acc[rows, :], gains_ref[1:2, :], scaled, inverse
            )
            grad_ref[rows, :] = grad
            branch = (grad * valid_ref[rows, :]).astype(bf16)
            branch_ref[rows, :] = branch
            att_ref[rows, :] = dot_nt(branch, out_ref[...]).astype(bf16)


def middle_back_call(
    meta, grad_hidden, owns, parts, out_own, middle, upstream, valid, gains, block
):
    rows, width = middle.shape
    slab = owns[0].shape[0]
    hidden = grad_hidden.shape[2]
    steps = hidden // block
    whole = fixed(rows, width)
    own = pl.BlockSpec((slab, block), lambda i: (0, i))
    flat_low = jax.ShapeDtypeStruct((rows, width), bf16)
    return pl.pallas_call(
        middle_back_kernel,
        grid=(hidden // block,),
        in_specs=[SMEM_SPEC, pl.BlockSpec((2, rows, block), lambda i: (0, 0, i)), own]
        + part_specs(parts, block, lambda i: i)
        + [own]
        + part_specs(parts, block, lambda i: i + steps)
        + [once(slab, width)]
        + stretch_specs(parts, 2 * hidden, block)
        + [whole, whole, once(rows, 1), once(8, width)],
        out_specs=[whole, whole, whole],
        out_shape=[jax.ShapeDtypeStruct((rows, width), f32), flat_low, flat_low],
        scratch_shapes=[
            pltpu.VMEM((rows, width), f32),
            pltpu.VMEM((width, block), bf16),
            pltpu.VMEM((width, block), bf16),
            pltpu.VMEM((width, width), bf16),
        ],
        compiler_params=params(38, "arbitrary"),
        cost_estimate=cost(4 * rows * width * hidden, 4 * width * hidden + 4 * rows * hidden + 12 * rows * width),
        name="middle_back",
    )(meta, grad_hidden, *far(owns[0], *parts, owns[1], *parts, out_own, *parts, *parts, middle, upstream), valid, gains)


def input_back_kernel(
    meta_ref, gqkv_ref, own_ref, p0, p1, p2, p3, x_ref, grad_ref, gains_ref, out_ref, acc, whole_ref
):
    step = pl.program_id(0)
    assemble(meta_ref, whole_ref, own_ref, (p0, p1, p2, p3))
    total = dot_nt(gqkv_ref[...], whole_ref[...])

    @pl.when(step == 0)
    def _():
        acc[...] = total

    @pl.when(step > 0)
    def _():
        acc[...] += total

    @pl.when(step == pl.num_programs(0) - 1)
    def _():
        for top in range(0, acc.shape[0], 128):
            rows = slice(top, top + 128)
            scaled, inverse = normalized(x_ref[rows, :].astype(f32))
            out_ref[rows, :] = (
                grad_ref[rows, :] + norm_back(acc[rows, :], gains_ref[0:1, :], scaled, inverse)
            ).astype(bf16)


def input_back_call(meta, grad_joint, own, parts, x, grad_middle, gains):
    rows, width = x.shape
    slab = own.shape[0]
    block = width
    whole = fixed(rows, width)
    return pl.pallas_call(
        input_back_kernel,
        grid=(3 * width // block,),
        in_specs=[
            SMEM_SPEC,
            pl.BlockSpec((rows, block), lambda i: (0, i)),
            pl.BlockSpec((slab, block), lambda i: (0, i)),
        ]
        + part_specs(parts, block, lambda i: i)
        + [whole, whole, once(8, width)],
        out_specs=whole,
        out_shape=jax.ShapeDtypeStruct((rows, width), bf16),
        scratch_shapes=[pltpu.VMEM((rows, width), f32), pltpu.VMEM((width, block), bf16)],
        compiler_params=params(24, "arbitrary"),
        cost_estimate=cost(6 * rows * width * width, 6 * width * width + 14 * rows * width),
        name="input_back",
    )(meta, grad_joint, *far(own, *parts, x, grad_middle), gains)


def rope_tables(positions):
    halfway = HEAD_DIM // 2
    frequency = 10000.0 ** (-(2.0 * jnp.arange(halfway, dtype=f32)) / HEAD_DIM)
    angles = positions.astype(f32)[:, None] * frequency[None, :]
    cosine, sine = jnp.cos(angles), jnp.sin(angles)
    return (
        jnp.concatenate([cosine] * (LANES // halfway), axis=1),
        jnp.concatenate([-sine, sine] * (LANES // HEAD_DIM), axis=1),
    )


def on_device(inputs, cotangent, lengths, norm_first, w_qkv, w_out, norm_second, w_in, w_down):
    seqs, shard_rows, width = inputs.shape
    rows = seqs * shard_rows
    size = lax.axis_size("fsdp")
    me = lax.axis_index("fsdp")
    hidden = w_in.shape[1] // 2
    block = 896
    hidden_pad = -(-hidden // block) * block
    pad = hidden_pad - hidden
    steps = link_orders()
    near, far, middle_way = runs()

    gains = jnp.pad(jnp.stack([norm_first, norm_second], axis=1), ((0, 0), (0, LANES - 2)))
    came_one = turned_before(row_piece([w_qkv, gains]), range(1, size))
    own_in = [jnp.pad(w_in[:, half * hidden :][:, :hidden], ((0, 0), (0, pad))) for half in range(2)]
    piece_two = row_piece([own_in[0], own_in[1], w_out])
    piece_three = column_piece(w_down)
    first_row = me * shard_rows
    query_pos = first_row + jnp.arange(shard_rows, dtype=jnp.int32)
    rim_pos = first_row - WIN + jnp.arange(shard_rows + 2 * WIN, dtype=jnp.int32)
    cosine, sine = rope_tables(rim_pos)
    valid = (query_pos[None, :] < lengths[:, None]).astype(f32).reshape(rows, 1)
    bits = [bit_value(bit) for pair in steps for bit in pair]
    meta = jnp.stack([first_row, me, bit_value(0)] + bits).astype(jnp.int32)
    meta_rows = jnp.concatenate([first_row.astype(jnp.int32)[None], lengths.astype(jnp.int32)])
    x = inputs.reshape(rows, width)
    upstream = cotangent.reshape(rows, width)
    grad_result = (upstream.astype(f32) * valid).astype(bf16)
    grad_give = lax.dynamic_slice_in_dim(grad_result, (1 - bit_value(0)) * (width // 2), width // 2, 1)
    grad_other = flip(grad_give, 0)
    own_rows = slice(WIN, WIN + shard_rows)
    own_cosine, own_sine = cosine[own_rows], sine[own_rows]
    (
        came_one, piece_two, piece_three, own_in, gains, cosine, sine, own_cosine, own_sine, grad_result, grad_other,
        valid,
    ) = after(
        (
            came_one, piece_two, piece_three, own_in, gains, cosine, sine, own_cosine, own_sine, grad_result,
            grad_other, valid,
        )
    )

    one = widen(row_states(came_one), steps[0], 1)
    came_two = turned_before(piece_two, near)
    one, came_two, piece_two = after((one, came_two, piece_two))

    for bits in steps[1:]:
        one = widen(one, bits, 1)
    came_two = came_two + turned_before(piece_two, far)
    one, came_two, piece_two = after((one, came_two, piece_two))

    parts_one = row_parts(one)
    came_two = came_two + turned_before(piece_two, middle_way)
    normed_first, qkv, gains_all = qkv_call(meta, x, w_qkv, parts_one, gains, own_cosine, own_sine)
    by_seq = qkv.reshape(3, seqs, shard_rows, width)[1:]
    edge = (2, seqs * WIN, width)
    edge_up, edge_down = by_seq[:, :, :WIN].reshape(edge), by_seq[:, :, shard_rows - WIN :].reshape(edge)
    qkv, edge_up, edge_down, came_two, piece_three = after((qkv, edge_up, edge_down, came_two, piece_three))

    rim_down, rim_up = neighbours(edge_up, edge_down)
    two = widen(in_turn(row_states, came_two), steps[0], 1)
    rim_down, rim_up, two, piece_three = after((rim_down, rim_up, two, piece_three))

    for bits in steps[1:]:
        two = widen(two, bits, 1)
    came_three = turned_before(piece_three, range(1, size))
    attended, saved = attend_call(meta_rows, qkv, rim_up, rim_down, seqs)
    two, came_three, attended, normed_first = after((two, came_three, attended, normed_first))

    parts_two = row_parts(two)
    three = widen(column_states(came_three), steps[0], 1)
    first_other = flip(half_of(normed_first, False), 0)
    parts_two, three, attended, first_other = after((parts_two, three, attended, first_other))

    for bits in steps[1:]:
        three = widen(three, bits, 1)
    middle, normed_second, attended_split = out_call(
        meta, attended, w_out, parts_two, 2 * hidden_pad, block, x, valid, gains_all
    )
    second_other = flip(half_of(normed_second, False), 0)
    attended_other = flip(half_of(attended_split, False), 0)
    mixed, slope, act = gate_call(meta, normed_second, own_in, parts_two, block)
    three, mixed, slope, act, second_other, attended_other = after(
        (three, mixed, slope, act, second_other, attended_other)
    )

    parts_three = column_parts(three)
    parts_three, mixed, slope, act = after((parts_three, mixed, slope, act))

    mixed_other = flip(mixed, 0)
    grad_hidden, whole_down = gate_back_call(meta, grad_result, w_down, parts_three, slope, act, block)
    grad_hidden, mixed, mixed_other = after((grad_hidden, mixed, mixed_other))

    hidden_other = flip(grad_hidden, 0)
    down = down_call(meta, mixed, mixed_other, grad_result, grad_other, hidden, block)
    result = jnp.dot(mixed, whole_down, preferred_element_type=f32)
    output = (middle + valid * result).astype(bf16)
    down, hidden_other, grad_hidden, output = after((down, hidden_other, grad_hidden, output))

    down = swap(down, 0)
    one, two = sum_call(meta, normed_second, second_other, grad_hidden, hidden_other, block)
    down, one, two, grad_hidden = after((down, one, two, grad_hidden))

    one = swap(one, 0)
    for done in range(1, len(steps)):
        down = swap(fold_next(meta, [down], done), done)
    grad_middle, grad_branch, grad_att = middle_back_call(
        meta, grad_hidden, own_in, parts_two, w_out, middle, upstream, valid, gains_all, block
    )
    one, two, grad_branch, grad_att, down = after((one, two, grad_branch, grad_att, down))

    two = swap(two, 0)
    for done in range(1, len(steps)):
        one = swap(fold_next(meta, [one], done), done)
    down_slots = fold_last(down)
    down_came = turned_slots(down_slots, near)
    grad_q, grad_k, grad_v, edge_up, edge_down = attend_back_call(
        qkv, rim_up, rim_down, saved, grad_att, cosine, sine, seqs
    )
    one, two, edge_up, edge_down, grad_q, grad_branch, down_slots, down_came = after(
        (one, two, edge_up, edge_down, grad_q, grad_branch, down_slots, down_came)
    )

    def spread_start(owned):
        ones = (1,) * link_count()
        cut = owned.shape[0] // 2
        return [part.reshape(ones + part.shape) for part in (owned[:cut], owned[cut:])]

    def spread_end(states):
        mine = jnp.stack([state.reshape((-1,) + state.shape[-2:]) for state in states])
        return in_order(mine[None], flip(mine, 0)[None], 0, 0)

    from_next, from_before = neighbours(edge_up, edge_down)
    branch_other = flip(grad_branch, 0)
    two, branch_other = after((two, branch_other))
    for done in range(1, len(steps)):
        two = swap(fold_next(meta, [two], done), done)
    (outs,) = sum_call(meta, attended_split, attended_other, grad_branch[None], branch_other[None], width // 2)
    one_slots = fold_last(one)
    from_next, from_before, two, one_slots, outs = after((from_next, from_before, two, one_slots, outs))

    def with_edges(own, plane):
        own = own.reshape(seqs, shard_rows, width)
        before = from_before[plane].reshape(seqs, WIN, width).astype(f32)
        later = from_next[plane].reshape(seqs, WIN, width).astype(f32)
        rest = ((0, 0), (0, shard_rows - WIN), (0, 0))
        own = own + jnp.pad(before, rest) + jnp.pad(later, (rest[0], rest[1][::-1], rest[2]))
        return own.reshape(rows, width).astype(bf16)

    outs = swap(outs, 0)
    down_came = down_came + turned_slots(down_slots, far) + turned_slots(down_slots, middle_way)
    grad_joint = jnp.concatenate([grad_q, with_edges(grad_k, 0), with_edges(grad_v, 1)], axis=1)
    joint_other = flip(grad_joint, 0)
    (last,) = sum_call(meta, normed_first, first_other, grad_joint[None], joint_other[None], width)
    two_slots = fold_last(two)
    last, grad_joint, outs, one_slots, two_slots, down_came, down_slots = after(
        (last, grad_joint, outs, one_slots, two_slots, down_came, down_slots)
    )

    last = swap(last, 0)
    one_came = turned_slots(one_slots, range(1, size))
    grad_inputs = input_back_call(meta, grad_joint, w_qkv, parts_one, x, grad_middle, gains_all)
    last, grad_inputs, one_came, one_slots, two_slots, down_came, down_slots = after(
        (last, grad_inputs, one_came, one_slots, two_slots, down_came, down_slots)
    )

    last = [last, outs]
    for done in range(1, len(steps)):
        last = [swap(fold_next(meta, last, done), done)]
    two_came = turned_slots(two_slots, range(1, size))
    owned = [slot_sum(one_slots, one_came), slot_sum(down_slots, down_came)]
    last, two_came, two_slots, owned = after((last, two_came, two_slots, owned))

    last_slots = fold_last(last[0])
    last_came = turned_slots(last_slots, near) + turned_slots(last_slots, far)
    spread_in = widen(
        spread_start(jnp.concatenate([owned[0], slot_sum(two_slots, two_came), owned[1]], axis=1)), steps[0], 0
    )
    last_came, spread_in, last_slots = after((last_came, spread_in, last_slots))

    last_came = last_came + turned_slots(last_slots, middle_way)
    for bits in steps[1:]:
        spread_in = widen(spread_in, bits, 0)
    last_came, spread_in, last_slots = after((last_came, spread_in, last_slots))

    spread_last = widen(spread_start(slot_sum(last_slots, last_came)), steps[0], 0)
    in_parts = [state.reshape((-1, state.shape[-1])) for state in spread_in]
    in_parts = in_parts + [flip(part, 0) for part in in_parts]
    spread_last, in_parts = after((spread_last, in_parts))

    for bits in steps[1:]:
        spread_last = widen(spread_last, bits, 0)
    grad_in, grad_second, grad_down = finish_call(meta, in_parts, w_in, hidden_pad, hidden // size, width)
    spread_last, grad_in, grad_second, grad_down = after((spread_last, grad_in, grad_second, grad_down))

    grad_second = grad_second.reshape(-1) / norm_second.astype(f32)
    grad_last = spread_end(spread_last)
    grad_last = grad_last.reshape(-1, grad_last.shape[-1])
    grad_qkv = grad_last[:, : 3 * width].astype(f32)
    grad_out = grad_last[:, 3 * width :].astype(f32)
    grad_first = jnp.sum(grad_qkv * w_qkv.astype(f32), axis=1) / norm_first.astype(f32)
    return (
        output.reshape(inputs.shape),
        grad_inputs.reshape(inputs.shape),
        grad_first,
        grad_qkv,
        grad_out,
        grad_second,
        grad_in,
        grad_down,
    )


def solution(mesh):
    in_specs = (
        P("rep", "fsdp", None),
        P("rep", "fsdp", None),
        P("rep"),
        P("fsdp"),
        P("fsdp", None),
        P("fsdp", None),
        P("fsdp"),
        P("fsdp", None),
        P("fsdp", None),
    )
    out_specs = (
        P("rep", "fsdp", None),
        P("rep", "fsdp", None),
        P("fsdp"),
        P("fsdp", None),
        P("fsdp", None),
        P("fsdp"),
        P("fsdp", None),
        P("fsdp", None),
    )
    return jax.shard_map(
        on_device, mesh=mesh, in_specs=in_specs, out_specs=out_specs, check_vma=False
    )
```

```python
import functools

import jax
import jax.numpy as jnp
from jax import lax
from jax.experimental import pallas as pl
from jax.experimental.pallas import tpu as pltpu
from jax.sharding import PartitionSpec as P

HEAD_DIM = 64
WIN = 64
BLOCK_Q = 128
LANES = 128

epsilon = 1e-05
root_half = 0.7071067811865476
inv_root_two_pi = 0.3989422804014327
f32 = jnp.float32
bf16 = jnp.bfloat16
COST_SCALE = 1.0


def after(value, *before):
    return lax.optimization_barrier((value, before))[0]


def bit_count():
    return lax.axis_size("rep").bit_length() - 1


def bit_value(bit):
    return (lax.axis_index("rep") >> bit) & 1


def link_count():
    return bit_count() - 1


def link_axis(bit):
    return bit_count() - 1 - bit


def flip(value, bit):
    size = lax.axis_size("rep")
    return lax.ppermute(value, "rep", [(i, i ^ (1 << bit)) for i in range(size)])


def turn(value, steps):
    size = lax.axis_size("fsdp")
    return lax.ppermute(value, "fsdp", [(i, (i + steps) % size) for i in range(size)])


def link_orders():
    bits = list(range(1, bit_count()))
    return list(zip(bits, bits[::-1]))


def in_order(mine, got, bit, axis):
    first = bit_value(bit) == 0
    return jnp.concatenate([jnp.where(first, mine, got), jnp.where(first, got, mine)], axis=axis)


def widen(states, bits, lead):
    return [
        in_order(state, flip(state, bit), bit, lead + link_axis(bit)) for state, bit in zip(states, bits)
    ]


def row_piece(shards):
    width = sum(shard.shape[1] for shard in shards)
    links = 1 << link_count()
    core, link = bit_value(0), lax.axis_index("rep") >> 1
    views = [shard.reshape(2, 2, links, -1, shard.shape[1]) for shard in shards]
    rows = views[0].shape[3]
    pieces = [
        lax.dynamic_slice(view, (core, 0, link, 0, 0), (1, 2, 1, rows, view.shape[4])) for view in views
    ]
    return jnp.concatenate(pieces, axis=-1).reshape(2, rows, width)


def row_states(came):
    ones = (1,) * link_count()
    return [
        jnp.stack([piece[part] for piece in came]).reshape((len(came),) + ones + came[0].shape[1:])
        for part in range(2)
    ]


def row_parts(states):
    mine = [state.reshape(state.shape[0], -1, state.shape[-1]) for state in states]
    return mine + [flip(state, 0) for state in mine]


def half_rows(rows):
    return -(-rows // 2 // 16) * 16


def column_piece(shard):
    columns = shard.shape[1] // lax.axis_size("rep")
    place = (bit_value(0) << link_count()) + (lax.axis_index("rep") >> 1)
    return lax.dynamic_slice_in_dim(shard, place * columns, columns, 1)


def column_states(came):
    cut = half_rows(came[0].shape[0])
    ones = (1,) * link_count()
    stacked = jnp.stack(came)
    return [
        part.reshape(part.shape[:1] + ones + part.shape[1:]) for part in (stacked[:, :cut], stacked[:, cut:])
    ]


def column_parts(states):
    mine = [state.reshape((state.shape[0], -1) + state.shape[-2:]) for state in states]
    return mine + [flip(state, 0) for state in mine]


def whole_columns(shard, parts, pad_rows):
    size = lax.axis_size("fsdp")
    me = lax.axis_index("fsdp")
    rows, width = shard.shape
    mine, got = [jnp.concatenate(pair, axis=2) for pair in (parts[:2], parts[2:])]
    joined = in_order(mine, got, 0, 1)
    joined = jnp.transpose(joined, (0, 2, 1, 3)).reshape(size - 1, rows, width)
    whole = jnp.zeros((size * rows + pad_rows, width), shard.dtype)
    whole = lax.dynamic_update_slice(whole, shard, (me * rows, 0))
    for steps in range(1, size):
        source = lax.rem(me - steps + size, size)
        whole = lax.dynamic_update_slice(whole, joined[steps - 1], (source * rows, 0))
    return whole


def turned_before(piece, steps):
    return [turn(piece, step) for step in steps]


def runs():
    size = lax.axis_size("fsdp")
    order = sorted(range(1, size), key=lambda step: (min(step, size - step), step))
    cuts = [(size - 1) * part // 3 for part in range(4)]
    return [order[first:last] for first, last in zip(cuts, cuts[1:])]


def in_turn(states, came):
    order = [step for run in runs() for step in run]
    return states([came[order.index(step)] for step in range(1, lax.axis_size("fsdp"))])


def tokens_dot(left, right):
    return lax.dot_general(left, right, (((0,), (0,)), ((), ())), preferred_element_type=f32)


def half_of(split, mine):
    index = bit_value(0) if mine else 1 - bit_value(0)
    return lax.dynamic_index_in_dim(split, index, 0, False)


def turned_slots(slots, steps):
    size = lax.axis_size("fsdp")
    me = lax.axis_index("fsdp")
    return [
        turn(lax.dynamic_index_in_dim(slots, lax.rem(me + step, size), 0, False), step) for step in steps
    ]


def slot_sum(slots, came):
    total = lax.dynamic_index_in_dim(slots, lax.axis_index("fsdp"), 0, False).astype(f32)
    for part in came:
        total = total + part.astype(f32)
    return total.astype(bf16)


def bits_left(done):
    orders = zip(*link_orders())
    return [sorted(order[done:]) for order in orders]


def split_index(number, place):
    low = number & ((1 << place) - 1)
    return ((number >> place) << (place + 1)) | low


def halves(state, done, part):
    bit = link_orders()[done][part]
    place = bits_left(done)[part].index(bit)
    size, links = state.shape[:2]
    view = state.reshape((size, links >> (place + 1), 2, 1 << place) + state.shape[2:])
    shape = (size, links // 2) + state.shape[2:]
    keep, give = [
        lax.dynamic_index_in_dim(view, index, 2, False).reshape(shape)
        for index in (bit_value(bit), 1 - bit_value(bit))
    ]
    return keep, give


def swap(parts, done):
    return [(keep, flip(give, bit)) for (keep, give), bit in zip(parts, link_orders()[done])]


def added(keep, got):
    return (keep.astype(f32) + got.astype(f32)).astype(bf16)


def neighbours(up, down):
    size = lax.axis_size("fsdp")
    forward = [(i, i + 1) for i in range(size - 1)]
    backward = [(i + 1, i) for i in range(size - 1)]
    return lax.ppermute(up, "fsdp", backward), lax.ppermute(down, "fsdp", forward)


def params(megabytes, *semantics):
    return pltpu.CompilerParams(dimension_semantics=semantics, vmem_limit_bytes=megabytes << 20)


def cost(flops, nbytes):
    return pl.CostEstimate(flops=int(flops * COST_SCALE), bytes_accessed=int(nbytes * COST_SCALE), transcendentals=0)


def far(*arrays):
    return [pltpu.with_memory_space_constraint(array, pltpu.HBM) for array in arrays]


def dot_nn(left, right):
    return jnp.dot(left, right, preferred_element_type=f32)


def dot_nt(left, right):
    return lax.dot_general(left, right, (((1,), (1,)), ((), ())), preferred_element_type=f32)


def normalized(values):
    centred = values - jnp.mean(values, axis=-1, keepdims=True)
    inverse = lax.rsqrt(jnp.mean(centred * centred, axis=-1, keepdims=True) + epsilon)
    return centred * inverse, inverse


def norm_back(grad_out, gain, scaled, inverse):
    grad_scaled = grad_out * gain
    return inverse * (
        grad_scaled
        - jnp.mean(grad_scaled, axis=-1, keepdims=True)
        - scaled * jnp.mean(grad_scaled * scaled, axis=-1, keepdims=True)
    )


def swapped_halves(values):
    width = values.shape[-1]
    lane = lax.broadcasted_iota(jnp.int32, values.shape, values.ndim - 1)
    ahead = pltpu.roll(values, width - HEAD_DIM // 2, values.ndim - 1)
    behind = pltpu.roll(values, HEAD_DIM // 2, values.ndim - 1)
    return jnp.where(lane % HEAD_DIM < HEAD_DIM // 2, ahead, behind)


def assemble(meta_ref, whole_ref, own_ref, part_refs):
    rows = own_ref.shape[0]
    count, quarter = part_refs[0].shape[:2]
    size = count + 1
    me, core = meta_ref[1], meta_ref[2]
    whole_ref[pl.ds(pl.multiple_of(me * rows, quarter), rows), :] = own_ref[...]
    for steps in range(1, size):
        base = lax.rem(me - steps + size, size) * rows
        for number, part_ref in enumerate(part_refs):
            half = core if number < 2 else 1 - core
            start = base + half * (rows // 2) + (number % 2) * quarter
            whole_ref[pl.ds(pl.multiple_of(start, quarter), quarter), :] = part_ref[steps - 1]


def split_columns(values, split_ref, rows, size):
    half = values.shape[1] // size // 2
    for place in range(size):
        for core in range(2):
            start = (2 * place + core) * half
            split_ref[core, rows, place * half : (place + 1) * half] = values[:, start : start + half]


def joined_columns(split_ref, rows, size):
    half = split_ref.shape[2] // size
    return jnp.concatenate(
        [
            split_ref[core, rows, place * half : (place + 1) * half]
            for place in range(size)
            for core in range(2)
        ],
        axis=1,
    )


def assemble_two(meta_ref, whole_ref, own_ref, wide_refs, narrow_refs):
    cut = wide_refs[0].shape[2]
    assemble(meta_ref, whole_ref.at[:, :cut], own_ref.at[:, :cut], wide_refs)
    assemble(meta_ref, whole_ref.at[:, cut:], own_ref.at[:, cut:], narrow_refs)


def stretch_specs(parts, start, block):
    rest = parts[0].shape[2] - start - block
    wide = part_specs(parts, block, lambda i: start // block)
    return wide + part_specs(parts, rest, lambda i: (start + block) // rest)


def part_specs(parts, block, place):
    count, quarter, _ = parts[0].shape
    return [pl.BlockSpec((count, quarter, block), lambda i: (0, 0, place(i)))] * 4


def qkv_kernel(
    meta_ref, x_ref, own_ref, p0, p1, p2, p3, gain_ref, g0, g1, g2, g3, cos_ref, sin_ref,
    split_ref, out_ref, gains_ref, whole_ref, normed_ref, column_ref, *, rope_steps, size,
):
    step = pl.program_id(0)

    @pl.when(step == 0)
    def _():
        assemble(meta_ref, column_ref, gain_ref, (g0, g1, g2, g3))
        row = lax.broadcasted_iota(jnp.int32, gains_ref.shape[:1] + (LANES,), 0)
        lane = lax.broadcasted_iota(jnp.int32, gains_ref.shape[:1] + (LANES,), 1)
        gains_ref[...] = dot_nt((row == lane).astype(f32).astype(bf16), column_ref[...])
        for top in range(0, x_ref.shape[0], 128):
            rows = slice(top, top + 128)
            scaled, _inverse = normalized(x_ref[rows, :].astype(f32))
            normed = (scaled * gains_ref[0:1, :]).astype(bf16)
            normed_ref[rows, :] = normed
            split_columns(normed, split_ref, rows, size)

    assemble(meta_ref, whole_ref, own_ref, (p0, p1, p2, p3))
    product = dot_nn(normed_ref[...], whole_ref[...])

    @pl.when(step >= rope_steps)
    def _():
        out_ref[0] = product.astype(bf16)

    @pl.when(step < rope_steps)
    def _():
        seq_rows = cos_ref.shape[0]
        cosine, sine = cos_ref[...], sin_ref[...]
        for top in range(0, product.shape[0], seq_rows):
            for lane in range(0, product.shape[1], LANES):
                tile = product[top : top + seq_rows, lane : lane + LANES]
                out_ref[0, top : top + seq_rows, lane : lane + LANES] = (
                    tile * cosine + swapped_halves(tile) * sine
                ).astype(bf16)


SMEM_SPEC = pl.BlockSpec(memory_space=pltpu.SMEM)


def fixed(*shape):
    return pl.BlockSpec(shape, lambda i: (0,) * len(shape))


def once(*shape):
    return pl.BlockSpec(shape, lambda i: (0,) * len(shape), pipeline_mode=pl.Buffered(1))


def qkv_call(meta, x, own, parts, own_gains, cosine, sine):
    rows, width = x.shape
    slab = own.shape[0]
    size = width // slab
    block = 512
    per_plane = width // block
    return pl.pallas_call(
        functools.partial(qkv_kernel, rope_steps=2 * per_plane, size=size),
        grid=(3 * per_plane,),
        in_specs=[SMEM_SPEC, once(rows, width), pl.BlockSpec((slab, block), lambda i: (0, i))]
        + part_specs(parts, block, lambda i: i)
        + [once(slab, LANES)]
        + part_specs(parts, LANES, lambda i: 3 * width // LANES)
        + [once(*cosine.shape), once(*sine.shape)],
        out_specs=[
            fixed(2, rows, width // 2),
            pl.BlockSpec((1, rows, block), lambda i: (i // per_plane, 0, i % per_plane)),
            fixed(8, width),
        ],
        out_shape=[
            jax.ShapeDtypeStruct((2, rows, width // 2), bf16),
            jax.ShapeDtypeStruct((3, rows, width), bf16),
            jax.ShapeDtypeStruct((8, width), f32),
        ],
        scratch_shapes=[
            pltpu.VMEM((width, block), bf16),
            pltpu.VMEM((rows, width), bf16),
            pltpu.VMEM((width, LANES), bf16),
        ],
        compiler_params=params(20, "arbitrary"),
        cost_estimate=cost(6 * rows * width * width, 6 * width * width + 10 * rows * width),
        name="qkv",
    )(meta, *far(x, own, *parts), own_gains, *far(*parts), cosine, sine)


def head_masks():
    lane = lax.broadcasted_iota(jnp.int32, (1, LANES), 1)
    first = lane < HEAD_DIM
    return first, first.astype(f32).astype(bf16), (~first).astype(f32).astype(bf16)


def two_heads(tile, low_mask, high_mask):
    return jnp.concatenate([tile * low_mask, tile * high_mask], axis=0)


def score_bias(first_row, length):
    shape = (BLOCK_Q + 2 * WIN, BLOCK_Q)
    key = first_row - WIN + lax.broadcasted_iota(jnp.int32, shape, 0)
    query = first_row + lax.broadcasted_iota(jnp.int32, shape, 1)
    near = jnp.abs(query - key) <= WIN
    live = (key >= 0) & (key < length)
    bias = jnp.where(near & (live | (query == key)), 0.0, -1e30).astype(f32)
    return jnp.concatenate([bias, bias], axis=1)


def softmax_of(queries, keys, bias):
    scores = dot_nt(keys, queries) * (HEAD_DIM**-0.5) + bias
    exponent = jnp.exp(scores - jnp.max(scores, axis=0, keepdims=True))
    return exponent / jnp.sum(exponent, axis=0, keepdims=True)


def attend_kernel(
    meta_ref, q_ref, k_ref, v_ref, k_up_ref, v_up_ref, k_down_ref, v_down_ref, out_ref, probs_ref
):
    length = meta_ref[1 + pl.program_id(0)]
    rows, width = q_ref.shape[1:]
    first_head, low_mask, high_mask = head_masks()
    for lane in range(0, width, LANES):
        lanes = slice(lane, lane + LANES)
        keys = jnp.concatenate([k_up_ref[0, :, lanes], k_ref[0, :, lanes], k_down_ref[0, :, lanes]], 0)
        values = jnp.concatenate([v_up_ref[0, :, lanes], v_ref[0, :, lanes], v_down_ref[0, :, lanes]], 0)
        for top in range(0, rows, BLOCK_Q):
            bias = score_bias(meta_ref[0] + top, length)
            span = slice(top, top + BLOCK_Q + 2 * WIN)
            queries = two_heads(q_ref[0, top : top + BLOCK_Q, lanes], low_mask, high_mask)
            probs = softmax_of(queries, keys[span], bias).astype(bf16)
            probs_ref[0, lane // LANES, top // BLOCK_Q] = probs
            result = tokens_dot(probs, values[span])
            out_ref[top : top + BLOCK_Q, lanes] = jnp.where(
                first_head, result[:BLOCK_Q], result[BLOCK_Q:]
            ).astype(bf16)


def attention_specs(seqs, seq_rows, width, block):
    own = lambda plane: pl.BlockSpec((1, seq_rows, block), lambda s, h: (plane, s, h))
    rim = lambda plane: pl.BlockSpec((1, WIN, block), lambda s, h: (plane, s, h))
    flat = pl.BlockSpec((seq_rows, block), lambda s, h: (s, h))
    inner = (seq_rows // BLOCK_Q, BLOCK_Q + 2 * WIN, 2 * BLOCK_Q)
    probs = pl.BlockSpec((1, block // LANES) + inner, lambda s, h: (s, h, 0, 0, 0))
    probs_shape = pltpu.HBM((seqs, width // LANES) + inner, bf16)
    return own, rim, flat, probs, probs_shape


def attend_call(meta, qkv, rim_up, rim_down, seqs):
    _, rows, width = qkv.shape
    seq_rows = rows // seqs
    block = 256
    own, rim, flat, probs, probs_shape = attention_specs(seqs, seq_rows, width, block)
    return pl.pallas_call(
        attend_kernel,
        grid=(seqs, width // block),
        in_specs=[SMEM_SPEC, own(0), own(1), own(2), rim(0), rim(1), rim(0), rim(1)],
        out_specs=[flat, probs],
        out_shape=[jax.ShapeDtypeStruct((rows, width), bf16), probs_shape],
        compiler_params=params(16, "arbitrary", "arbitrary"),
        cost_estimate=cost(8 * rows * width * (BLOCK_Q + 2 * WIN), 10 * rows * width),
        name="attend",
    )(meta, qkv, qkv, qkv, rim_up, rim_up, rim_down, rim_down)


def attend_back_kernel(
    q_ref,
    k_ref,
    v_ref,
    k_up_ref,
    v_up_ref,
    k_down_ref,
    v_down_ref,
    probs_ref,
    go_ref,
    cos_ref,
    sin_ref,
    gq_ref,
    gk_ref,
    gv_ref,
    up_ref,
    down_ref,
):
    rows, width = q_ref.shape[1:]
    scale = HEAD_DIM**-0.5
    first_head, low_mask, high_mask = head_masks()

    def turned_back(tile, span):
        return tile * cos_ref[span, :] - swapped_halves(tile) * sin_ref[span, :]

    for lane in range(0, width, LANES):
        lanes = slice(lane, lane + LANES)
        keys = jnp.concatenate([k_up_ref[0, :, lanes], k_ref[0, :, lanes], k_down_ref[0, :, lanes]], 0)
        values = jnp.concatenate([v_up_ref[0, :, lanes], v_ref[0, :, lanes], v_down_ref[0, :, lanes]], 0)
        key_parts, value_parts = [], []
        for top in range(0, rows, BLOCK_Q):
            span = slice(top, top + BLOCK_Q + 2 * WIN)
            queries = two_heads(q_ref[0, top : top + BLOCK_Q, lanes], low_mask, high_mask)
            grads = two_heads(go_ref[top : top + BLOCK_Q, lanes], low_mask, high_mask)
            probs_low = probs_ref[0, lane // LANES, top // BLOCK_Q]
            probs = probs_low.astype(f32)
            grad_probs = dot_nt(values[span], grads)
            delta = jnp.sum(probs * grad_probs, axis=0, keepdims=True)
            grad_scores = (probs * (grad_probs - delta)).astype(bf16)
            result = tokens_dot(grad_scores, keys[span])
            result = jnp.where(first_head, result[:BLOCK_Q], result[BLOCK_Q:]) * scale
            own = slice(WIN + top, WIN + top + BLOCK_Q)
            gq_ref[top : top + BLOCK_Q, lanes] = turned_back(result, own).astype(bf16)
            key_parts.append(dot_nn(grad_scores, queries))
            value_parts.append(dot_nn(probs_low, grads))

        def laid_out(parts):
            pieces = [parts[0][:BLOCK_Q]]
            for before, part in zip(parts, parts[1:]):
                pieces.append(before[BLOCK_Q:] + part[:BLOCK_Q])
            return jnp.concatenate(pieces + [parts[-1][BLOCK_Q:]], axis=0)

        grad_keys = turned_back(laid_out(key_parts) * scale, slice(None))
        grad_values = laid_out(value_parts)
        up_ref[0, :, lanes] = grad_keys[:WIN].astype(bf16)
        up_ref[1, :, lanes] = grad_values[:WIN].astype(bf16)
        down_ref[0, :, lanes] = grad_keys[WIN + rows :].astype(bf16)
        down_ref[1, :, lanes] = grad_values[WIN + rows :].astype(bf16)
        gk_ref[:, lanes] = grad_keys[WIN : WIN + rows]
        gv_ref[:, lanes] = grad_values[WIN : WIN + rows]


def attend_back_call(qkv, rim_up, rim_down, saved, grad_out, cosine, sine, seqs):
    _, rows, width = qkv.shape
    seq_rows = rows // seqs
    block = 256
    own, rim, flat, probs, probs_shape = attention_specs(seqs, seq_rows, width, block)
    table = pl.BlockSpec(cosine.shape, lambda s, h: (0, 0))
    edge = pl.BlockSpec((2, WIN, block), lambda s, h: (0, s, h))
    edge_shape = jax.ShapeDtypeStruct((2, seqs * WIN, width), bf16)
    return pl.pallas_call(
        attend_back_kernel,
        grid=(seqs, width // block),
        in_specs=[
            own(0), own(1), own(2), rim(0), rim(1), rim(0), rim(1),
            probs, flat, table, table,
        ],
        out_specs=[flat, flat, flat, edge, edge],
        out_shape=[
            jax.ShapeDtypeStruct((rows, width), bf16),
            jax.ShapeDtypeStruct((rows, width), f32),
            jax.ShapeDtypeStruct((rows, width), f32),
            edge_shape,
            edge_shape,
        ],
        compiler_params=params(16, "arbitrary", "arbitrary"),
        cost_estimate=cost(20 * rows * width * (BLOCK_Q + 2 * WIN), 20 * rows * width),
        name="attend_back",
    )(qkv, qkv, qkv, rim_up, rim_up, rim_down, rim_down, *far(saved), grad_out, cosine, sine)


def out_kernel(
    meta_ref, o_ref, own_ref, p0, p1, p2, p3, q0, q1, q2, q3, x_ref, valid_ref, gains_ref,
    middle_ref, n_split_ref, o_split_ref, whole_ref, *, size,
):
    @pl.when(pl.program_id(0) == 0)
    def _():
        assemble_two(meta_ref, whole_ref, own_ref, (p0, p1, p2, p3), (q0, q1, q2, q3))

    values = o_ref[...]
    split_columns(values, o_split_ref, slice(None), size)
    middle = x_ref[...].astype(f32) + valid_ref[...] * dot_nn(values, whole_ref[...])
    middle_ref[...] = middle
    scaled, _inverse = normalized(middle)
    split_columns((scaled * gains_ref[1:2, :]).astype(bf16), n_split_ref, slice(None), size)


def out_call(meta, attended, own, parts, start, stretch, x, valid, gains):
    rows, width = x.shape
    slab = own.shape[0]
    size = width // slab
    block = 128
    tile = pl.BlockSpec((block, width), lambda i: (i, 0))
    split = pl.BlockSpec((2, block, width // 2), lambda i: (0, i, 0))
    split_shape = jax.ShapeDtypeStruct((2, rows, width // 2), bf16)
    return pl.pallas_call(
        functools.partial(out_kernel, size=size),
        grid=(rows // block,),
        in_specs=[SMEM_SPEC, tile, once(slab, width)]
        + stretch_specs(parts, start, stretch)
        + [tile, pl.BlockSpec((block, 1), lambda i: (i, 0)), once(8, width)],
        out_specs=[tile, split, split],
        out_shape=[pltpu.HBM((rows, width), f32), split_shape, split_shape],
        scratch_shapes=[pltpu.VMEM((width, width), bf16)],
        compiler_params=params(16, "arbitrary"),
        cost_estimate=cost(2 * rows * width * width, 2 * width * width + 12 * rows * width),
        name="out_norm",
    )(meta, attended, *far(own, *parts, *parts, x), valid, gains)


def gate_kernel(
    meta_ref, n_ref, own1_ref, p0, p1, p2, p3, own2_ref, q0, q1, q2, q3,
    mixed_ref, slope_ref, act_ref, normed_ref, first_ref, second_ref, *, size,
):
    @pl.when(pl.program_id(0) == 0)
    def _():
        for top in range(0, normed_ref.shape[0], 128):
            rows = slice(top, top + 128)
            normed_ref[rows, :] = joined_columns(n_ref, rows, size)

    assemble(meta_ref, first_ref, own1_ref, (p0, p1, p2, p3))
    assemble(meta_ref, second_ref, own2_ref, (q0, q1, q2, q3))
    gate_in = dot_nn(normed_ref[...], first_ref[...])
    gate_up = dot_nn(normed_ref[...], second_ref[...])
    normal_cdf = 0.5 * (1.0 + lax.erf(gate_in * root_half))
    density = jnp.exp(-0.5 * gate_in * gate_in) * inv_root_two_pi
    activated = gate_in * normal_cdf
    mixed_ref[...] = (activated * gate_up).astype(bf16)
    slope_ref[...] = (gate_up * (normal_cdf + gate_in * density)).astype(bf16)
    act_ref[...] = activated.astype(bf16)


def gate_call(meta, normed, owns, parts, block):
    _, rows, half = normed.shape
    width = 2 * half
    slab, hidden = owns[0].shape
    steps = hidden // block
    size = width // slab
    tile = pl.BlockSpec((rows, block), lambda i: (0, i))
    own = pl.BlockSpec((slab, block), lambda i: (0, i))
    return pl.pallas_call(
        functools.partial(gate_kernel, size=size),
        grid=(hidden // block,),
        in_specs=[SMEM_SPEC, once(2, rows, half), own]
        + part_specs(parts, block, lambda i: i)
        + [own]
        + part_specs(parts, block, lambda i: i + steps),
        out_specs=[tile, tile, tile],
        out_shape=[pltpu.HBM((rows, hidden), bf16)] * 3,
        scratch_shapes=[
            pltpu.VMEM((rows, width), bf16),
            pltpu.VMEM((width, block), bf16),
            pltpu.VMEM((width, block), bf16),
        ],
        compiler_params=params(32, "arbitrary"),
        cost_estimate=cost(4 * rows * width * hidden, 4 * width * hidden + 6 * rows * hidden),
        name="gate",
    )(meta, normed, *far(owns[0], *parts, owns[1], *parts))


def gate_back_kernel(
    meta_ref, g_ref, own_ref, p0, p1, p2, p3, slope_ref, act_ref, out_ref, whole_ref, *, block
):
    step = pl.program_id(0)

    @pl.when(step == 0)
    def _():
        rows = own_ref.shape[0]
        count, links, cut, columns = p0.shape
        size = count + 1
        me, core = meta_ref[1], meta_ref[2]
        whole_ref[size * rows :, :] = jnp.zeros_like(whole_ref[size * rows :, :])
        whole_ref[pl.ds(pl.multiple_of(me * rows, 16), rows), :] = own_ref[...]

        def put(halves):
            for steps in range(1, size):
                base = lax.rem(me - steps + size, size) * rows
                for half, parts in enumerate(halves):
                    for part, start in zip(parts, (0, cut)):
                        target = pl.ds(pl.multiple_of(base + start, 16), part.shape[2])
                        for link in range(links):
                            lane = (half * links + link) * columns
                            whole_ref[target, lane : lane + columns] = part[steps - 1, link]

        @pl.when(core == 0)
        def _():
            put(((p0, p1), (p2, p3)))

        @pl.when(core == 1)
        def _():
            put(((p2, p3), (p0, p1)))

    weight = whole_ref[pl.ds(pl.multiple_of(step * block, block), block), :]
    grad_mixed = dot_nt(g_ref[...], weight)
    out_ref[0] = (grad_mixed * slope_ref[...].astype(f32)).astype(bf16)
    out_ref[1] = (grad_mixed * act_ref[...].astype(f32)).astype(bf16)


def gate_back_plain_kernel(g_ref, w_ref, slope_ref, act_ref, out_ref):
    grad_mixed = dot_nt(g_ref[...], w_ref[...])
    out_ref[0] = (grad_mixed * slope_ref[...].astype(f32)).astype(bf16)
    out_ref[1] = (grad_mixed * act_ref[...].astype(f32)).astype(bf16)


def gate_back_call(meta, grad_result, own, parts, slope, act, block):
    rows, width = grad_result.shape
    hidden = slope.shape[1]
    tile = pl.BlockSpec((rows, block), lambda i: (0, i))
    out_spec = pl.BlockSpec((2, rows, block), lambda i: (0, 0, i))
    out_shape = jax.ShapeDtypeStruct((2, rows, hidden), bf16)
    settings = dict(
        grid=(hidden // block,),
        compiler_params=params(28, "arbitrary"),
        cost_estimate=cost(2 * rows * width * hidden, 4 * width * hidden + 8 * rows * hidden),
        name="gate_back",
    )
    if own.shape[0] % 16:
        whole = whole_columns(own, parts, hidden - own.shape[0] * (parts[0].shape[0] + 1))
        out = pl.pallas_call(
            gate_back_plain_kernel,
            in_specs=[once(rows, width), pl.BlockSpec((block, width), lambda i: (i, 0)), tile, tile],
            out_specs=out_spec,
            out_shape=out_shape,
            **settings,
        )(grad_result, whole, slope, act)
        return out, whole
    return pl.pallas_call(
        functools.partial(gate_back_kernel, block=block),
        in_specs=[SMEM_SPEC, once(rows, width), once(*own.shape)]
        + [once(*part.shape) for part in parts]
        + [tile, tile],
        out_specs=[out_spec, fixed(hidden, width)],
        out_shape=[out_shape, jax.ShapeDtypeStruct((hidden, width), bf16)],
        **settings,
    )(meta, *far(grad_result, own, *parts, slope, act))


def down_kernel(
    meta_ref, m_ref, n_ref, g_ref, h_ref, keep0, give0, keep1, give1, state_ref, *, hidden, places
):
    step = pl.program_id(0)
    block, half = m_ref.shape[1], h_ref.shape[1]
    size, links, rows, columns = state_ref.shape
    right = g_ref[:, pl.ds(pl.multiple_of(meta_ref[2] * half, half), half)]
    sums = tokens_dot(m_ref[...], right) + tokens_dot(n_ref[...], h_ref[...])

    def put(first):
        for place in range(size):
            top, end = max(place * rows, first), min((place + 1) * rows, first + block)
            if top >= end:
                continue
            for link in range(links):
                value = sums[top - first : end - first, link * columns : (link + 1) * columns]
                state_ref[place, link, top - place * rows : end - place * rows, :] = value.astype(bf16)

    for number in range(-(-hidden // block)):
        pl.when(step == number)(functools.partial(put, number * block))

    @pl.when(step == pl.num_programs(0) - 1)
    def _():
        height, width = keep0.shape[2:]
        tiles = rows // height
        for part, (keep_ref, give_ref) in enumerate(((keep0, give0), (keep1, give1))):
            own = meta_ref[3 + part]
            span = range(part * (width // columns), min((part + 1) * (width // columns), tiles))
            for place in range(size):
                for number in range(links // 2):
                    base = split_index(number, places[part])
                    for ref, value in ((keep_ref, own), (give_ref, 1 - own)):
                        link = base + value * (1 << places[part])
                        for lane, tile in enumerate(span):
                            ref[place, number, :, lane * columns : (lane + 1) * columns] = state_ref[
                                place, link, tile * height : (tile + 1) * height, :
                            ]
                        if len(span) * columns < width:
                            ref[place, number, :, len(span) * columns :] = jnp.zeros(
                                (height, width - len(span) * columns), bf16
                            )


def first_places():
    return [left.index(bit) for left, bit in zip(bits_left(0), link_orders()[0])]


def piece_rows(width):
    return width // lax.axis_size("fsdp") // (4 << link_count())


def fits(shard, columns, height):
    return shard % 16 == 0 and columns == LANES and height == 16


def down_call(meta, mixed, mixed_other, grad_result, grad_other, hidden, block):
    rows, hidden_pad = mixed.shape
    width = grad_result.shape[1]
    size = lax.axis_size("fsdp")
    links = 1 << link_count()
    shard, columns, height = hidden // size, width // 2 // links, piece_rows(width)
    if not fits(shard, columns, height):
        own = lax.dynamic_slice_in_dim(grad_result, bit_value(0) * (width // 2), width // 2, 1)
        sums = tokens_dot(mixed, own) + tokens_dot(mixed_other, grad_other)
        state = sums[:hidden].astype(bf16).reshape(size, shard, links, columns)
        state = jnp.moveaxis(state, 2, 1).reshape(size, links, 2, height, -1)
        return [halves(state[:, :, part], 0, part) for part in range(2)]
    tiles = -(-shard // height // 2)
    shape = (size, links // 2, height, tiles * columns)
    out = pl.pallas_call(
        functools.partial(down_kernel, hidden=hidden, places=first_places()),
        grid=(hidden_pad // block,),
        in_specs=[SMEM_SPEC]
        + [pl.BlockSpec((rows, block), lambda i: (0, i))] * 2
        + [once(rows, width), once(rows, width // 2)],
        out_specs=[fixed(*shape)] * 4,
        out_shape=[pltpu.HBM(shape, bf16)] * 4,
        scratch_shapes=[pltpu.VMEM((size, links, shard, columns), bf16)],
        compiler_params=params(24, "arbitrary"),
        cost_estimate=cost(2 * rows * width * hidden, width * hidden + 4 * rows * (hidden + width)),
        name="down_sum",
    )(meta, *far(mixed, mixed_other, grad_result, grad_other))
    return [(out[0], out[1]), (out[2], out[3])]


def sum_kernel(meta_ref, left_ref, left_other_ref, right_ref, right_other_ref, *rest, size, links, places, steps):
    state_ref = rest[-1]
    state_ref[...] = (
        tokens_dot(left_ref[meta_ref[2]], right_ref[0]) + tokens_dot(left_other_ref[...], right_other_ref[0])
    ).astype(bf16)
    rows = state_ref.shape[0] // (2 * size * links)

    def put(outs):
        for part in range(2):
            own = meta_ref[3 + part]
            for place in range(size):
                for number in range(links // 2):
                    base = (2 * place + part) * links + split_index(number, places[part])
                    for ref, value in ((outs[2 * part], own), (outs[2 * part + 1], 1 - own)):
                        start = (base + value * (1 << places[part])) * rows
                        ref[place, number] = state_ref[pl.ds(pl.multiple_of(start, rows), rows), :]

    planes = (len(rest) - 1) // 4
    for plane in range(planes):
        pl.when(pl.program_id(0) // steps == plane)(functools.partial(put, rest[4 * plane : 4 * plane + 4]))


def sum_call(meta, left, left_other, right, right_other, block, outside=False):
    _, tokens, height = left.shape
    planes, _, width = right.shape
    size = lax.axis_size("fsdp")
    links = 1 << link_count()
    rows = height // (2 * size * links)
    steps = width // block
    if rows % 16:
        result = []
        for plane in range(planes):
            state = tokens_dot(half_of(left, True), right[plane]) + tokens_dot(left_other, right_other[plane])
            state = state.astype(bf16).reshape(size, 2, links, rows, width)
            result.append([halves(state[:, part], 0, part) for part in range(2)])
        return result
    shape = (size, links // 2, rows, width)
    right_spec = pl.BlockSpec((1, tokens, block), lambda i: (i // steps, 0, i % steps))

    def out_spec(plane):
        return pl.BlockSpec(
            shape[:3] + (block,), lambda i: (0, 0, 0, jnp.clip(i - plane * steps, 0, steps - 1))
        )

    out = pl.pallas_call(
        functools.partial(sum_kernel, size=size, links=links, places=first_places(), steps=steps),
        grid=(planes * steps,),
        in_specs=[SMEM_SPEC, once(2, tokens, height), once(tokens, height), right_spec, right_spec],
        out_specs=[out_spec(plane) for plane in range(planes) for _ in range(4)],
        out_shape=[pltpu.HBM(shape, bf16)] * (4 * planes),
        scratch_shapes=[pltpu.VMEM((height, block), bf16)],
        compiler_params=params(22, "arbitrary"),
        cost_estimate=cost(4 * tokens * height * width * planes, 4 * planes * (height + tokens) * width),
        name="sum_rows",
    )(meta, *far(left, left_other), *(far(right, right_other) if outside else [right] + far(right_other)))
    return [[(out[k], out[k + 1]), (out[k + 2], out[k + 3])] for k in range(0, 4 * planes, 4)]


def fold_kernel(meta_ref, *refs, count, done, places):
    ins, outs = refs[: 4 * count], refs[4 * count :]
    for part in range(2):
        own = meta_ref[3 + 2 * done + part]
        start = 0
        for number in range(count):
            keep_ref, got_ref = ins[4 * number + 2 * part], ins[4 * number + 2 * part + 1]
            size, links, _, width = keep_ref.shape
            for place in range(size):
                for index in range(links // 2):
                    base = split_index(index, places[part])
                    for ref, value in ((outs[2 * part], own), (outs[2 * part + 1], 1 - own)):
                        link = base + value * (1 << places[part])
                        ref[place, index, :, start : start + width] = added(
                            keep_ref[place, link], got_ref[place, link]
                        )
            start += width


def fold_next(meta, blocks, done):
    size = blocks[0][0][0].shape[0]
    places = [left.index(bit) for left, bit in zip(bits_left(done), link_orders()[done])]
    flat = [array for block in blocks for pair in block for array in pair]
    shapes = []
    for part in range(2):
        _, links, rows, _ = blocks[0][part][0].shape
        width = sum(block[part][0].shape[3] for block in blocks)
        shapes += [(size, links // 2, rows, width)] * 2
    if any(shape[2] % 16 for shape in shapes):
        result = []
        for part in range(2):
            state = jnp.concatenate([added(*block[part]) for block in blocks], axis=3)
            result.append(halves(state, done, part))
        return result
    out = pl.pallas_call(
        functools.partial(fold_kernel, count=len(blocks), done=done, places=places),
        grid=(1,),
        in_specs=[SMEM_SPEC] + [once(*array.shape) for array in flat],
        out_specs=[fixed(*shape) for shape in shapes],
        out_shape=[pltpu.HBM(shape, bf16) for shape in shapes],
        compiler_params=params(16, "arbitrary"),
        cost_estimate=cost(0, 3 * sum(array.size for array in flat)),
        name="fold",
    )(meta, *far(*flat))
    return [(out[0], out[1]), (out[2], out[3])]


def finish_kernel(meta_ref, m0, m1, g0, g1, w_ref, out_ref, norm_ref, *down_refs, padded, links):
    step = pl.program_id(0)
    mine = (step < 2) == (meta_ref[2] == 0)
    first = step % 2 == 0
    own = jnp.where(first, m0[...].astype(f32), m1[...].astype(f32))
    got = jnp.where(first, g0[...].astype(f32), g1[...].astype(f32))
    value = jnp.where(mine, own, got)
    hidden = out_ref.shape[1] // 2
    out_ref[:, :hidden] = value[:, :hidden]
    out_ref[:, hidden:] = value[:, padded : padded + hidden]
    sums = jnp.sum(out_ref[...] * w_ref[...].astype(f32), axis=1, keepdims=True)
    norm_ref[0] = jnp.broadcast_to(sums, (sums.shape[0], LANES)).T[:1]
    if down_refs:
        (down_ref,) = down_refs
        height = value.shape[0] // links
        tiles = (value.shape[1] - 2 * padded) // LANES

        def put(core, part):
            for link in range(links):
                for tile in range(tiles):
                    top = (part * tiles + tile) * height
                    if top < down_ref.shape[0]:
                        lane = (core * links + link) * LANES
                        start = 2 * padded + tile * LANES
                        down_ref[top : top + height, lane : lane + LANES] = value[
                            link * height : (link + 1) * height, start : start + LANES
                        ]

        for number in range(4):
            pl.when(step == number)(functools.partial(put, number // 2, number % 2))


def finish_call(meta, parts, w_in, padded, shard, model):
    rows, columns = w_in.shape
    quarter, width = parts[0].shape
    links = 1 << link_count()
    height = quarter // links
    fast = fits(shard, model // 2 // links, height)
    out = pl.pallas_call(
        functools.partial(finish_kernel, padded=padded, links=links),
        grid=(4,),
        in_specs=[SMEM_SPEC]
        + [once(quarter, width)] * 4
        + [pl.BlockSpec((quarter, columns), lambda i: (i, 0))],
        out_specs=[
            pl.BlockSpec((quarter, columns), lambda i: (i, 0)),
            pl.BlockSpec((1, 1, quarter), lambda i: (i, 0, 0)),
        ]
        + [fixed(shard, model)] * fast,
        out_shape=[jax.ShapeDtypeStruct((rows, columns), f32), jax.ShapeDtypeStruct((4, 1, quarter), f32)]
        + [jax.ShapeDtypeStruct((shard, model), f32)] * fast,
        compiler_params=params(30, "arbitrary"),
        cost_estimate=cost(4 * rows * columns, 10 * rows * columns),
        name="finish",
    )(meta, *far(*parts, w_in))
    if fast:
        return out
    mine, got = [
        jnp.stack([part[:, 2 * padded :] for part in pair]).reshape(1, 2, links, height, -1)
        for pair in (parts[:2], parts[2:])
    ]
    whole = jnp.moveaxis(in_order(mine, got, 0, 0), 2, 1).reshape(2 * links, shard, -1)
    return out[0], out[1], jnp.transpose(whole, (1, 0, 2)).reshape(shard, model).astype(f32)


def last_kernel(*refs):
    k0, g0, k1, g1, out_ref = refs
    cut = k0.shape[2]
    for place in range(k0.shape[0]):
        out_ref[place, :cut, :] = added(k0[place, 0], g0[place, 0])
        out_ref[place, cut:, :] = added(k1[place, 0], g1[place, 0])


def fold_last(parts):
    (k0, g0), (k1, g1) = parts
    size, _, cut, width = k0.shape
    rows = cut + k1.shape[2]
    if cut % 16 or k1.shape[2] % 16:
        return jnp.concatenate([added(k0, g0)[:, 0], added(k1, g1)[:, 0]], axis=1)
    return pl.pallas_call(
        last_kernel,
        grid=(1,),
        in_specs=[once(*array.shape) for array in (k0, g0, k1, g1)],
        out_specs=fixed(size, rows, width),
        out_shape=jax.ShapeDtypeStruct((size, rows, width), bf16),
        compiler_params=params(16, "arbitrary"),
        cost_estimate=cost(0, 6 * size * rows * width),
        name="fold_last",
    )(*far(k0, g0, k1, g1))


def middle_back_kernel(
    meta_ref, gu_ref, own1_ref, p0, p1, p2, p3, own2_ref, q0, q1, q2, q3, out_own_ref, r0, r1, r2, r3,
    s0, s1, s2, s3, middle_ref, upstream_ref, valid_ref, gains_ref, grad_ref, branch_ref, att_ref,
    acc, first_ref, second_ref, out_ref,
):
    step = pl.program_id(0)
    assemble(meta_ref, first_ref, own1_ref, (p0, p1, p2, p3))
    assemble(meta_ref, second_ref, own2_ref, (q0, q1, q2, q3))
    total = dot_nt(gu_ref[0], first_ref[...]) + dot_nt(gu_ref[1], second_ref[...])

    @pl.when(step == 0)
    def _():
        acc[...] = total
        assemble_two(meta_ref, out_ref, out_own_ref, (r0, r1, r2, r3), (s0, s1, s2, s3))

    @pl.when(step > 0)
    def _():
        acc[...] += total

    @pl.when(step == pl.num_programs(0) - 1)
    def _():
        for top in range(0, acc.shape[0], 128):
            rows = slice(top, top + 128)
            scaled, inverse = normalized(middle_ref[rows, :])
            grad = upstream_ref[rows, :].astype(f32) + norm_back(
                acc[rows, :], gains_ref[1:2, :], scaled, inverse
            )
            grad_ref[rows, :] = grad
            branch = (grad * valid_ref[rows, :]).astype(bf16)
            branch_ref[rows, :] = branch
            att_ref[rows, :] = dot_nt(branch, out_ref[...]).astype(bf16)


def middle_back_call(
    meta, grad_hidden, owns, parts, out_own, middle, upstream, valid, gains, block
):
    rows, width = middle.shape
    slab = owns[0].shape[0]
    hidden = grad_hidden.shape[2]
    steps = hidden // block
    whole = fixed(rows, width)
    own = pl.BlockSpec((slab, block), lambda i: (0, i))
    flat_low = jax.ShapeDtypeStruct((rows, width), bf16)
    return pl.pallas_call(
        middle_back_kernel,
        grid=(hidden // block,),
        in_specs=[SMEM_SPEC, pl.BlockSpec((2, rows, block), lambda i: (0, 0, i)), own]
        + part_specs(parts, block, lambda i: i)
        + [own]
        + part_specs(parts, block, lambda i: i + steps)
        + [once(slab, width)]
        + stretch_specs(parts, 2 * hidden, block)
        + [whole, whole, once(rows, 1), once(8, width)],
        out_specs=[whole, whole, whole],
        out_shape=[pltpu.HBM((rows, width), f32), flat_low, flat_low],
        scratch_shapes=[
            pltpu.VMEM((rows, width), f32),
            pltpu.VMEM((width, block), bf16),
            pltpu.VMEM((width, block), bf16),
            pltpu.VMEM((width, width), bf16),
        ],
        compiler_params=params(38, "arbitrary"),
        cost_estimate=cost(4 * rows * width * hidden, 4 * width * hidden + 4 * rows * hidden + 12 * rows * width),
        name="middle_back",
    )(meta, grad_hidden, *far(owns[0], *parts, owns[1], *parts, out_own, *parts, *parts, middle, upstream), valid, gains)


def input_back_kernel(
    meta_ref, gqkv_ref, own_ref, p0, p1, p2, p3, x_ref, grad_ref, gains_ref, out_ref, acc, whole_ref
):
    step = pl.program_id(0)
    assemble(meta_ref, whole_ref, own_ref, (p0, p1, p2, p3))
    total = dot_nt(gqkv_ref[...], whole_ref[...])

    @pl.when(step == 0)
    def _():
        acc[...] = total

    @pl.when(step > 0)
    def _():
        acc[...] += total

    @pl.when(step == pl.num_programs(0) - 1)
    def _():
        for top in range(0, acc.shape[0], 128):
            rows = slice(top, top + 128)
            scaled, inverse = normalized(x_ref[rows, :].astype(f32))
            out_ref[rows, :] = (
                grad_ref[rows, :] + norm_back(acc[rows, :], gains_ref[0:1, :], scaled, inverse)
            ).astype(bf16)


def input_back_call(meta, grad_joint, own, parts, x, grad_middle, gains):
    rows, width = x.shape
    slab = own.shape[0]
    block = width
    whole = fixed(rows, width)
    return pl.pallas_call(
        input_back_kernel,
        grid=(3 * width // block,),
        in_specs=[
            SMEM_SPEC,
            pl.BlockSpec((rows, block), lambda i: (0, i)),
            pl.BlockSpec((slab, block), lambda i: (0, i)),
        ]
        + part_specs(parts, block, lambda i: i)
        + [whole, whole, once(8, width)],
        out_specs=whole,
        out_shape=jax.ShapeDtypeStruct((rows, width), bf16),
        scratch_shapes=[pltpu.VMEM((rows, width), f32), pltpu.VMEM((width, block), bf16)],
        compiler_params=params(24, "arbitrary"),
        cost_estimate=cost(6 * rows * width * width, 6 * width * width + 14 * rows * width),
        name="input_back",
    )(meta, *far(grad_joint, own, *parts, x, grad_middle), gains)


def rope_tables(positions):
    halfway = HEAD_DIM // 2
    frequency = 10000.0 ** (-(2.0 * jnp.arange(halfway, dtype=f32)) / HEAD_DIM)
    angles = positions.astype(f32)[:, None] * frequency[None, :]
    cosine, sine = jnp.cos(angles), jnp.sin(angles)
    return (
        jnp.concatenate([cosine] * (LANES // halfway), axis=1),
        jnp.concatenate([-sine, sine] * (LANES // HEAD_DIM), axis=1),
    )


def on_device(inputs, cotangent, lengths, norm_first, w_qkv, w_out, norm_second, w_in, w_down):
    seqs, shard_rows, width = inputs.shape
    rows = seqs * shard_rows
    size = lax.axis_size("fsdp")
    me = lax.axis_index("fsdp")
    hidden = w_in.shape[1] // 2
    block = 896
    hidden_pad = -(-hidden // block) * block
    pad = hidden_pad - hidden
    steps = link_orders()
    near, far, middle_way = runs()

    gains = jnp.pad(jnp.stack([norm_first, norm_second], axis=1), ((0, 0), (0, LANES - 2)))
    came_one = turned_before(row_piece([w_qkv, gains]), range(1, size))
    own_in = [jnp.pad(w_in[:, half * hidden :][:, :hidden], ((0, 0), (0, pad))) for half in range(2)]
    piece_two = row_piece([own_in[0], own_in[1], w_out])
    piece_three = column_piece(w_down)
    first_row = me * shard_rows
    query_pos = first_row + jnp.arange(shard_rows, dtype=jnp.int32)
    rim_pos = first_row - WIN + jnp.arange(shard_rows + 2 * WIN, dtype=jnp.int32)
    cosine, sine = rope_tables(rim_pos)
    valid = (query_pos[None, :] < lengths[:, None]).astype(f32).reshape(rows, 1)
    bits = [bit_value(bit) for pair in steps for bit in pair]
    meta = jnp.stack([first_row, me, bit_value(0)] + bits).astype(jnp.int32)
    meta_rows = jnp.concatenate([first_row.astype(jnp.int32)[None], lengths.astype(jnp.int32)])
    x = inputs.reshape(rows, width)
    upstream = cotangent.reshape(rows, width)
    grad_result = (upstream.astype(f32) * valid).astype(bf16)
    grad_give = lax.dynamic_slice_in_dim(grad_result, (1 - bit_value(0)) * (width // 2), width // 2, 1)
    grad_other = flip(grad_give, 0)
    own_rows = slice(WIN, WIN + shard_rows)
    own_cosine, own_sine = cosine[own_rows], sine[own_rows]
    (
        came_one, piece_two, piece_three, own_in, gains, cosine, sine, own_cosine, own_sine, grad_result, grad_other,
        valid,
    ) = after(
        (
            came_one, piece_two, piece_three, own_in, gains, cosine, sine, own_cosine, own_sine, grad_result,
            grad_other, valid,
        )
    )

    one = widen(row_states(came_one), steps[0], 1)
    came_two = turned_before(piece_two, near)
    one, came_two, piece_two = after((one, came_two, piece_two))

    for bits in steps[1:]:
        one = widen(one, bits, 1)
    came_two = came_two + turned_before(piece_two, far)
    one, came_two, piece_two = after((one, came_two, piece_two))

    parts_one = row_parts(one)
    came_two = came_two + turned_before(piece_two, middle_way)
    normed_first, qkv, gains_all = qkv_call(meta, x, w_qkv, parts_one, gains, own_cosine, own_sine)
    by_seq = qkv.reshape(3, seqs, shard_rows, width)[1:]
    edge = (2, seqs * WIN, width)
    edge_up, edge_down = by_seq[:, :, :WIN].reshape(edge), by_seq[:, :, shard_rows - WIN :].reshape(edge)
    qkv, edge_up, edge_down, came_two, piece_three = after((qkv, edge_up, edge_down, came_two, piece_three))

    rim_down, rim_up = neighbours(edge_up, edge_down)
    two = widen(in_turn(row_states, came_two), steps[0], 1)
    rim_down, rim_up, two, piece_three = after((rim_down, rim_up, two, piece_three))

    for bits in steps[1:]:
        two = widen(two, bits, 1)
    came_three = turned_before(piece_three, range(1, size))
    attended, saved = attend_call(meta_rows, qkv, rim_up, rim_down, seqs)
    two, came_three, attended, normed_first = after((two, came_three, attended, normed_first))

    parts_two = row_parts(two)
    three = widen(column_states(came_three), steps[0], 1)
    first_other = flip(half_of(normed_first, False), 0)
    parts_two, three, attended, first_other = after((parts_two, three, attended, first_other))

    for bits in steps[1:]:
        three = widen(three, bits, 1)
    middle, normed_second, attended_split = out_call(
        meta, attended, w_out, parts_two, 2 * hidden_pad, block, x, valid, gains_all
    )
    second_other = flip(half_of(normed_second, False), 0)
    attended_other = flip(half_of(attended_split, False), 0)
    mixed, slope, act = gate_call(meta, normed_second, own_in, parts_two, block)
    three, mixed, slope, act, second_other, attended_other = after(
        (three, mixed, slope, act, second_other, attended_other)
    )

    parts_three = column_parts(three)
    parts_three, mixed, slope, act = after((parts_three, mixed, slope, act))

    mixed_other = flip(mixed, 0)
    grad_hidden, whole_down = gate_back_call(meta, grad_result, w_down, parts_three, slope, act, block)
    grad_hidden, mixed, mixed_other = after((grad_hidden, mixed, mixed_other))

    hidden_other = flip(grad_hidden, 0)
    down = down_call(meta, mixed, mixed_other, grad_result, grad_other, hidden, block)
    down, hidden_other, grad_hidden = after((down, hidden_other, grad_hidden))

    down = swap(down, 0)
    one, two = sum_call(meta, normed_second, second_other, grad_hidden, hidden_other, block)
    down, one, two, grad_hidden = after((down, one, two, grad_hidden))

    one = swap(one, 0)
    for done in range(1, len(steps)):
        down = swap(fold_next(meta, [down], done), done)
    grad_middle, grad_branch, grad_att = middle_back_call(
        meta, grad_hidden, own_in, parts_two, w_out, middle, upstream, valid, gains_all, block
    )
    one, two, grad_branch, grad_att, down = after((one, two, grad_branch, grad_att, down))

    two = swap(two, 0)
    for done in range(1, len(steps)):
        one = swap(fold_next(meta, [one], done), done)
    down_slots = fold_last(down)
    down_came = turned_slots(down_slots, near)
    grad_q, grad_k, grad_v, edge_up, edge_down = attend_back_call(
        qkv, rim_up, rim_down, saved, grad_att, cosine, sine, seqs
    )
    one, two, edge_up, edge_down, grad_q, grad_branch, down_slots, down_came = after(
        (one, two, edge_up, edge_down, grad_q, grad_branch, down_slots, down_came)
    )

    def spread_start(owned):
        ones = (1,) * link_count()
        cut = owned.shape[0] // 2
        return [part.reshape(ones + part.shape) for part in (owned[:cut], owned[cut:])]

    def spread_end(states):
        mine = jnp.stack([state.reshape((-1,) + state.shape[-2:]) for state in states])
        return in_order(mine[None], flip(mine, 0)[None], 0, 0)

    from_next, from_before = neighbours(edge_up, edge_down)
    branch_other = flip(grad_branch, 0)
    two, branch_other = after((two, branch_other))
    for done in range(1, len(steps)):
        two = swap(fold_next(meta, [two], done), done)
    (outs,) = sum_call(meta, attended_split, attended_other, grad_branch[None], branch_other[None], width // 2)
    one_slots = fold_last(one)
    from_next, from_before, two, one_slots, outs = after((from_next, from_before, two, one_slots, outs))

    def with_edges(own, plane):
        own = own.reshape(seqs, shard_rows, width)
        before = from_before[plane].reshape(seqs, WIN, width).astype(f32)
        later = from_next[plane].reshape(seqs, WIN, width).astype(f32)
        rest = ((0, 0), (0, shard_rows - WIN), (0, 0))
        own = own + jnp.pad(before, rest) + jnp.pad(later, (rest[0], rest[1][::-1], rest[2]))
        return own.reshape(rows, width).astype(bf16)

    outs = swap(outs, 0)
    down_came = down_came + turned_slots(down_slots, far) + turned_slots(down_slots, middle_way)
    grad_joint = jnp.concatenate([grad_q, with_edges(grad_k, 0), with_edges(grad_v, 1)], axis=1)
    joint_other = flip(grad_joint, 0)
    (last,) = sum_call(meta, normed_first, first_other, grad_joint[None], joint_other[None], width, True)
    two_slots = fold_last(two)
    last, grad_joint, outs, one_slots, two_slots, down_came, down_slots = after(
        (last, grad_joint, outs, one_slots, two_slots, down_came, down_slots)
    )

    last = swap(last, 0)
    one_came = turned_slots(one_slots, range(1, size))
    grad_inputs = input_back_call(meta, grad_joint, w_qkv, parts_one, x, grad_middle, gains_all)
    last, grad_inputs, one_came, one_slots, two_slots, down_came, down_slots, mixed = after(
        (last, grad_inputs, one_came, one_slots, two_slots, down_came, down_slots, mixed)
    )

    last = [last, outs]
    for done in range(1, len(steps)):
        last = [swap(fold_next(meta, last, done), done)]
    two_came = turned_slots(two_slots, range(1, size))
    owned = [slot_sum(one_slots, one_came), slot_sum(down_slots, down_came)]
    result = jnp.dot(mixed, whole_down, preferred_element_type=f32)
    output = (middle + valid * result).astype(bf16)
    last, two_came, two_slots, owned, output = after((last, two_came, two_slots, owned, output))

    last_slots = fold_last(last[0])
    last_came = turned_slots(last_slots, near) + turned_slots(last_slots, far)
    spread_in = widen(
        spread_start(jnp.concatenate([owned[0], slot_sum(two_slots, two_came), owned[1]], axis=1)), steps[0], 0
    )
    last_came, spread_in, last_slots = after((last_came, spread_in, last_slots))

    last_came = last_came + turned_slots(last_slots, middle_way)
    for bits in steps[1:]:
        spread_in = widen(spread_in, bits, 0)
    last_came, spread_in, last_slots = after((last_came, spread_in, last_slots))

    spread_last = widen(spread_start(slot_sum(last_slots, last_came)), steps[0], 0)
    in_parts = [state.reshape((-1, state.shape[-1])) for state in spread_in]
    in_parts = in_parts + [flip(part, 0) for part in in_parts]
    spread_last, in_parts = after((spread_last, in_parts))

    for bits in steps[1:]:
        spread_last = widen(spread_last, bits, 0)
    grad_in, grad_second, grad_down = finish_call(meta, in_parts, w_in, hidden_pad, hidden // size, width)
    spread_last, grad_in, grad_second, grad_down = after((spread_last, grad_in, grad_second, grad_down))

    grad_second = grad_second.reshape(-1) / norm_second.astype(f32)
    grad_last = spread_end(spread_last)
    grad_last = grad_last.reshape(-1, grad_last.shape[-1])
    grad_qkv = grad_last[:, : 3 * width].astype(f32)
    grad_out = grad_last[:, 3 * width :].astype(f32)
    grad_first = jnp.sum(grad_qkv * w_qkv.astype(f32), axis=1) / norm_first.astype(f32)
    return (
        output.reshape(inputs.shape),
        grad_inputs.reshape(inputs.shape),
        grad_first,
        grad_qkv,
        grad_out,
        grad_second,
        grad_in,
        grad_down,
    )


def solution(mesh):
    in_specs = (
        P("rep", "fsdp", None),
        P("rep", "fsdp", None),
        P("rep"),
        P("fsdp"),
        P("fsdp", None),
        P("fsdp", None),
        P("fsdp"),
        P("fsdp", None),
        P("fsdp", None),
    )
    out_specs = (
        P("rep", "fsdp", None),
        P("rep", "fsdp", None),
        P("fsdp"),
        P("fsdp", None),
        P("fsdp", None),
        P("fsdp"),
        P("fsdp", None),
        P("fsdp", None),
    )
    return jax.shard_map(
        on_device, mesh=mesh, in_specs=in_specs, out_specs=out_specs, check_vma=False
    )
```

```python
import functools

import jax
import jax.numpy as jnp
from jax import lax
from jax.experimental import pallas as pl
from jax.experimental.pallas import tpu as pltpu
from jax.sharding import PartitionSpec as P

HEAD_DIM = 64
WIN = 64
BLOCK_Q = 128
LANES = 128

epsilon = 1e-05
root_half = 0.7071067811865476
inv_root_two_pi = 0.3989422804014327
f32 = jnp.float32
bf16 = jnp.bfloat16
COST_SCALE = 1.0


def after(value, *before):
    return lax.optimization_barrier((value, before))[0]


def bit_count():
    return lax.axis_size("rep").bit_length() - 1


def bit_value(bit):
    return (lax.axis_index("rep") >> bit) & 1


def link_count():
    return bit_count() - 1


def link_axis(bit):
    return bit_count() - 1 - bit


def flip(value, bit):
    size = lax.axis_size("rep")
    return lax.ppermute(value, "rep", [(i, i ^ (1 << bit)) for i in range(size)])


def turn(value, steps):
    size = lax.axis_size("fsdp")
    return lax.ppermute(value, "fsdp", [(i, (i + steps) % size) for i in range(size)])


def link_orders():
    bits = list(range(1, bit_count()))
    return list(zip(bits, bits[::-1]))


def in_order(mine, got, bit, axis):
    first = bit_value(bit) == 0
    return jnp.concatenate([jnp.where(first, mine, got), jnp.where(first, got, mine)], axis=axis)


def widen(states, bits, lead):
    return [
        in_order(state, flip(state, bit), bit, lead + link_axis(bit)) for state, bit in zip(states, bits)
    ]


def row_piece(shards):
    width = sum(shard.shape[1] for shard in shards)
    links = 1 << link_count()
    core, link = bit_value(0), lax.axis_index("rep") >> 1
    views = [shard.reshape(2, 2, links, -1, shard.shape[1]) for shard in shards]
    rows = views[0].shape[3]
    pieces = [
        lax.dynamic_slice(view, (core, 0, link, 0, 0), (1, 2, 1, rows, view.shape[4])) for view in views
    ]
    return jnp.concatenate(pieces, axis=-1).reshape(2, rows, width)


def row_states(came):
    ones = (1,) * link_count()
    return [
        jnp.stack([piece[part] for piece in came]).reshape((len(came),) + ones + came[0].shape[1:])
        for part in range(2)
    ]


def row_parts(states):
    mine = [state.reshape(state.shape[0], -1, state.shape[-1]) for state in states]
    return mine + [flip(state, 0) for state in mine]


def half_rows(rows):
    return -(-rows // 2 // 16) * 16


def column_piece(shard):
    columns = shard.shape[1] // lax.axis_size("rep")
    place = (bit_value(0) << link_count()) + (lax.axis_index("rep") >> 1)
    return lax.dynamic_slice_in_dim(shard, place * columns, columns, 1)


def column_states(came):
    cut = half_rows(came[0].shape[0])
    ones = (1,) * link_count()
    stacked = jnp.stack(came)
    return [
        part.reshape(part.shape[:1] + ones + part.shape[1:]) for part in (stacked[:, :cut], stacked[:, cut:])
    ]


def column_parts(states):
    mine = [state.reshape((state.shape[0], -1) + state.shape[-2:]) for state in states]
    return mine + [flip(state, 0) for state in mine]


def whole_columns(shard, parts, pad_rows):
    size = lax.axis_size("fsdp")
    me = lax.axis_index("fsdp")
    rows, width = shard.shape
    mine, got = [jnp.concatenate(pair, axis=2) for pair in (parts[:2], parts[2:])]
    joined = in_order(mine, got, 0, 1)
    joined = jnp.transpose(joined, (0, 2, 1, 3)).reshape(size - 1, rows, width)
    whole = jnp.zeros((size * rows + pad_rows, width), shard.dtype)
    whole = lax.dynamic_update_slice(whole, shard, (me * rows, 0))
    for steps in range(1, size):
        source = lax.rem(me - steps + size, size)
        whole = lax.dynamic_update_slice(whole, joined[steps - 1], (source * rows, 0))
    return whole


def turned_before(piece, steps):
    return [turn(piece, step) for step in steps]


def runs():
    size = lax.axis_size("fsdp")
    order = sorted(range(1, size), key=lambda step: (min(step, size - step), step))
    cuts = [(size - 1) * part // 3 for part in range(4)]
    return [order[first:last] for first, last in zip(cuts, cuts[1:])]


def in_turn(states, came):
    order = [step for run in runs() for step in run]
    return states([came[order.index(step)] for step in range(1, lax.axis_size("fsdp"))])


def tokens_dot(left, right):
    return lax.dot_general(left, right, (((0,), (0,)), ((), ())), preferred_element_type=f32)


def half_of(split, mine):
    index = bit_value(0) if mine else 1 - bit_value(0)
    return lax.dynamic_index_in_dim(split, index, 0, False)


def turned_slots(slots, steps):
    size = lax.axis_size("fsdp")
    me = lax.axis_index("fsdp")
    return [
        turn(lax.dynamic_index_in_dim(slots, lax.rem(me + step, size), 0, False), step) for step in steps
    ]


def slot_sum(slots, came):
    total = lax.dynamic_index_in_dim(slots, lax.axis_index("fsdp"), 0, False).astype(f32)
    for part in came:
        total = total + part.astype(f32)
    return total.astype(bf16)


def bits_left(done):
    orders = zip(*link_orders())
    return [sorted(order[done:]) for order in orders]


def split_index(number, place):
    low = number & ((1 << place) - 1)
    return ((number >> place) << (place + 1)) | low


def halves(state, done, part):
    bit = link_orders()[done][part]
    place = bits_left(done)[part].index(bit)
    size, links = state.shape[:2]
    view = state.reshape((size, links >> (place + 1), 2, 1 << place) + state.shape[2:])
    shape = (size, links // 2) + state.shape[2:]
    keep, give = [
        lax.dynamic_index_in_dim(view, index, 2, False).reshape(shape)
        for index in (bit_value(bit), 1 - bit_value(bit))
    ]
    return keep, give


def swap(parts, done):
    return [(keep, flip(give, bit)) for (keep, give), bit in zip(parts, link_orders()[done])]


def added(keep, got):
    return (keep.astype(f32) + got.astype(f32)).astype(bf16)


def neighbours(up, down):
    size = lax.axis_size("fsdp")
    forward = [(i, i + 1) for i in range(size - 1)]
    backward = [(i + 1, i) for i in range(size - 1)]
    return lax.ppermute(up, "fsdp", backward), lax.ppermute(down, "fsdp", forward)


def params(megabytes, *semantics):
    return pltpu.CompilerParams(dimension_semantics=semantics, vmem_limit_bytes=megabytes << 20)


def cost(flops, nbytes):
    return pl.CostEstimate(flops=int(flops * COST_SCALE), bytes_accessed=int(nbytes * COST_SCALE), transcendentals=0)


def far(*arrays):
    return [pltpu.with_memory_space_constraint(array, pltpu.HBM) for array in arrays]


def dot_nn(left, right):
    return jnp.dot(left, right, preferred_element_type=f32)


def dot_nt(left, right):
    return lax.dot_general(left, right, (((1,), (1,)), ((), ())), preferred_element_type=f32)


def normalized(values):
    centred = values - jnp.mean(values, axis=-1, keepdims=True)
    inverse = lax.rsqrt(jnp.mean(centred * centred, axis=-1, keepdims=True) + epsilon)
    return centred * inverse, inverse


def norm_back(grad_out, gain, scaled, inverse):
    grad_scaled = grad_out * gain
    return inverse * (
        grad_scaled
        - jnp.mean(grad_scaled, axis=-1, keepdims=True)
        - scaled * jnp.mean(grad_scaled * scaled, axis=-1, keepdims=True)
    )


def swapped_halves(values):
    width = values.shape[-1]
    lane = lax.broadcasted_iota(jnp.int32, values.shape, values.ndim - 1)
    ahead = pltpu.roll(values, width - HEAD_DIM // 2, values.ndim - 1)
    behind = pltpu.roll(values, HEAD_DIM // 2, values.ndim - 1)
    return jnp.where(lane % HEAD_DIM < HEAD_DIM // 2, ahead, behind)


def assemble(meta_ref, whole_ref, own_ref, part_refs):
    rows = own_ref.shape[0]
    count, quarter = part_refs[0].shape[:2]
    size = count + 1
    me, core = meta_ref[1], meta_ref[2]
    whole_ref[pl.ds(pl.multiple_of(me * rows, quarter), rows), :] = own_ref[...]
    for steps in range(1, size):
        base = lax.rem(me - steps + size, size) * rows
        for number, part_ref in enumerate(part_refs):
            half = core if number < 2 else 1 - core
            start = base + half * (rows // 2) + (number % 2) * quarter
            whole_ref[pl.ds(pl.multiple_of(start, quarter), quarter), :] = part_ref[steps - 1]


def split_columns(values, split_ref, rows, size):
    half = values.shape[1] // size // 2
    for place in range(size):
        for core in range(2):
            start = (2 * place + core) * half
            split_ref[core, rows, place * half : (place + 1) * half] = values[:, start : start + half]


def joined_columns(split_ref, rows, size):
    half = split_ref.shape[2] // size
    return jnp.concatenate(
        [
            split_ref[core, rows, place * half : (place + 1) * half]
            for place in range(size)
            for core in range(2)
        ],
        axis=1,
    )


def assemble_two(meta_ref, whole_ref, own_ref, wide_refs, narrow_refs):
    cut = wide_refs[0].shape[2]
    assemble(meta_ref, whole_ref.at[:, :cut], own_ref.at[:, :cut], wide_refs)
    assemble(meta_ref, whole_ref.at[:, cut:], own_ref.at[:, cut:], narrow_refs)


def stretch_specs(parts, start, block):
    rest = parts[0].shape[2] - start - block
    wide = part_specs(parts, block, lambda i: start // block)
    return wide + part_specs(parts, rest, lambda i: (start + block) // rest)


def part_specs(parts, block, place):
    count, quarter, _ = parts[0].shape
    return [pl.BlockSpec((count, quarter, block), lambda i: (0, 0, place(i)))] * 4


def qkv_kernel(
    meta_ref, x_ref, own_ref, p0, p1, p2, p3, gain_ref, g0, g1, g2, g3, cos_ref, sin_ref,
    split_ref, out_ref, gains_ref, whole_ref, normed_ref, column_ref, *, rope_steps, size,
):
    step = pl.program_id(0)

    @pl.when(step == 0)
    def _():
        assemble(meta_ref, column_ref, gain_ref, (g0, g1, g2, g3))
        row = lax.broadcasted_iota(jnp.int32, gains_ref.shape[:1] + (LANES,), 0)
        lane = lax.broadcasted_iota(jnp.int32, gains_ref.shape[:1] + (LANES,), 1)
        gains_ref[...] = dot_nt((row == lane).astype(f32).astype(bf16), column_ref[...])
        for top in range(0, x_ref.shape[0], 128):
            rows = slice(top, top + 128)
            scaled, _inverse = normalized(x_ref[rows, :].astype(f32))
            normed = (scaled * gains_ref[0:1, :]).astype(bf16)
            normed_ref[rows, :] = normed
            split_columns(normed, split_ref, rows, size)

    assemble(meta_ref, whole_ref, own_ref, (p0, p1, p2, p3))
    product = dot_nn(normed_ref[...], whole_ref[...])

    @pl.when(step >= rope_steps)
    def _():
        out_ref[0] = product.astype(bf16)

    @pl.when(step < rope_steps)
    def _():
        seq_rows = cos_ref.shape[0]
        cosine, sine = cos_ref[...], sin_ref[...]
        for top in range(0, product.shape[0], seq_rows):
            for lane in range(0, product.shape[1], LANES):
                tile = product[top : top + seq_rows, lane : lane + LANES]
                out_ref[0, top : top + seq_rows, lane : lane + LANES] = (
                    tile * cosine + swapped_halves(tile) * sine
                ).astype(bf16)


SMEM_SPEC = pl.BlockSpec(memory_space=pltpu.SMEM)


def fixed(*shape):
    return pl.BlockSpec(shape, lambda i: (0,) * len(shape))


def once(*shape):
    return pl.BlockSpec(shape, lambda i: (0,) * len(shape), pipeline_mode=pl.Buffered(1))


def qkv_call(meta, x, own, parts, own_gains, cosine, sine):
    rows, width = x.shape
    slab = own.shape[0]
    size = width // slab
    block = 512
    per_plane = width // block
    return pl.pallas_call(
        functools.partial(qkv_kernel, rope_steps=2 * per_plane, size=size),
        grid=(3 * per_plane,),
        in_specs=[SMEM_SPEC, once(rows, width), pl.BlockSpec((slab, block), lambda i: (0, i))]
        + part_specs(parts, block, lambda i: i)
        + [once(slab, LANES)]
        + part_specs(parts, LANES, lambda i: 3 * width // LANES)
        + [once(*cosine.shape), once(*sine.shape)],
        out_specs=[
            fixed(2, rows, width // 2),
            pl.BlockSpec((1, rows, block), lambda i: (i // per_plane, 0, i % per_plane)),
            fixed(8, width),
        ],
        out_shape=[
            jax.ShapeDtypeStruct((2, rows, width // 2), bf16),
            jax.ShapeDtypeStruct((3, rows, width), bf16),
            jax.ShapeDtypeStruct((8, width), f32),
        ],
        scratch_shapes=[
            pltpu.VMEM((width, block), bf16),
            pltpu.VMEM((rows, width), bf16),
            pltpu.VMEM((width, LANES), bf16),
        ],
        compiler_params=params(20, "arbitrary"),
        cost_estimate=cost(6 * rows * width * width, 6 * width * width + 10 * rows * width),
        name="qkv",
    )(meta, *far(x, own, *parts), own_gains, *far(*parts), cosine, sine)


def head_masks():
    lane = lax.broadcasted_iota(jnp.int32, (1, LANES), 1)
    first = lane < HEAD_DIM
    return first, first.astype(f32).astype(bf16), (~first).astype(f32).astype(bf16)


def two_heads(tile, low_mask, high_mask):
    return jnp.concatenate([tile * low_mask, tile * high_mask], axis=0)


def score_bias(first_row, length):
    shape = (BLOCK_Q + 2 * WIN, BLOCK_Q)
    key = first_row - WIN + lax.broadcasted_iota(jnp.int32, shape, 0)
    query = first_row + lax.broadcasted_iota(jnp.int32, shape, 1)
    near = jnp.abs(query - key) <= WIN
    live = (key >= 0) & (key < length)
    bias = jnp.where(near & (live | (query == key)), 0.0, -1e30).astype(f32)
    return jnp.concatenate([bias, bias], axis=1)


def softmax_of(queries, keys, bias):
    scores = dot_nt(keys, queries) * (HEAD_DIM**-0.5) + bias
    exponent = jnp.exp(scores - jnp.max(scores, axis=0, keepdims=True))
    return exponent / jnp.sum(exponent, axis=0, keepdims=True)


def attend_kernel(
    meta_ref, q_ref, k_ref, v_ref, k_up_ref, v_up_ref, k_down_ref, v_down_ref, out_ref, probs_ref
):
    length = meta_ref[1 + pl.program_id(0)]
    rows, width = q_ref.shape[1:]
    first_head, low_mask, high_mask = head_masks()
    for lane in range(0, width, LANES):
        lanes = slice(lane, lane + LANES)
        keys = jnp.concatenate([k_up_ref[0, :, lanes], k_ref[0, :, lanes], k_down_ref[0, :, lanes]], 0)
        values = jnp.concatenate([v_up_ref[0, :, lanes], v_ref[0, :, lanes], v_down_ref[0, :, lanes]], 0)
        for top in range(0, rows, BLOCK_Q):
            bias = score_bias(meta_ref[0] + top, length)
            span = slice(top, top + BLOCK_Q + 2 * WIN)
            queries = two_heads(q_ref[0, top : top + BLOCK_Q, lanes], low_mask, high_mask)
            probs = softmax_of(queries, keys[span], bias).astype(bf16)
            probs_ref[0, lane // LANES, top // BLOCK_Q] = probs
            result = tokens_dot(probs, values[span])
            out_ref[top : top + BLOCK_Q, lanes] = jnp.where(
                first_head, result[:BLOCK_Q], result[BLOCK_Q:]
            ).astype(bf16)


def attention_specs(seqs, seq_rows, width, block):
    own = lambda plane: pl.BlockSpec((1, seq_rows, block), lambda s, h: (plane, s, h))
    rim = lambda plane: pl.BlockSpec((1, WIN, block), lambda s, h: (plane, s, h))
    flat = pl.BlockSpec((seq_rows, block), lambda s, h: (s, h))
    inner = (seq_rows // BLOCK_Q, BLOCK_Q + 2 * WIN, 2 * BLOCK_Q)
    probs = pl.BlockSpec((1, block // LANES) + inner, lambda s, h: (s, h, 0, 0, 0))
    probs_shape = pltpu.HBM((seqs, width // LANES) + inner, bf16)
    return own, rim, flat, probs, probs_shape


def attend_call(meta, qkv, rim_up, rim_down, seqs):
    _, rows, width = qkv.shape
    seq_rows = rows // seqs
    block = 256
    own, rim, flat, probs, probs_shape = attention_specs(seqs, seq_rows, width, block)
    return pl.pallas_call(
        attend_kernel,
        grid=(seqs, width // block),
        in_specs=[SMEM_SPEC, own(0), own(1), own(2), rim(0), rim(1), rim(0), rim(1)],
        out_specs=[flat, probs],
        out_shape=[jax.ShapeDtypeStruct((rows, width), bf16), probs_shape],
        compiler_params=params(16, "arbitrary", "arbitrary"),
        cost_estimate=cost(8 * rows * width * (BLOCK_Q + 2 * WIN), 10 * rows * width),
        name="attend",
    )(meta, qkv, qkv, qkv, rim_up, rim_up, rim_down, rim_down)


def attend_back_kernel(
    q_ref,
    k_ref,
    v_ref,
    k_up_ref,
    v_up_ref,
    k_down_ref,
    v_down_ref,
    probs_ref,
    go_ref,
    cos_ref,
    sin_ref,
    gq_ref,
    gk_ref,
    gv_ref,
    up_ref,
    down_ref,
):
    rows, width = q_ref.shape[1:]
    scale = HEAD_DIM**-0.5
    first_head, low_mask, high_mask = head_masks()

    def turned_back(tile, span):
        return tile * cos_ref[span, :] - swapped_halves(tile) * sin_ref[span, :]

    for lane in range(0, width, LANES):
        lanes = slice(lane, lane + LANES)
        keys = jnp.concatenate([k_up_ref[0, :, lanes], k_ref[0, :, lanes], k_down_ref[0, :, lanes]], 0)
        values = jnp.concatenate([v_up_ref[0, :, lanes], v_ref[0, :, lanes], v_down_ref[0, :, lanes]], 0)
        key_parts, value_parts = [], []
        for top in range(0, rows, BLOCK_Q):
            span = slice(top, top + BLOCK_Q + 2 * WIN)
            queries = two_heads(q_ref[0, top : top + BLOCK_Q, lanes], low_mask, high_mask)
            grads = two_heads(go_ref[top : top + BLOCK_Q, lanes], low_mask, high_mask)
            probs_low = probs_ref[0, lane // LANES, top // BLOCK_Q]
            probs = probs_low.astype(f32)
            grad_probs = dot_nt(values[span], grads)
            delta = jnp.sum(probs * grad_probs, axis=0, keepdims=True)
            grad_scores = (probs * (grad_probs - delta)).astype(bf16)
            result = tokens_dot(grad_scores, keys[span])
            result = jnp.where(first_head, result[:BLOCK_Q], result[BLOCK_Q:]) * scale
            own = slice(WIN + top, WIN + top + BLOCK_Q)
            gq_ref[top : top + BLOCK_Q, lanes] = turned_back(result, own).astype(bf16)
            key_parts.append(dot_nn(grad_scores, queries))
            value_parts.append(dot_nn(probs_low, grads))

        def laid_out(parts):
            pieces = [parts[0][:BLOCK_Q]]
            for before, part in zip(parts, parts[1:]):
                pieces.append(before[BLOCK_Q:] + part[:BLOCK_Q])
            return jnp.concatenate(pieces + [parts[-1][BLOCK_Q:]], axis=0)

        grad_keys = turned_back(laid_out(key_parts) * scale, slice(None))
        grad_values = laid_out(value_parts)
        up_ref[0, :, lanes] = grad_keys[:WIN].astype(bf16)
        up_ref[1, :, lanes] = grad_values[:WIN].astype(bf16)
        down_ref[0, :, lanes] = grad_keys[WIN + rows :].astype(bf16)
        down_ref[1, :, lanes] = grad_values[WIN + rows :].astype(bf16)
        gk_ref[:, lanes] = grad_keys[WIN : WIN + rows]
        gv_ref[:, lanes] = grad_values[WIN : WIN + rows]


def attend_back_call(qkv, rim_up, rim_down, saved, grad_out, cosine, sine, seqs):
    _, rows, width = qkv.shape
    seq_rows = rows // seqs
    block = 256
    own, rim, flat, probs, probs_shape = attention_specs(seqs, seq_rows, width, block)
    table = pl.BlockSpec(cosine.shape, lambda s, h: (0, 0))
    edge = pl.BlockSpec((2, WIN, block), lambda s, h: (0, s, h))
    edge_shape = jax.ShapeDtypeStruct((2, seqs * WIN, width), bf16)
    return pl.pallas_call(
        attend_back_kernel,
        grid=(seqs, width // block),
        in_specs=[
            own(0), own(1), own(2), rim(0), rim(1), rim(0), rim(1),
            probs, flat, table, table,
        ],
        out_specs=[flat, flat, flat, edge, edge],
        out_shape=[
            jax.ShapeDtypeStruct((rows, width), bf16),
            jax.ShapeDtypeStruct((rows, width), f32),
            jax.ShapeDtypeStruct((rows, width), f32),
            edge_shape,
            edge_shape,
        ],
        compiler_params=params(16, "arbitrary", "arbitrary"),
        cost_estimate=cost(20 * rows * width * (BLOCK_Q + 2 * WIN), 20 * rows * width),
        name="attend_back",
    )(qkv, qkv, qkv, rim_up, rim_up, rim_down, rim_down, *far(saved), grad_out, cosine, sine)


def out_kernel(
    meta_ref, o_ref, own_ref, p0, p1, p2, p3, q0, q1, q2, q3, x_ref, valid_ref, gains_ref,
    middle_ref, n_split_ref, o_split_ref, whole_ref, *, size,
):
    @pl.when(pl.program_id(0) == 0)
    def _():
        assemble_two(meta_ref, whole_ref, own_ref, (p0, p1, p2, p3), (q0, q1, q2, q3))

    values = o_ref[...]
    split_columns(values, o_split_ref, slice(None), size)
    middle = x_ref[...].astype(f32) + valid_ref[...] * dot_nn(values, whole_ref[...])
    middle_ref[...] = middle
    scaled, _inverse = normalized(middle)
    split_columns((scaled * gains_ref[1:2, :]).astype(bf16), n_split_ref, slice(None), size)


def out_call(meta, attended, own, parts, start, stretch, x, valid, gains):
    rows, width = x.shape
    slab = own.shape[0]
    size = width // slab
    block = 128
    tile = pl.BlockSpec((block, width), lambda i: (i, 0))
    split = pl.BlockSpec((2, block, width // 2), lambda i: (0, i, 0))
    split_shape = jax.ShapeDtypeStruct((2, rows, width // 2), bf16)
    return pl.pallas_call(
        functools.partial(out_kernel, size=size),
        grid=(rows // block,),
        in_specs=[SMEM_SPEC, tile, once(slab, width)]
        + stretch_specs(parts, start, stretch)
        + [tile, pl.BlockSpec((block, 1), lambda i: (i, 0)), once(8, width)],
        out_specs=[tile, split, split],
        out_shape=[pltpu.HBM((rows, width), f32), split_shape, split_shape],
        scratch_shapes=[pltpu.VMEM((width, width), bf16)],
        compiler_params=params(16, "arbitrary"),
        cost_estimate=cost(2 * rows * width * width, 2 * width * width + 12 * rows * width),
        name="out_norm",
    )(meta, attended, *far(own, *parts, *parts, x), valid, gains)


def gate_kernel(
    meta_ref, n_ref, own1_ref, p0, p1, p2, p3, own2_ref, q0, q1, q2, q3,
    mixed_ref, slope_ref, act_ref, normed_ref, first_ref, second_ref, *, size,
):
    @pl.when(pl.program_id(0) == 0)
    def _():
        for top in range(0, normed_ref.shape[0], 128):
            rows = slice(top, top + 128)
            normed_ref[rows, :] = joined_columns(n_ref, rows, size)

    assemble(meta_ref, first_ref, own1_ref, (p0, p1, p2, p3))
    assemble(meta_ref, second_ref, own2_ref, (q0, q1, q2, q3))
    gate_in = dot_nn(normed_ref[...], first_ref[...])
    gate_up = dot_nn(normed_ref[...], second_ref[...])
    normal_cdf = 0.5 * (1.0 + lax.erf(gate_in * root_half))
    density = jnp.exp(-0.5 * gate_in * gate_in) * inv_root_two_pi
    activated = gate_in * normal_cdf
    mixed_ref[...] = (activated * gate_up).astype(bf16)
    slope_ref[...] = (gate_up * (normal_cdf + gate_in * density)).astype(bf16)
    act_ref[...] = activated.astype(bf16)


def gate_call(meta, normed, owns, parts, block):
    _, rows, half = normed.shape
    width = 2 * half
    slab, hidden = owns[0].shape
    steps = hidden // block
    size = width // slab
    tile = pl.BlockSpec((rows, block), lambda i: (0, i))
    own = pl.BlockSpec((slab, block), lambda i: (0, i))
    return pl.pallas_call(
        functools.partial(gate_kernel, size=size),
        grid=(hidden // block,),
        in_specs=[SMEM_SPEC, once(2, rows, half), own]
        + part_specs(parts, block, lambda i: i)
        + [own]
        + part_specs(parts, block, lambda i: i + steps),
        out_specs=[tile, tile, tile],
        out_shape=[pltpu.HBM((rows, hidden), bf16)] * 3,
        scratch_shapes=[
            pltpu.VMEM((rows, width), bf16),
            pltpu.VMEM((width, block), bf16),
            pltpu.VMEM((width, block), bf16),
        ],
        compiler_params=params(32, "arbitrary"),
        cost_estimate=cost(4 * rows * width * hidden, 4 * width * hidden + 6 * rows * hidden),
        name="gate",
    )(meta, normed, *far(owns[0], *parts, owns[1], *parts))


def gate_back_kernel(
    meta_ref, g_ref, own_ref, p0, p1, p2, p3, slope_ref, act_ref, out_ref, whole_ref, *, block
):
    step = pl.program_id(0)

    @pl.when(step == 0)
    def _():
        rows = own_ref.shape[0]
        count, links, cut, columns = p0.shape
        size = count + 1
        me, core = meta_ref[1], meta_ref[2]
        whole_ref[size * rows :, :] = jnp.zeros_like(whole_ref[size * rows :, :])
        whole_ref[pl.ds(pl.multiple_of(me * rows, 16), rows), :] = own_ref[...]

        def put(halves):
            for steps in range(1, size):
                base = lax.rem(me - steps + size, size) * rows
                for half, parts in enumerate(halves):
                    for part, start in zip(parts, (0, cut)):
                        target = pl.ds(pl.multiple_of(base + start, 16), part.shape[2])
                        for link in range(links):
                            lane = (half * links + link) * columns
                            whole_ref[target, lane : lane + columns] = part[steps - 1, link]

        @pl.when(core == 0)
        def _():
            put(((p0, p1), (p2, p3)))

        @pl.when(core == 1)
        def _():
            put(((p2, p3), (p0, p1)))

    weight = whole_ref[pl.ds(pl.multiple_of(step * block, block), block), :]
    grad_mixed = dot_nt(g_ref[...], weight)
    out_ref[0] = (grad_mixed * slope_ref[...].astype(f32)).astype(bf16)
    out_ref[1] = (grad_mixed * act_ref[...].astype(f32)).astype(bf16)


def gate_back_plain_kernel(g_ref, w_ref, slope_ref, act_ref, out_ref):
    grad_mixed = dot_nt(g_ref[...], w_ref[...])
    out_ref[0] = (grad_mixed * slope_ref[...].astype(f32)).astype(bf16)
    out_ref[1] = (grad_mixed * act_ref[...].astype(f32)).astype(bf16)


def gate_back_call(meta, grad_result, own, parts, slope, act, block):
    rows, width = grad_result.shape
    hidden = slope.shape[1]
    tile = pl.BlockSpec((rows, block), lambda i: (0, i))
    out_spec = pl.BlockSpec((2, rows, block), lambda i: (0, 0, i))
    out_shape = jax.ShapeDtypeStruct((2, rows, hidden), bf16)
    settings = dict(
        grid=(hidden // block,),
        compiler_params=params(28, "arbitrary"),
        cost_estimate=cost(2 * rows * width * hidden, 4 * width * hidden + 8 * rows * hidden),
        name="gate_back",
    )
    if own.shape[0] % 16:
        whole = whole_columns(own, parts, hidden - own.shape[0] * (parts[0].shape[0] + 1))
        out = pl.pallas_call(
            gate_back_plain_kernel,
            in_specs=[once(rows, width), pl.BlockSpec((block, width), lambda i: (i, 0)), tile, tile],
            out_specs=out_spec,
            out_shape=out_shape,
            **settings,
        )(grad_result, whole, slope, act)
        return out, whole
    return pl.pallas_call(
        functools.partial(gate_back_kernel, block=block),
        in_specs=[SMEM_SPEC, once(rows, width), once(*own.shape)]
        + [once(*part.shape) for part in parts]
        + [tile, tile],
        out_specs=[out_spec, fixed(hidden, width)],
        out_shape=[out_shape, jax.ShapeDtypeStruct((hidden, width), bf16)],
        **settings,
    )(meta, *far(grad_result, own, *parts, slope, act))


def down_kernel(
    meta_ref, m_ref, n_ref, g_ref, h_ref, keep0, give0, keep1, give1, state_ref, *, hidden, places
):
    step = pl.program_id(0)
    block, half = m_ref.shape[1], h_ref.shape[1]
    size, links, rows, columns = state_ref.shape
    right = g_ref[:, pl.ds(pl.multiple_of(meta_ref[2] * half, half), half)]
    sums = tokens_dot(m_ref[...], right) + tokens_dot(n_ref[...], h_ref[...])

    def put(first):
        for place in range(size):
            top, end = max(place * rows, first), min((place + 1) * rows, first + block)
            if top >= end:
                continue
            for link in range(links):
                value = sums[top - first : end - first, link * columns : (link + 1) * columns]
                state_ref[place, link, top - place * rows : end - place * rows, :] = value.astype(bf16)

    for number in range(-(-hidden // block)):
        pl.when(step == number)(functools.partial(put, number * block))

    @pl.when(step == pl.num_programs(0) - 1)
    def _():
        height, width = keep0.shape[2:]
        tiles = rows // height
        for part, (keep_ref, give_ref) in enumerate(((keep0, give0), (keep1, give1))):
            own = meta_ref[3 + part]
            span = range(part * (width // columns), min((part + 1) * (width // columns), tiles))
            for place in range(size):
                for number in range(links // 2):
                    base = split_index(number, places[part])
                    for ref, value in ((keep_ref, own), (give_ref, 1 - own)):
                        link = base + value * (1 << places[part])
                        for lane, tile in enumerate(span):
                            ref[place, number, :, lane * columns : (lane + 1) * columns] = state_ref[
                                place, link, tile * height : (tile + 1) * height, :
                            ]
                        if len(span) * columns < width:
                            ref[place, number, :, len(span) * columns :] = jnp.zeros(
                                (height, width - len(span) * columns), bf16
                            )


def first_places():
    return [left.index(bit) for left, bit in zip(bits_left(0), link_orders()[0])]


def piece_rows(width):
    return width // lax.axis_size("fsdp") // (4 << link_count())


def fits(shard, columns, height):
    return shard % 16 == 0 and columns == LANES and height == 16


def down_call(meta, mixed, mixed_other, grad_result, grad_other, hidden, block):
    rows, hidden_pad = mixed.shape
    width = grad_result.shape[1]
    size = lax.axis_size("fsdp")
    links = 1 << link_count()
    shard, columns, height = hidden // size, width // 2 // links, piece_rows(width)
    if not fits(shard, columns, height):
        own = lax.dynamic_slice_in_dim(grad_result, bit_value(0) * (width // 2), width // 2, 1)
        sums = tokens_dot(mixed, own) + tokens_dot(mixed_other, grad_other)
        state = sums[:hidden].astype(bf16).reshape(size, shard, links, columns)
        state = jnp.moveaxis(state, 2, 1).reshape(size, links, 2, height, -1)
        return [halves(state[:, :, part], 0, part) for part in range(2)]
    tiles = -(-shard // height // 2)
    shape = (size, links // 2, height, tiles * columns)
    out = pl.pallas_call(
        functools.partial(down_kernel, hidden=hidden, places=first_places()),
        grid=(hidden_pad // block,),
        in_specs=[SMEM_SPEC]
        + [pl.BlockSpec((rows, block), lambda i: (0, i))] * 2
        + [once(rows, width), once(rows, width // 2)],
        out_specs=[fixed(*shape)] * 4,
        out_shape=[pltpu.HBM(shape, bf16)] * 4,
        scratch_shapes=[pltpu.VMEM((size, links, shard, columns), bf16)],
        compiler_params=params(24, "arbitrary"),
        cost_estimate=cost(2 * rows * width * hidden, width * hidden + 4 * rows * (hidden + width)),
        name="down_sum",
    )(meta, *far(mixed, mixed_other, grad_result, grad_other))
    return [(out[0], out[1]), (out[2], out[3])]


def sum_kernel(meta_ref, left_ref, left_other_ref, right_ref, right_other_ref, *rest, size, links, places, steps):
    state_ref = rest[-1]
    state_ref[...] = (
        tokens_dot(left_ref[meta_ref[2]], right_ref[0]) + tokens_dot(left_other_ref[...], right_other_ref[0])
    ).astype(bf16)
    rows = state_ref.shape[0] // (2 * size * links)

    def put(outs):
        for part in range(2):
            own = meta_ref[3 + part]
            for place in range(size):
                for number in range(links // 2):
                    base = (2 * place + part) * links + split_index(number, places[part])
                    for ref, value in ((outs[2 * part], own), (outs[2 * part + 1], 1 - own)):
                        start = (base + value * (1 << places[part])) * rows
                        ref[place, number] = state_ref[pl.ds(pl.multiple_of(start, rows), rows), :]

    planes = (len(rest) - 1) // 4
    for plane in range(planes):
        pl.when(pl.program_id(0) // steps == plane)(functools.partial(put, rest[4 * plane : 4 * plane + 4]))


def sum_call(meta, left, left_other, right, right_other, block, outside=False):
    _, tokens, height = left.shape
    planes, _, width = right.shape
    size = lax.axis_size("fsdp")
    links = 1 << link_count()
    rows = height // (2 * size * links)
    steps = width // block
    if rows % 16:
        result = []
        for plane in range(planes):
            state = tokens_dot(half_of(left, True), right[plane]) + tokens_dot(left_other, right_other[plane])
            state = state.astype(bf16).reshape(size, 2, links, rows, width)
            result.append([halves(state[:, part], 0, part) for part in range(2)])
        return result
    shape = (size, links // 2, rows, width)
    right_spec = pl.BlockSpec((1, tokens, block), lambda i: (i // steps, 0, i % steps))

    def out_spec(plane):
        return pl.BlockSpec(
            shape[:3] + (block,), lambda i: (0, 0, 0, jnp.clip(i - plane * steps, 0, steps - 1))
        )

    out = pl.pallas_call(
        functools.partial(sum_kernel, size=size, links=links, places=first_places(), steps=steps),
        grid=(planes * steps,),
        in_specs=[SMEM_SPEC, once(2, tokens, height), once(tokens, height), right_spec, right_spec],
        out_specs=[out_spec(plane) for plane in range(planes) for _ in range(4)],
        out_shape=[jax.ShapeDtypeStruct(shape, bf16) if outside else pltpu.HBM(shape, bf16)] * (4 * planes),
        scratch_shapes=[pltpu.VMEM((height, block), bf16)],
        compiler_params=params(22, "arbitrary"),
        cost_estimate=cost(4 * tokens * height * width * planes, 4 * planes * (height + tokens) * width),
        name="sum_rows",
    )(meta, *far(left, left_other), *(far(right, right_other) if outside else [right] + far(right_other)))
    return [[(out[k], out[k + 1]), (out[k + 2], out[k + 3])] for k in range(0, 4 * planes, 4)]


def fold_kernel(meta_ref, *refs, count, done, places):
    ins, outs = refs[: 4 * count], refs[4 * count :]
    for part in range(2):
        own = meta_ref[3 + 2 * done + part]
        start = 0
        for number in range(count):
            keep_ref, got_ref = ins[4 * number + 2 * part], ins[4 * number + 2 * part + 1]
            size, links, _, width = keep_ref.shape
            for place in range(size):
                for index in range(links // 2):
                    base = split_index(index, places[part])
                    for ref, value in ((outs[2 * part], own), (outs[2 * part + 1], 1 - own)):
                        link = base + value * (1 << places[part])
                        ref[place, index, :, start : start + width] = added(
                            keep_ref[place, link], got_ref[place, link]
                        )
            start += width


def fold_next(meta, blocks, done, near_by=False):
    size = blocks[0][0][0].shape[0]
    places = [left.index(bit) for left, bit in zip(bits_left(done), link_orders()[done])]
    flat = [array for block in blocks for pair in block for array in pair]
    shapes = []
    for part in range(2):
        _, links, rows, _ = blocks[0][part][0].shape
        width = sum(block[part][0].shape[3] for block in blocks)
        shapes += [(size, links // 2, rows, width)] * 2
    if any(shape[2] % 16 for shape in shapes):
        result = []
        for part in range(2):
            state = jnp.concatenate([added(*block[part]) for block in blocks], axis=3)
            result.append(halves(state, done, part))
        return result
    out = pl.pallas_call(
        functools.partial(fold_kernel, count=len(blocks), done=done, places=places),
        grid=(1,),
        in_specs=[SMEM_SPEC] + [once(*array.shape) for array in flat],
        out_specs=[fixed(*shape) for shape in shapes],
        out_shape=[jax.ShapeDtypeStruct(shape, bf16) if near_by else pltpu.HBM(shape, bf16) for shape in shapes],
        compiler_params=params(16, "arbitrary"),
        cost_estimate=cost(0, 3 * sum(array.size for array in flat)),
        name="fold",
    )(meta, *(flat if near_by else far(*flat)))
    return [(out[0], out[1]), (out[2], out[3])]


def finish_kernel(meta_ref, m0, m1, g0, g1, w_ref, out_ref, norm_ref, *rest, padded, links):
    step = pl.program_id(0)
    mine = (step < 2) == (meta_ref[2] == 0)
    first = step % 2 == 0
    down_refs, rows_ref = rest[:-1], rest[-1]
    for source, own, even in ((m0, True, True), (m1, True, False), (g0, False, True), (g1, False, False)):

        @pl.when((mine == own) & (first == even))
        def _(source=source):
            rows_ref[...] = source[...]

    value = rows_ref[...].astype(f32)
    hidden = out_ref.shape[1] // 2
    out_ref[:, :hidden] = value[:, :hidden]
    out_ref[:, hidden:] = value[:, padded : padded + hidden]
    sums = jnp.sum(out_ref[...] * w_ref[...].astype(f32), axis=1, keepdims=True)
    norm_ref[0] = jnp.broadcast_to(sums, (sums.shape[0], LANES)).T[:1]
    if down_refs:
        (down_ref,) = down_refs
        height = value.shape[0] // links
        tiles = (value.shape[1] - 2 * padded) // LANES

        def put(core, part):
            for link in range(links):
                for tile in range(tiles):
                    top = (part * tiles + tile) * height
                    if top < down_ref.shape[0]:
                        lane = (core * links + link) * LANES
                        start = 2 * padded + tile * LANES
                        down_ref[top : top + height, lane : lane + LANES] = value[
                            link * height : (link + 1) * height, start : start + LANES
                        ]

        for number in range(4):
            pl.when(step == number)(functools.partial(put, number // 2, number % 2))


def finish_call(meta, parts, w_in, padded, shard, model):
    rows, columns = w_in.shape
    quarter, width = parts[0].shape
    links = 1 << link_count()
    height = quarter // links
    fast = fits(shard, model // 2 // links, height)
    out = pl.pallas_call(
        functools.partial(finish_kernel, padded=padded, links=links),
        grid=(4,),
        in_specs=[SMEM_SPEC]
        + [once(quarter, width)] * 4
        + [pl.BlockSpec((quarter, columns), lambda i: (i, 0))],
        out_specs=[
            pl.BlockSpec((quarter, columns), lambda i: (i, 0)),
            pl.BlockSpec((1, 1, quarter), lambda i: (i, 0, 0)),
        ]
        + [fixed(shard, model)] * fast,
        out_shape=[jax.ShapeDtypeStruct((rows, columns), f32), jax.ShapeDtypeStruct((4, 1, quarter), f32)]
        + [jax.ShapeDtypeStruct((shard, model), f32)] * fast,
        scratch_shapes=[pltpu.VMEM((quarter, width), bf16)],
        compiler_params=params(30, "arbitrary"),
        cost_estimate=cost(4 * rows * columns, 10 * rows * columns),
        name="finish",
    )(meta, *far(*parts, w_in))
    if fast:
        return out
    mine, got = [
        jnp.stack([part[:, 2 * padded :] for part in pair]).reshape(1, 2, links, height, -1)
        for pair in (parts[:2], parts[2:])
    ]
    whole = jnp.moveaxis(in_order(mine, got, 0, 0), 2, 1).reshape(2 * links, shard, -1)
    return out[0], out[1], jnp.transpose(whole, (1, 0, 2)).reshape(shard, model).astype(f32)


def last_kernel(*refs):
    k0, g0, k1, g1, out_ref = refs
    cut = k0.shape[2]
    for place in range(k0.shape[0]):
        out_ref[place, :cut, :] = added(k0[place, 0], g0[place, 0])
        out_ref[place, cut:, :] = added(k1[place, 0], g1[place, 0])


def fold_last(parts, near_by=False):
    (k0, g0), (k1, g1) = parts
    size, _, cut, width = k0.shape
    rows = cut + k1.shape[2]
    if cut % 16 or k1.shape[2] % 16:
        return jnp.concatenate([added(k0, g0)[:, 0], added(k1, g1)[:, 0]], axis=1)
    return pl.pallas_call(
        last_kernel,
        grid=(1,),
        in_specs=[once(*array.shape) for array in (k0, g0, k1, g1)],
        out_specs=fixed(size, rows, width),
        out_shape=jax.ShapeDtypeStruct((size, rows, width), bf16),
        compiler_params=params(16, "arbitrary"),
        cost_estimate=cost(0, 6 * size * rows * width),
        name="fold_last",
    )(*((k0, g0, k1, g1) if near_by else far(k0, g0, k1, g1)))


def middle_back_kernel(
    meta_ref, gu_ref, own1_ref, p0, p1, p2, p3, own2_ref, q0, q1, q2, q3, out_own_ref, r0, r1, r2, r3,
    s0, s1, s2, s3, middle_ref, upstream_ref, valid_ref, gains_ref, grad_ref, branch_ref, att_ref,
    acc, first_ref, second_ref, out_ref,
):
    step = pl.program_id(0)
    assemble(meta_ref, first_ref, own1_ref, (p0, p1, p2, p3))
    assemble(meta_ref, second_ref, own2_ref, (q0, q1, q2, q3))
    total = dot_nt(gu_ref[0], first_ref[...]) + dot_nt(gu_ref[1], second_ref[...])

    @pl.when(step == 0)
    def _():
        acc[...] = total
        assemble_two(meta_ref, out_ref, out_own_ref, (r0, r1, r2, r3), (s0, s1, s2, s3))

    @pl.when(step > 0)
    def _():
        acc[...] += total

    @pl.when(step == pl.num_programs(0) - 1)
    def _():
        for top in range(0, acc.shape[0], 128):
            rows = slice(top, top + 128)
            scaled, inverse = normalized(middle_ref[rows, :])
            grad = upstream_ref[rows, :].astype(f32) + norm_back(
                acc[rows, :], gains_ref[1:2, :], scaled, inverse
            )
            grad_ref[rows, :] = grad
            branch = (grad * valid_ref[rows, :]).astype(bf16)
            branch_ref[rows, :] = branch
            att_ref[rows, :] = dot_nt(branch, out_ref[...]).astype(bf16)


def middle_back_call(
    meta, grad_hidden, owns, parts, out_own, middle, upstream, valid, gains, block
):
    rows, width = middle.shape
    slab = owns[0].shape[0]
    hidden = grad_hidden.shape[2]
    steps = hidden // block
    whole = fixed(rows, width)
    own = pl.BlockSpec((slab, block), lambda i: (0, i))
    flat_low = jax.ShapeDtypeStruct((rows, width), bf16)
    return pl.pallas_call(
        middle_back_kernel,
        grid=(hidden // block,),
        in_specs=[SMEM_SPEC, pl.BlockSpec((2, rows, block), lambda i: (0, 0, i)), own]
        + part_specs(parts, block, lambda i: i)
        + [own]
        + part_specs(parts, block, lambda i: i + steps)
        + [once(slab, width)]
        + stretch_specs(parts, 2 * hidden, block)
        + [whole, whole, once(rows, 1), once(8, width)],
        out_specs=[whole, whole, whole],
        out_shape=[pltpu.HBM((rows, width), f32), flat_low, flat_low],
        scratch_shapes=[
            pltpu.VMEM((rows, width), f32),
            pltpu.VMEM((width, block), bf16),
            pltpu.VMEM((width, block), bf16),
            pltpu.VMEM((width, width), bf16),
        ],
        compiler_params=params(38, "arbitrary"),
        cost_estimate=cost(4 * rows * width * hidden, 4 * width * hidden + 4 * rows * hidden + 12 * rows * width),
        name="middle_back",
    )(meta, grad_hidden, *far(owns[0], *parts, owns[1], *parts, out_own, *parts, *parts, middle, upstream), valid, gains)


def input_back_kernel(
    meta_ref, gqkv_ref, own_ref, p0, p1, p2, p3, x_ref, grad_ref, gains_ref, out_ref, acc, whole_ref
):
    step = pl.program_id(0)
    assemble(meta_ref, whole_ref, own_ref, (p0, p1, p2, p3))
    total = dot_nt(gqkv_ref[...], whole_ref[...])

    @pl.when(step == 0)
    def _():
        acc[...] = total

    @pl.when(step > 0)
    def _():
        acc[...] += total

    @pl.when(step == pl.num_programs(0) - 1)
    def _():
        for top in range(0, acc.shape[0], 128):
            rows = slice(top, top + 128)
            scaled, inverse = normalized(x_ref[rows, :].astype(f32))
            out_ref[rows, :] = (
                grad_ref[rows, :] + norm_back(acc[rows, :], gains_ref[0:1, :], scaled, inverse)
            ).astype(bf16)


def input_back_call(meta, grad_joint, own, parts, x, grad_middle, gains):
    rows, width = x.shape
    slab = own.shape[0]
    block = width
    whole = fixed(rows, width)
    return pl.pallas_call(
        input_back_kernel,
        grid=(3 * width // block,),
        in_specs=[
            SMEM_SPEC,
            pl.BlockSpec((rows, block), lambda i: (0, i)),
            pl.BlockSpec((slab, block), lambda i: (0, i)),
        ]
        + part_specs(parts, block, lambda i: i)
        + [whole, whole, once(8, width)],
        out_specs=whole,
        out_shape=jax.ShapeDtypeStruct((rows, width), bf16),
        scratch_shapes=[pltpu.VMEM((rows, width), f32), pltpu.VMEM((width, block), bf16)],
        compiler_params=params(24, "arbitrary"),
        cost_estimate=cost(6 * rows * width * width, 6 * width * width + 14 * rows * width),
        name="input_back",
    )(meta, *far(grad_joint, own, *parts, x, grad_middle), gains)


def rope_tables(positions):
    halfway = HEAD_DIM // 2
    frequency = 10000.0 ** (-(2.0 * jnp.arange(halfway, dtype=f32)) / HEAD_DIM)
    angles = positions.astype(f32)[:, None] * frequency[None, :]
    cosine, sine = jnp.cos(angles), jnp.sin(angles)
    return (
        jnp.concatenate([cosine] * (LANES // halfway), axis=1),
        jnp.concatenate([-sine, sine] * (LANES // HEAD_DIM), axis=1),
    )


def on_device(inputs, cotangent, lengths, norm_first, w_qkv, w_out, norm_second, w_in, w_down):
    seqs, shard_rows, width = inputs.shape
    rows = seqs * shard_rows
    size = lax.axis_size("fsdp")
    me = lax.axis_index("fsdp")
    hidden = w_in.shape[1] // 2
    block = 896
    hidden_pad = -(-hidden // block) * block
    pad = hidden_pad - hidden
    steps = link_orders()
    near, far, middle_way = runs()

    gains = jnp.pad(jnp.stack([norm_first, norm_second], axis=1), ((0, 0), (0, LANES - 2)))
    came_one = turned_before(row_piece([w_qkv, gains]), range(1, size))
    own_in = [jnp.pad(w_in[:, half * hidden :][:, :hidden], ((0, 0), (0, pad))) for half in range(2)]
    piece_two = row_piece([own_in[0], own_in[1], w_out])
    piece_three = column_piece(w_down)
    first_row = me * shard_rows
    query_pos = first_row + jnp.arange(shard_rows, dtype=jnp.int32)
    rim_pos = first_row - WIN + jnp.arange(shard_rows + 2 * WIN, dtype=jnp.int32)
    cosine, sine = rope_tables(rim_pos)
    valid = (query_pos[None, :] < lengths[:, None]).astype(f32).reshape(rows, 1)
    bits = [bit_value(bit) for pair in steps for bit in pair]
    meta = jnp.stack([first_row, me, bit_value(0)] + bits).astype(jnp.int32)
    meta_rows = jnp.concatenate([first_row.astype(jnp.int32)[None], lengths.astype(jnp.int32)])
    x = inputs.reshape(rows, width)
    upstream = cotangent.reshape(rows, width)
    grad_result = (upstream.astype(f32) * valid).astype(bf16)
    grad_give = lax.dynamic_slice_in_dim(grad_result, (1 - bit_value(0)) * (width // 2), width // 2, 1)
    grad_other = flip(grad_give, 0)
    own_rows = slice(WIN, WIN + shard_rows)
    own_cosine, own_sine = cosine[own_rows], sine[own_rows]
    (
        came_one, piece_two, piece_three, own_in, gains, cosine, sine, own_cosine, own_sine, grad_result, grad_other,
        valid,
    ) = after(
        (
            came_one, piece_two, piece_three, own_in, gains, cosine, sine, own_cosine, own_sine, grad_result,
            grad_other, valid,
        )
    )

    one = widen(row_states(came_one), steps[0], 1)
    came_two = turned_before(piece_two, near)
    one, came_two, piece_two = after((one, came_two, piece_two))

    for bits in steps[1:]:
        one = widen(one, bits, 1)
    came_two = came_two + turned_before(piece_two, far)
    one, came_two, piece_two = after((one, came_two, piece_two))

    parts_one = row_parts(one)
    came_two = came_two + turned_before(piece_two, middle_way)
    normed_first, qkv, gains_all = qkv_call(meta, x, w_qkv, parts_one, gains, own_cosine, own_sine)
    by_seq = qkv.reshape(3, seqs, shard_rows, width)[1:]
    edge = (2, seqs * WIN, width)
    edge_up, edge_down = by_seq[:, :, :WIN].reshape(edge), by_seq[:, :, shard_rows - WIN :].reshape(edge)
    qkv, edge_up, edge_down, came_two, piece_three = after((qkv, edge_up, edge_down, came_two, piece_three))

    rim_down, rim_up = neighbours(edge_up, edge_down)
    two = widen(in_turn(row_states, came_two), steps[0], 1)
    rim_down, rim_up, two, piece_three = after((rim_down, rim_up, two, piece_three))

    for bits in steps[1:]:
        two = widen(two, bits, 1)
    came_three = turned_before(piece_three, range(1, size))
    attended, saved = attend_call(meta_rows, qkv, rim_up, rim_down, seqs)
    two, came_three, attended, normed_first = after((two, came_three, attended, normed_first))

    parts_two = row_parts(two)
    three = widen(column_states(came_three), steps[0], 1)
    first_other = flip(half_of(normed_first, False), 0)
    parts_two, three, attended, first_other = after((parts_two, three, attended, first_other))

    for bits in steps[1:]:
        three = widen(three, bits, 1)
    middle, normed_second, attended_split = out_call(
        meta, attended, w_out, parts_two, 2 * hidden_pad, block, x, valid, gains_all
    )
    second_other = flip(half_of(normed_second, False), 0)
    attended_other = flip(half_of(attended_split, False), 0)
    mixed, slope, act = gate_call(meta, normed_second, own_in, parts_two, block)
    three, mixed, slope, act, second_other, attended_other = after(
        (three, mixed, slope, act, second_other, attended_other)
    )

    parts_three = column_parts(three)
    parts_three, mixed, slope, act = after((parts_three, mixed, slope, act))

    mixed_other = flip(mixed, 0)
    grad_hidden, whole_down = gate_back_call(meta, grad_result, w_down, parts_three, slope, act, block)
    grad_hidden, mixed, mixed_other = after((grad_hidden, mixed, mixed_other))

    hidden_other = flip(grad_hidden, 0)
    down = down_call(meta, mixed, mixed_other, grad_result, grad_other, hidden, block)
    down, hidden_other, grad_hidden = after((down, hidden_other, grad_hidden))

    down = swap(down, 0)
    one, two = sum_call(meta, normed_second, second_other, grad_hidden, hidden_other, block)
    down, one, two, grad_hidden = after((down, one, two, grad_hidden))

    one = swap(one, 0)
    for done in range(1, len(steps)):
        down = swap(fold_next(meta, [down], done), done)
    grad_middle, grad_branch, grad_att = middle_back_call(
        meta, grad_hidden, own_in, parts_two, w_out, middle, upstream, valid, gains_all, block
    )
    one, two, grad_branch, grad_att, down = after((one, two, grad_branch, grad_att, down))

    two = swap(two, 0)
    for done in range(1, len(steps)):
        one = swap(fold_next(meta, [one], done), done)
    down_slots = fold_last(down)
    down_came = turned_slots(down_slots, near)
    grad_q, grad_k, grad_v, edge_up, edge_down = attend_back_call(
        qkv, rim_up, rim_down, saved, grad_att, cosine, sine, seqs
    )
    one, two, edge_up, edge_down, grad_q, grad_branch, down_slots, down_came = after(
        (one, two, edge_up, edge_down, grad_q, grad_branch, down_slots, down_came)
    )

    def spread_start(owned):
        ones = (1,) * link_count()
        cut = owned.shape[0] // 2
        return [part.reshape(ones + part.shape) for part in (owned[:cut], owned[cut:])]

    def spread_end(states):
        mine = jnp.stack([state.reshape((-1,) + state.shape[-2:]) for state in states])
        return in_order(mine[None], flip(mine, 0)[None], 0, 0)

    from_next, from_before = neighbours(edge_up, edge_down)
    branch_other = flip(grad_branch, 0)
    two, branch_other = after((two, branch_other))
    for done in range(1, len(steps)):
        two = swap(fold_next(meta, [two], done), done)
    (outs,) = sum_call(meta, attended_split, attended_other, grad_branch[None], branch_other[None], width // 2)
    one_slots = fold_last(one)
    from_next, from_before, two, one_slots, outs = after((from_next, from_before, two, one_slots, outs))

    def with_edges(own, plane):
        own = own.reshape(seqs, shard_rows, width)
        before = from_before[plane].reshape(seqs, WIN, width).astype(f32)
        later = from_next[plane].reshape(seqs, WIN, width).astype(f32)
        rest = ((0, 0), (0, shard_rows - WIN), (0, 0))
        own = own + jnp.pad(before, rest) + jnp.pad(later, (rest[0], rest[1][::-1], rest[2]))
        return own.reshape(rows, width).astype(bf16)

    outs = swap(outs, 0)
    down_came = down_came + turned_slots(down_slots, far) + turned_slots(down_slots, middle_way)
    grad_joint = jnp.concatenate([grad_q, with_edges(grad_k, 0), with_edges(grad_v, 1)], axis=1)
    joint_other = flip(grad_joint, 0)
    (last,) = sum_call(meta, normed_first, first_other, grad_joint[None], joint_other[None], width, True)
    two_slots = fold_last(two)
    last, grad_joint, outs, one_slots, two_slots, down_came, down_slots = after(
        (last, grad_joint, outs, one_slots, two_slots, down_came, down_slots)
    )

    last = swap(last, 0)
    one_came = turned_slots(one_slots, range(1, size))
    grad_inputs = input_back_call(meta, grad_joint, w_qkv, parts_one, x, grad_middle, gains_all)
    last, grad_inputs, one_came, one_slots, two_slots, down_came, down_slots, mixed = after(
        (last, grad_inputs, one_came, one_slots, two_slots, down_came, down_slots, mixed)
    )

    last = [last, outs]
    for done in range(1, len(steps)):
        last = [swap(fold_next(meta, last, done, True), done)]
    two_came = turned_slots(two_slots, range(1, size))
    owned = [slot_sum(one_slots, one_came), slot_sum(down_slots, down_came)]
    result = jnp.dot(mixed, whole_down, preferred_element_type=f32)
    output = (middle + valid * result).astype(bf16)
    last, two_came, two_slots, owned, output = after((last, two_came, two_slots, owned, output))

    last_slots = fold_last(last[0], True)
    last_came = turned_slots(last_slots, near) + turned_slots(last_slots, far)
    spread_in = widen(
        spread_start(jnp.concatenate([owned[0], slot_sum(two_slots, two_came), owned[1]], axis=1)), steps[0], 0
    )
    last_came, spread_in, last_slots = after((last_came, spread_in, last_slots))

    last_came = last_came + turned_slots(last_slots, middle_way)
    for bits in steps[1:]:
        spread_in = widen(spread_in, bits, 0)
    last_came, spread_in, last_slots = after((last_came, spread_in, last_slots))

    spread_last = widen(spread_start(slot_sum(last_slots, last_came)), steps[0], 0)
    in_parts = [state.reshape((-1, state.shape[-1])) for state in spread_in]
    in_parts = in_parts + [flip(part, 0) for part in in_parts]
    spread_last, in_parts = after((spread_last, in_parts))

    for bits in steps[1:]:
        spread_last = widen(spread_last, bits, 0)
    grad_in, grad_second, grad_down = finish_call(meta, in_parts, w_in, hidden_pad, hidden // size, width)
    spread_last, grad_in, grad_second, grad_down = after((spread_last, grad_in, grad_second, grad_down))

    grad_second = grad_second.reshape(-1) / norm_second.astype(f32)
    grad_last = spread_end(spread_last)
    grad_last = grad_last.reshape(-1, grad_last.shape[-1])
    grad_qkv = grad_last[:, : 3 * width].astype(f32)
    grad_out = grad_last[:, 3 * width :].astype(f32)
    grad_first = jnp.sum(grad_qkv * w_qkv.astype(f32), axis=1) / norm_first.astype(f32)
    return (
        output.reshape(inputs.shape),
        grad_inputs.reshape(inputs.shape),
        grad_first,
        grad_qkv,
        grad_out,
        grad_second,
        grad_in,
        grad_down,
    )


def solution(mesh):
    in_specs = (
        P("rep", "fsdp", None),
        P("rep", "fsdp", None),
        P("rep"),
        P("fsdp"),
        P("fsdp", None),
        P("fsdp", None),
        P("fsdp"),
        P("fsdp", None),
        P("fsdp", None),
    )
    out_specs = (
        P("rep", "fsdp", None),
        P("rep", "fsdp", None),
        P("fsdp"),
        P("fsdp", None),
        P("fsdp", None),
        P("fsdp"),
        P("fsdp", None),
        P("fsdp", None),
    )
    return jax.shard_map(
        on_device, mesh=mesh, in_specs=in_specs, out_specs=out_specs, check_vma=False
    )
```

```python
import functools

import jax
import jax.numpy as jnp
from jax import lax
from jax.experimental import pallas as pl
from jax.experimental.pallas import tpu as pltpu
from jax.sharding import PartitionSpec as P

HEAD_DIM = 64
WIN = 64
BLOCK_Q = 128
LANES = 128

epsilon = 1e-05
root_half = 0.7071067811865476
inv_root_two_pi = 0.3989422804014327
f32 = jnp.float32
bf16 = jnp.bfloat16
COST_SCALE = 1.0


def after(value, *before):
    return lax.optimization_barrier((value, before))[0]


def bit_count():
    return lax.axis_size("rep").bit_length() - 1


def bit_value(bit):
    return (lax.axis_index("rep") >> bit) & 1


def link_count():
    return bit_count() - 1


def link_axis(bit):
    return bit_count() - 1 - bit


def flip(value, bit):
    size = lax.axis_size("rep")
    return lax.ppermute(value, "rep", [(i, i ^ (1 << bit)) for i in range(size)])


def turn(value, steps):
    size = lax.axis_size("fsdp")
    return lax.ppermute(value, "fsdp", [(i, (i + steps) % size) for i in range(size)])


def link_orders():
    bits = list(range(1, bit_count()))
    return list(zip(bits, bits[::-1]))


def in_order(mine, got, bit, axis):
    first = bit_value(bit) == 0
    return jnp.concatenate([jnp.where(first, mine, got), jnp.where(first, got, mine)], axis=axis)


def widen(states, bits, lead):
    return [
        in_order(state, flip(state, bit), bit, lead + link_axis(bit)) for state, bit in zip(states, bits)
    ]


def row_piece(shards):
    width = sum(shard.shape[1] for shard in shards)
    links = 1 << link_count()
    core, link = bit_value(0), lax.axis_index("rep") >> 1
    views = [shard.reshape(2, 2, links, -1, shard.shape[1]) for shard in shards]
    rows = views[0].shape[3]
    pieces = [
        lax.dynamic_slice(view, (core, 0, link, 0, 0), (1, 2, 1, rows, view.shape[4])) for view in views
    ]
    return jnp.concatenate(pieces, axis=-1).reshape(2, rows, width)


def row_states(came):
    ones = (1,) * link_count()
    return [
        jnp.stack([piece[part] for piece in came]).reshape((len(came),) + ones + came[0].shape[1:])
        for part in range(2)
    ]


def row_parts(states):
    mine = [state.reshape(state.shape[0], -1, state.shape[-1]) for state in states]
    return mine + [flip(state, 0) for state in mine]


def half_rows(rows):
    return -(-rows // 2 // 16) * 16


def column_piece(shard):
    columns = shard.shape[1] // lax.axis_size("rep")
    place = (bit_value(0) << link_count()) + (lax.axis_index("rep") >> 1)
    return lax.dynamic_slice_in_dim(shard, place * columns, columns, 1)


def column_states(came):
    cut = half_rows(came[0].shape[0])
    ones = (1,) * link_count()
    stacked = jnp.stack(came)
    return [
        part.reshape(part.shape[:1] + ones + part.shape[1:]) for part in (stacked[:, :cut], stacked[:, cut:])
    ]


def column_parts(states):
    mine = [state.reshape((state.shape[0], -1) + state.shape[-2:]) for state in states]
    return mine + [flip(state, 0) for state in mine]


def whole_columns(shard, parts, pad_rows):
    size = lax.axis_size("fsdp")
    me = lax.axis_index("fsdp")
    rows, width = shard.shape
    mine, got = [jnp.concatenate(pair, axis=2) for pair in (parts[:2], parts[2:])]
    joined = in_order(mine, got, 0, 1)
    joined = jnp.transpose(joined, (0, 2, 1, 3)).reshape(size - 1, rows, width)
    whole = jnp.zeros((size * rows + pad_rows, width), shard.dtype)
    whole = lax.dynamic_update_slice(whole, shard, (me * rows, 0))
    for steps in range(1, size):
        source = lax.rem(me - steps + size, size)
        whole = lax.dynamic_update_slice(whole, joined[steps - 1], (source * rows, 0))
    return whole


def turned_before(piece, steps):
    return [turn(piece, step) for step in steps]


def runs():
    size = lax.axis_size("fsdp")
    order = sorted(range(1, size), key=lambda step: (min(step, size - step), step))
    cuts = [(size - 1) * part // 3 for part in range(4)]
    return [order[first:last] for first, last in zip(cuts, cuts[1:])]


def in_turn(states, came):
    order = [step for run in runs() for step in run]
    return states([came[order.index(step)] for step in range(1, lax.axis_size("fsdp"))])


def tokens_dot(left, right):
    return lax.dot_general(left, right, (((0,), (0,)), ((), ())), preferred_element_type=f32)


def half_of(split, mine):
    index = bit_value(0) if mine else 1 - bit_value(0)
    return lax.dynamic_index_in_dim(split, index, 0, False)


def turned_slots(slots, steps):
    size = lax.axis_size("fsdp")
    me = lax.axis_index("fsdp")
    return [
        turn(lax.dynamic_index_in_dim(slots, lax.rem(me + step, size), 0, False), step) for step in steps
    ]


def slot_sum(slots, came):
    total = lax.dynamic_index_in_dim(slots, lax.axis_index("fsdp"), 0, False).astype(f32)
    for part in came:
        total = total + part.astype(f32)
    return total.astype(bf16)


def bits_left(done):
    orders = zip(*link_orders())
    return [sorted(order[done:]) for order in orders]


def split_index(number, place):
    low = number & ((1 << place) - 1)
    return ((number >> place) << (place + 1)) | low


def halves(state, done, part):
    bit = link_orders()[done][part]
    place = bits_left(done)[part].index(bit)
    size, links = state.shape[:2]
    view = state.reshape((size, links >> (place + 1), 2, 1 << place) + state.shape[2:])
    shape = (size, links // 2) + state.shape[2:]
    keep, give = [
        lax.dynamic_index_in_dim(view, index, 2, False).reshape(shape)
        for index in (bit_value(bit), 1 - bit_value(bit))
    ]
    return keep, give


def swap(parts, done):
    return [(keep, flip(give, bit)) for (keep, give), bit in zip(parts, link_orders()[done])]


def added(keep, got):
    return (keep.astype(f32) + got.astype(f32)).astype(bf16)


def neighbours(up, down):
    size = lax.axis_size("fsdp")
    forward = [(i, i + 1) for i in range(size - 1)]
    backward = [(i + 1, i) for i in range(size - 1)]
    return lax.ppermute(up, "fsdp", backward), lax.ppermute(down, "fsdp", forward)


def params(megabytes, *semantics):
    return pltpu.CompilerParams(dimension_semantics=semantics, vmem_limit_bytes=megabytes << 20)


def cost(flops, nbytes):
    return pl.CostEstimate(flops=int(flops * COST_SCALE), bytes_accessed=int(nbytes * COST_SCALE), transcendentals=0)


def far(*arrays):
    return [pltpu.with_memory_space_constraint(array, pltpu.HBM) for array in arrays]


def dot_nn(left, right):
    return jnp.dot(left, right, preferred_element_type=f32)


def dot_nt(left, right):
    return lax.dot_general(left, right, (((1,), (1,)), ((), ())), preferred_element_type=f32)


def normalized(values):
    centred = values - jnp.mean(values, axis=-1, keepdims=True)
    inverse = lax.rsqrt(jnp.mean(centred * centred, axis=-1, keepdims=True) + epsilon)
    return centred * inverse, inverse


def norm_back(grad_out, gain, scaled, inverse):
    grad_scaled = grad_out * gain
    return inverse * (
        grad_scaled
        - jnp.mean(grad_scaled, axis=-1, keepdims=True)
        - scaled * jnp.mean(grad_scaled * scaled, axis=-1, keepdims=True)
    )


def swapped_halves(values):
    width = values.shape[-1]
    lane = lax.broadcasted_iota(jnp.int32, values.shape, values.ndim - 1)
    ahead = pltpu.roll(values, width - HEAD_DIM // 2, values.ndim - 1)
    behind = pltpu.roll(values, HEAD_DIM // 2, values.ndim - 1)
    return jnp.where(lane % HEAD_DIM < HEAD_DIM // 2, ahead, behind)


def assemble(meta_ref, whole_ref, own_ref, part_refs):
    rows = own_ref.shape[0]
    count, quarter = part_refs[0].shape[:2]
    size = count + 1
    me, core = meta_ref[1], meta_ref[2]
    whole_ref[pl.ds(pl.multiple_of(me * rows, quarter), rows), :] = own_ref[...]
    for steps in range(1, size):
        base = lax.rem(me - steps + size, size) * rows
        for number, part_ref in enumerate(part_refs):
            half = core if number < 2 else 1 - core
            start = base + half * (rows // 2) + (number % 2) * quarter
            whole_ref[pl.ds(pl.multiple_of(start, quarter), quarter), :] = part_ref[steps - 1]


def split_columns(values, split_ref, rows, size):
    half = values.shape[1] // size // 2
    for place in range(size):
        for core in range(2):
            start = (2 * place + core) * half
            split_ref[core, rows, place * half : (place + 1) * half] = values[:, start : start + half]


def joined_columns(split_ref, rows, size):
    half = split_ref.shape[2] // size
    return jnp.concatenate(
        [
            split_ref[core, rows, place * half : (place + 1) * half]
            for place in range(size)
            for core in range(2)
        ],
        axis=1,
    )


def assemble_two(meta_ref, whole_ref, own_ref, wide_refs, narrow_refs):
    cut = wide_refs[0].shape[2]
    assemble(meta_ref, whole_ref.at[:, :cut], own_ref.at[:, :cut], wide_refs)
    assemble(meta_ref, whole_ref.at[:, cut:], own_ref.at[:, cut:], narrow_refs)


def stretch_specs(parts, start, block):
    rest = parts[0].shape[2] - start - block
    wide = part_specs(parts, block, lambda i: start // block)
    return wide + part_specs(parts, rest, lambda i: (start + block) // rest)


def part_specs(parts, block, place):
    count, quarter, _ = parts[0].shape
    return [pl.BlockSpec((count, quarter, block), lambda i: (0, 0, place(i)))] * 4


def qkv_kernel(
    meta_ref, x_ref, own_ref, p0, p1, p2, p3, gain_ref, g0, g1, g2, g3, cos_ref, sin_ref,
    split_ref, out_ref, gains_ref, whole_ref, normed_ref, column_ref, *, rope_steps, size,
):
    step = pl.program_id(0)

    @pl.when(step == 0)
    def _():
        assemble(meta_ref, column_ref, gain_ref, (g0, g1, g2, g3))
        row = lax.broadcasted_iota(jnp.int32, gains_ref.shape[:1] + (LANES,), 0)
        lane = lax.broadcasted_iota(jnp.int32, gains_ref.shape[:1] + (LANES,), 1)
        gains_ref[...] = dot_nt((row == lane).astype(f32).astype(bf16), column_ref[...])
        for top in range(0, x_ref.shape[0], 128):
            rows = slice(top, top + 128)
            scaled, _inverse = normalized(x_ref[rows, :].astype(f32))
            normed = (scaled * gains_ref[0:1, :]).astype(bf16)
            normed_ref[rows, :] = normed
            split_columns(normed, split_ref, rows, size)

    assemble(meta_ref, whole_ref, own_ref, (p0, p1, p2, p3))
    product = dot_nn(normed_ref[...], whole_ref[...])

    @pl.when(step >= rope_steps)
    def _():
        out_ref[0] = product.astype(bf16)

    @pl.when(step < rope_steps)
    def _():
        seq_rows = cos_ref.shape[0]
        cosine, sine = cos_ref[...], sin_ref[...]
        for top in range(0, product.shape[0], seq_rows):
            for lane in range(0, product.shape[1], LANES):
                tile = product[top : top + seq_rows, lane : lane + LANES]
                out_ref[0, top : top + seq_rows, lane : lane + LANES] = (
                    tile * cosine + swapped_halves(tile) * sine
                ).astype(bf16)


SMEM_SPEC = pl.BlockSpec(memory_space=pltpu.SMEM)


def fixed(*shape):
    return pl.BlockSpec(shape, lambda i: (0,) * len(shape))


def once(*shape):
    return pl.BlockSpec(shape, lambda i: (0,) * len(shape), pipeline_mode=pl.Buffered(1))


def qkv_call(meta, x, own, parts, own_gains, cosine, sine):
    rows, width = x.shape
    slab = own.shape[0]
    size = width // slab
    block = 512
    per_plane = width // block
    return pl.pallas_call(
        functools.partial(qkv_kernel, rope_steps=2 * per_plane, size=size),
        grid=(3 * per_plane,),
        in_specs=[SMEM_SPEC, once(rows, width), pl.BlockSpec((slab, block), lambda i: (0, i))]
        + part_specs(parts, block, lambda i: i)
        + [once(slab, LANES)]
        + part_specs(parts, LANES, lambda i: 3 * width // LANES)
        + [once(*cosine.shape), once(*sine.shape)],
        out_specs=[
            fixed(2, rows, width // 2),
            pl.BlockSpec((1, rows, block), lambda i: (i // per_plane, 0, i % per_plane)),
            fixed(8, width),
        ],
        out_shape=[
            jax.ShapeDtypeStruct((2, rows, width // 2), bf16),
            jax.ShapeDtypeStruct((3, rows, width), bf16),
            jax.ShapeDtypeStruct((8, width), f32),
        ],
        scratch_shapes=[
            pltpu.VMEM((width, block), bf16),
            pltpu.VMEM((rows, width), bf16),
            pltpu.VMEM((width, LANES), bf16),
        ],
        compiler_params=params(20, "arbitrary"),
        cost_estimate=cost(6 * rows * width * width, 6 * width * width + 10 * rows * width),
        name="qkv",
    )(meta, *far(x, own, *parts), own_gains, *far(*parts), cosine, sine)


def head_masks():
    lane = lax.broadcasted_iota(jnp.int32, (1, LANES), 1)
    first = lane < HEAD_DIM
    return first, first.astype(f32).astype(bf16), (~first).astype(f32).astype(bf16)


def two_heads(tile, low_mask, high_mask):
    return jnp.concatenate([tile * low_mask, tile * high_mask], axis=0)


def score_bias(first_row, length):
    shape = (BLOCK_Q + 2 * WIN, BLOCK_Q)
    key = first_row - WIN + lax.broadcasted_iota(jnp.int32, shape, 0)
    query = first_row + lax.broadcasted_iota(jnp.int32, shape, 1)
    near = jnp.abs(query - key) <= WIN
    live = (key >= 0) & (key < length)
    bias = jnp.where(near & (live | (query == key)), 0.0, -1e30).astype(f32)
    return jnp.concatenate([bias, bias], axis=1)


def softmax_of(queries, keys, bias):
    scores = dot_nt(keys, queries) * (HEAD_DIM**-0.5) + bias
    exponent = jnp.exp(scores - jnp.max(scores, axis=0, keepdims=True))
    return exponent / jnp.sum(exponent, axis=0, keepdims=True)


def attend_kernel(
    meta_ref, q_ref, k_ref, v_ref, k_up_ref, v_up_ref, k_down_ref, v_down_ref, out_ref, probs_ref
):
    length = meta_ref[1 + pl.program_id(0)]
    rows, width = q_ref.shape[1:]
    first_head, low_mask, high_mask = head_masks()
    for lane in range(0, width, LANES):
        lanes = slice(lane, lane + LANES)
        keys = jnp.concatenate([k_up_ref[0, :, lanes], k_ref[0, :, lanes], k_down_ref[0, :, lanes]], 0)
        values = jnp.concatenate([v_up_ref[0, :, lanes], v_ref[0, :, lanes], v_down_ref[0, :, lanes]], 0)
        for top in range(0, rows, BLOCK_Q):
            bias = score_bias(meta_ref[0] + top, length)
            span = slice(top, top + BLOCK_Q + 2 * WIN)
            queries = two_heads(q_ref[0, top : top + BLOCK_Q, lanes], low_mask, high_mask)
            probs = softmax_of(queries, keys[span], bias).astype(bf16)
            probs_ref[0, lane // LANES, top // BLOCK_Q] = probs
            result = tokens_dot(probs, values[span])
            out_ref[top : top + BLOCK_Q, lanes] = jnp.where(
                first_head, result[:BLOCK_Q], result[BLOCK_Q:]
            ).astype(bf16)


def attention_specs(seqs, seq_rows, width, block):
    own = lambda plane: pl.BlockSpec((1, seq_rows, block), lambda s, h: (plane, s, h))
    rim = lambda plane: pl.BlockSpec((1, WIN, block), lambda s, h: (plane, s, h))
    flat = pl.BlockSpec((seq_rows, block), lambda s, h: (s, h))
    inner = (seq_rows // BLOCK_Q, BLOCK_Q + 2 * WIN, 2 * BLOCK_Q)
    probs = pl.BlockSpec((1, block // LANES) + inner, lambda s, h: (s, h, 0, 0, 0))
    probs_shape = pltpu.HBM((seqs, width // LANES) + inner, bf16)
    return own, rim, flat, probs, probs_shape


def attend_call(meta, qkv, rim_up, rim_down, seqs):
    _, rows, width = qkv.shape
    seq_rows = rows // seqs
    block = 256
    own, rim, flat, probs, probs_shape = attention_specs(seqs, seq_rows, width, block)
    return pl.pallas_call(
        attend_kernel,
        grid=(seqs, width // block),
        in_specs=[SMEM_SPEC, own(0), own(1), own(2), rim(0), rim(1), rim(0), rim(1)],
        out_specs=[flat, probs],
        out_shape=[jax.ShapeDtypeStruct((rows, width), bf16), probs_shape],
        compiler_params=params(16, "arbitrary", "arbitrary"),
        cost_estimate=cost(8 * rows * width * (BLOCK_Q + 2 * WIN), 10 * rows * width),
        name="attend",
    )(meta, qkv, qkv, qkv, rim_up, rim_up, rim_down, rim_down)


def attend_back_kernel(
    q_ref,
    k_ref,
    v_ref,
    k_up_ref,
    v_up_ref,
    k_down_ref,
    v_down_ref,
    probs_ref,
    go_ref,
    cos_ref,
    sin_ref,
    gq_ref,
    gk_ref,
    gv_ref,
    up_ref,
    down_ref,
):
    rows, width = q_ref.shape[1:]
    scale = HEAD_DIM**-0.5
    first_head, low_mask, high_mask = head_masks()

    def turned_back(tile, span):
        return tile * cos_ref[span, :] - swapped_halves(tile) * sin_ref[span, :]

    for lane in range(0, width, LANES):
        lanes = slice(lane, lane + LANES)
        keys = jnp.concatenate([k_up_ref[0, :, lanes], k_ref[0, :, lanes], k_down_ref[0, :, lanes]], 0)
        values = jnp.concatenate([v_up_ref[0, :, lanes], v_ref[0, :, lanes], v_down_ref[0, :, lanes]], 0)
        key_parts, value_parts = [], []
        for top in range(0, rows, BLOCK_Q):
            span = slice(top, top + BLOCK_Q + 2 * WIN)
            queries = two_heads(q_ref[0, top : top + BLOCK_Q, lanes], low_mask, high_mask)
            grads = two_heads(go_ref[top : top + BLOCK_Q, lanes], low_mask, high_mask)
            probs_low = probs_ref[0, lane // LANES, top // BLOCK_Q]
            probs = probs_low.astype(f32)
            grad_probs = dot_nt(values[span], grads)
            delta = jnp.sum(probs * grad_probs, axis=0, keepdims=True)
            grad_scores = (probs * (grad_probs - delta)).astype(bf16)
            result = tokens_dot(grad_scores, keys[span])
            result = jnp.where(first_head, result[:BLOCK_Q], result[BLOCK_Q:]) * scale
            own = slice(WIN + top, WIN + top + BLOCK_Q)
            gq_ref[top : top + BLOCK_Q, lanes] = turned_back(result, own).astype(bf16)
            key_parts.append(dot_nn(grad_scores, queries))
            value_parts.append(dot_nn(probs_low, grads))

        def laid_out(parts):
            pieces = [parts[0][:BLOCK_Q]]
            for before, part in zip(parts, parts[1:]):
                pieces.append(before[BLOCK_Q:] + part[:BLOCK_Q])
            return jnp.concatenate(pieces + [parts[-1][BLOCK_Q:]], axis=0)

        grad_keys = turned_back(laid_out(key_parts) * scale, slice(None))
        grad_values = laid_out(value_parts)
        up_ref[0, :, lanes] = grad_keys[:WIN].astype(bf16)
        up_ref[1, :, lanes] = grad_values[:WIN].astype(bf16)
        down_ref[0, :, lanes] = grad_keys[WIN + rows :].astype(bf16)
        down_ref[1, :, lanes] = grad_values[WIN + rows :].astype(bf16)
        gk_ref[:, lanes] = grad_keys[WIN : WIN + rows]
        gv_ref[:, lanes] = grad_values[WIN : WIN + rows]


def attend_back_call(qkv, rim_up, rim_down, saved, grad_out, cosine, sine, seqs):
    _, rows, width = qkv.shape
    seq_rows = rows // seqs
    block = 256
    own, rim, flat, probs, probs_shape = attention_specs(seqs, seq_rows, width, block)
    table = pl.BlockSpec(cosine.shape, lambda s, h: (0, 0))
    edge = pl.BlockSpec((2, WIN, block), lambda s, h: (0, s, h))
    edge_shape = jax.ShapeDtypeStruct((2, seqs * WIN, width), bf16)
    return pl.pallas_call(
        attend_back_kernel,
        grid=(seqs, width // block),
        in_specs=[
            own(0), own(1), own(2), rim(0), rim(1), rim(0), rim(1),
            probs, flat, table, table,
        ],
        out_specs=[flat, flat, flat, edge, edge],
        out_shape=[
            jax.ShapeDtypeStruct((rows, width), bf16),
            jax.ShapeDtypeStruct((rows, width), f32),
            jax.ShapeDtypeStruct((rows, width), f32),
            edge_shape,
            edge_shape,
        ],
        compiler_params=params(16, "arbitrary", "arbitrary"),
        cost_estimate=cost(20 * rows * width * (BLOCK_Q + 2 * WIN), 20 * rows * width),
        name="attend_back",
    )(qkv, qkv, qkv, rim_up, rim_up, rim_down, rim_down, *far(saved), grad_out, cosine, sine)


def out_kernel(
    meta_ref, o_ref, own_ref, p0, p1, p2, p3, q0, q1, q2, q3, x_ref, valid_ref, gains_ref,
    middle_ref, n_split_ref, o_split_ref, whole_ref, *, size,
):
    @pl.when(pl.program_id(0) == 0)
    def _():
        assemble_two(meta_ref, whole_ref, own_ref, (p0, p1, p2, p3), (q0, q1, q2, q3))

    values = o_ref[...]
    split_columns(values, o_split_ref, slice(None), size)
    middle = x_ref[...].astype(f32) + valid_ref[...] * dot_nn(values, whole_ref[...])
    middle_ref[...] = middle
    scaled, _inverse = normalized(middle)
    split_columns((scaled * gains_ref[1:2, :]).astype(bf16), n_split_ref, slice(None), size)


def out_call(meta, attended, own, parts, start, stretch, x, valid, gains):
    rows, width = x.shape
    slab = own.shape[0]
    size = width // slab
    block = 128
    tile = pl.BlockSpec((block, width), lambda i: (i, 0))
    split = pl.BlockSpec((2, block, width // 2), lambda i: (0, i, 0))
    split_shape = jax.ShapeDtypeStruct((2, rows, width // 2), bf16)
    return pl.pallas_call(
        functools.partial(out_kernel, size=size),
        grid=(rows // block,),
        in_specs=[SMEM_SPEC, tile, once(slab, width)]
        + stretch_specs(parts, start, stretch)
        + [tile, pl.BlockSpec((block, 1), lambda i: (i, 0)), once(8, width)],
        out_specs=[tile, split, split],
        out_shape=[pltpu.HBM((rows, width), f32), split_shape, split_shape],
        scratch_shapes=[pltpu.VMEM((width, width), bf16)],
        compiler_params=params(16, "arbitrary"),
        cost_estimate=cost(2 * rows * width * width, 2 * width * width + 12 * rows * width),
        name="out_norm",
    )(meta, attended, *far(own, *parts, *parts, x), valid, gains)


def gate_kernel(
    meta_ref, n_ref, own1_ref, p0, p1, p2, p3, own2_ref, q0, q1, q2, q3,
    mixed_ref, slope_ref, act_ref, normed_ref, first_ref, second_ref, *, size,
):
    @pl.when(pl.program_id(0) == 0)
    def _():
        for top in range(0, normed_ref.shape[0], 128):
            rows = slice(top, top + 128)
            normed_ref[rows, :] = joined_columns(n_ref, rows, size)

    assemble(meta_ref, first_ref, own1_ref, (p0, p1, p2, p3))
    assemble(meta_ref, second_ref, own2_ref, (q0, q1, q2, q3))
    gate_in = dot_nn(normed_ref[...], first_ref[...])
    gate_up = dot_nn(normed_ref[...], second_ref[...])
    normal_cdf = 0.5 * (1.0 + lax.erf(gate_in * root_half))
    density = jnp.exp(-0.5 * gate_in * gate_in) * inv_root_two_pi
    activated = gate_in * normal_cdf
    mixed_ref[...] = (activated * gate_up).astype(bf16)
    slope_ref[...] = (gate_up * (normal_cdf + gate_in * density)).astype(bf16)
    act_ref[...] = activated.astype(bf16)


def gate_call(meta, normed, owns, parts, block):
    _, rows, half = normed.shape
    width = 2 * half
    slab, hidden = owns[0].shape
    steps = hidden // block
    size = width // slab
    tile = pl.BlockSpec((rows, block), lambda i: (0, i))
    own = pl.BlockSpec((slab, block), lambda i: (0, i))
    return pl.pallas_call(
        functools.partial(gate_kernel, size=size),
        grid=(hidden // block,),
        in_specs=[SMEM_SPEC, once(2, rows, half), own]
        + part_specs(parts, block, lambda i: i)
        + [own]
        + part_specs(parts, block, lambda i: i + steps),
        out_specs=[tile, tile, tile],
        out_shape=[pltpu.HBM((rows, hidden), bf16)] * 3,
        scratch_shapes=[
            pltpu.VMEM((rows, width), bf16),
            pltpu.VMEM((width, block), bf16),
            pltpu.VMEM((width, block), bf16),
        ],
        compiler_params=params(32, "arbitrary"),
        cost_estimate=cost(4 * rows * width * hidden, 4 * width * hidden + 6 * rows * hidden),
        name="gate",
    )(meta, normed, *far(owns[0], *parts, owns[1], *parts))


def gate_back_kernel(
    meta_ref, g_ref, own_ref, p0, p1, p2, p3, slope_ref, act_ref, out_ref, whole_ref, *, block
):
    step = pl.program_id(0)

    @pl.when(step == 0)
    def _():
        rows = own_ref.shape[0]
        count, links, cut, columns = p0.shape
        size = count + 1
        me, core = meta_ref[1], meta_ref[2]
        whole_ref[size * rows :, :] = jnp.zeros_like(whole_ref[size * rows :, :])
        whole_ref[pl.ds(pl.multiple_of(me * rows, 16), rows), :] = own_ref[...]

        def put(halves):
            for steps in range(1, size):
                base = lax.rem(me - steps + size, size) * rows
                for half, parts in enumerate(halves):
                    for part, start in zip(parts, (0, cut)):
                        target = pl.ds(pl.multiple_of(base + start, 16), part.shape[2])
                        for link in range(links):
                            lane = (half * links + link) * columns
                            whole_ref[target, lane : lane + columns] = part[steps - 1, link]

        @pl.when(core == 0)
        def _():
            put(((p0, p1), (p2, p3)))

        @pl.when(core == 1)
        def _():
            put(((p2, p3), (p0, p1)))

    weight = whole_ref[pl.ds(pl.multiple_of(step * block, block), block), :]
    grad_mixed = dot_nt(g_ref[...], weight)
    out_ref[0] = (grad_mixed * slope_ref[...].astype(f32)).astype(bf16)
    out_ref[1] = (grad_mixed * act_ref[...].astype(f32)).astype(bf16)


def gate_back_plain_kernel(g_ref, w_ref, slope_ref, act_ref, out_ref):
    grad_mixed = dot_nt(g_ref[...], w_ref[...])
    out_ref[0] = (grad_mixed * slope_ref[...].astype(f32)).astype(bf16)
    out_ref[1] = (grad_mixed * act_ref[...].astype(f32)).astype(bf16)


def gate_back_call(meta, grad_result, own, parts, slope, act, block):
    rows, width = grad_result.shape
    hidden = slope.shape[1]
    tile = pl.BlockSpec((rows, block), lambda i: (0, i))
    out_spec = pl.BlockSpec((2, rows, block), lambda i: (0, 0, i))
    out_shape = jax.ShapeDtypeStruct((2, rows, hidden), bf16)
    settings = dict(
        grid=(hidden // block,),
        compiler_params=params(28, "arbitrary"),
        cost_estimate=cost(2 * rows * width * hidden, 4 * width * hidden + 8 * rows * hidden),
        name="gate_back",
    )
    if own.shape[0] % 16:
        whole = whole_columns(own, parts, hidden - own.shape[0] * (parts[0].shape[0] + 1))
        out = pl.pallas_call(
            gate_back_plain_kernel,
            in_specs=[once(rows, width), pl.BlockSpec((block, width), lambda i: (i, 0)), tile, tile],
            out_specs=out_spec,
            out_shape=out_shape,
            **settings,
        )(grad_result, whole, slope, act)
        return out, whole
    return pl.pallas_call(
        functools.partial(gate_back_kernel, block=block),
        in_specs=[SMEM_SPEC, once(rows, width), once(*own.shape)]
        + [once(*part.shape) for part in parts]
        + [tile, tile],
        out_specs=[out_spec, fixed(hidden, width)],
        out_shape=[out_shape, jax.ShapeDtypeStruct((hidden, width), bf16)],
        **settings,
    )(meta, *far(grad_result, own, *parts, slope, act))


def down_kernel(
    meta_ref, m_ref, n_ref, g_ref, h_ref, keep0, give0, keep1, give1, state_ref, *, hidden, places
):
    step = pl.program_id(0)
    block, half = m_ref.shape[1], h_ref.shape[1]
    size, links, rows, columns = state_ref.shape
    right = g_ref[:, pl.ds(pl.multiple_of(meta_ref[2] * half, half), half)]
    sums = tokens_dot(m_ref[...], right) + tokens_dot(n_ref[...], h_ref[...])

    def put(first):
        for place in range(size):
            top, end = max(place * rows, first), min((place + 1) * rows, first + block)
            if top >= end:
                continue
            for link in range(links):
                value = sums[top - first : end - first, link * columns : (link + 1) * columns]
                state_ref[place, link, top - place * rows : end - place * rows, :] = value.astype(bf16)

    for number in range(-(-hidden // block)):
        pl.when(step == number)(functools.partial(put, number * block))

    @pl.when(step == pl.num_programs(0) - 1)
    def _():
        height, width = keep0.shape[2:]
        tiles = rows // height
        for part, (keep_ref, give_ref) in enumerate(((keep0, give0), (keep1, give1))):
            own = meta_ref[3 + part]
            span = range(part * (width // columns), min((part + 1) * (width // columns), tiles))
            for place in range(size):
                for number in range(links // 2):
                    base = split_index(number, places[part])
                    for ref, value in ((keep_ref, own), (give_ref, 1 - own)):
                        link = base + value * (1 << places[part])
                        for lane, tile in enumerate(span):
                            ref[place, number, :, lane * columns : (lane + 1) * columns] = state_ref[
                                place, link, tile * height : (tile + 1) * height, :
                            ]
                        if len(span) * columns < width:
                            ref[place, number, :, len(span) * columns :] = jnp.zeros(
                                (height, width - len(span) * columns), bf16
                            )


def first_places():
    return [left.index(bit) for left, bit in zip(bits_left(0), link_orders()[0])]


def piece_rows(width):
    return width // lax.axis_size("fsdp") // (4 << link_count())


def fits(shard, columns, height):
    return shard % 16 == 0 and columns == LANES and height == 16


def down_call(meta, mixed, mixed_other, grad_result, grad_other, hidden, block):
    rows, hidden_pad = mixed.shape
    width = grad_result.shape[1]
    size = lax.axis_size("fsdp")
    links = 1 << link_count()
    shard, columns, height = hidden // size, width // 2 // links, piece_rows(width)
    if not fits(shard, columns, height):
        own = lax.dynamic_slice_in_dim(grad_result, bit_value(0) * (width // 2), width // 2, 1)
        sums = tokens_dot(mixed, own) + tokens_dot(mixed_other, grad_other)
        state = sums[:hidden].astype(bf16).reshape(size, shard, links, columns)
        state = jnp.moveaxis(state, 2, 1).reshape(size, links, 2, height, -1)
        return [halves(state[:, :, part], 0, part) for part in range(2)]
    tiles = -(-shard // height // 2)
    shape = (size, links // 2, height, tiles * columns)
    out = pl.pallas_call(
        functools.partial(down_kernel, hidden=hidden, places=first_places()),
        grid=(hidden_pad // block,),
        in_specs=[SMEM_SPEC]
        + [pl.BlockSpec((rows, block), lambda i: (0, i))] * 2
        + [once(rows, width), once(rows, width // 2)],
        out_specs=[fixed(*shape)] * 4,
        out_shape=[pltpu.HBM(shape, bf16)] * 4,
        scratch_shapes=[pltpu.VMEM((size, links, shard, columns), bf16)],
        compiler_params=params(24, "arbitrary"),
        cost_estimate=cost(2 * rows * width * hidden, width * hidden + 4 * rows * (hidden + width)),
        name="down_sum",
    )(meta, *far(mixed), mixed_other, *far(grad_result), grad_other)
    return [(out[0], out[1]), (out[2], out[3])]


def sum_kernel(meta_ref, left_ref, left_other_ref, right_ref, right_other_ref, *rest, size, links, places, steps):
    state_ref = rest[-1]
    state_ref[...] = (
        tokens_dot(left_ref[meta_ref[2]], right_ref[0]) + tokens_dot(left_other_ref[...], right_other_ref[0])
    ).astype(bf16)
    rows = state_ref.shape[0] // (2 * size * links)

    def put(outs):
        for part in range(2):
            own = meta_ref[3 + part]
            for place in range(size):
                for number in range(links // 2):
                    base = (2 * place + part) * links + split_index(number, places[part])
                    for ref, value in ((outs[2 * part], own), (outs[2 * part + 1], 1 - own)):
                        start = (base + value * (1 << places[part])) * rows
                        ref[place, number] = state_ref[pl.ds(pl.multiple_of(start, rows), rows), :]

    planes = (len(rest) - 1) // 4
    for plane in range(planes):
        pl.when(pl.program_id(0) // steps == plane)(functools.partial(put, rest[4 * plane : 4 * plane + 4]))


def sum_call(meta, left, left_other, right, right_other, block, outside=False):
    _, tokens, height = left.shape
    planes, _, width = right.shape
    size = lax.axis_size("fsdp")
    links = 1 << link_count()
    rows = height // (2 * size * links)
    steps = width // block
    if rows % 16:
        result = []
        for plane in range(planes):
            state = tokens_dot(half_of(left, True), right[plane]) + tokens_dot(left_other, right_other[plane])
            state = state.astype(bf16).reshape(size, 2, links, rows, width)
            result.append([halves(state[:, part], 0, part) for part in range(2)])
        return result
    shape = (size, links // 2, rows, width)
    right_spec = pl.BlockSpec((1, tokens, block), lambda i: (i // steps, 0, i % steps))

    def out_spec(plane):
        return pl.BlockSpec(
            shape[:3] + (block,), lambda i: (0, 0, 0, jnp.clip(i - plane * steps, 0, steps - 1))
        )

    out = pl.pallas_call(
        functools.partial(sum_kernel, size=size, links=links, places=first_places(), steps=steps),
        grid=(planes * steps,),
        in_specs=[SMEM_SPEC, once(2, tokens, height), once(tokens, height), right_spec, right_spec],
        out_specs=[out_spec(plane) for plane in range(planes) for _ in range(4)],
        out_shape=[jax.ShapeDtypeStruct(shape, bf16) if outside else pltpu.HBM(shape, bf16)] * (4 * planes),
        scratch_shapes=[pltpu.VMEM((height, block), bf16)],
        compiler_params=params(22, "arbitrary"),
        cost_estimate=cost(4 * tokens * height * width * planes, 4 * planes * (height + tokens) * width),
        name="sum_rows",
    )(meta, *far(left, left_other), *(far(right, right_other) if outside else [right] + far(right_other)))
    return [[(out[k], out[k + 1]), (out[k + 2], out[k + 3])] for k in range(0, 4 * planes, 4)]


def fold_kernel(meta_ref, *refs, count, done, places):
    ins, outs = refs[: 4 * count], refs[4 * count :]
    for part in range(2):
        own = meta_ref[3 + 2 * done + part]
        start = 0
        for number in range(count):
            keep_ref, got_ref = ins[4 * number + 2 * part], ins[4 * number + 2 * part + 1]
            size, links, _, width = keep_ref.shape
            for place in range(size):
                for index in range(links // 2):
                    base = split_index(index, places[part])
                    for ref, value in ((outs[2 * part], own), (outs[2 * part + 1], 1 - own)):
                        link = base + value * (1 << places[part])
                        ref[place, index, :, start : start + width] = added(
                            keep_ref[place, link], got_ref[place, link]
                        )
            start += width


def fold_next(meta, blocks, done, near_by=False):
    size = blocks[0][0][0].shape[0]
    places = [left.index(bit) for left, bit in zip(bits_left(done), link_orders()[done])]
    flat = [array for block in blocks for pair in block for array in pair]
    shapes = []
    for part in range(2):
        _, links, rows, _ = blocks[0][part][0].shape
        width = sum(block[part][0].shape[3] for block in blocks)
        shapes += [(size, links // 2, rows, width)] * 2
    if any(shape[2] % 16 for shape in shapes):
        result = []
        for part in range(2):
            state = jnp.concatenate([added(*block[part]) for block in blocks], axis=3)
            result.append(halves(state, done, part))
        return result
    out = pl.pallas_call(
        functools.partial(fold_kernel, count=len(blocks), done=done, places=places),
        grid=(1,),
        in_specs=[SMEM_SPEC] + [once(*array.shape) for array in flat],
        out_specs=[fixed(*shape) for shape in shapes],
        out_shape=[jax.ShapeDtypeStruct(shape, bf16) if near_by else pltpu.HBM(shape, bf16) for shape in shapes],
        compiler_params=params(16, "arbitrary"),
        cost_estimate=cost(0, 3 * sum(array.size for array in flat)),
        name="fold",
    )(meta, *(flat if near_by else far(*flat)))
    return [(out[0], out[1]), (out[2], out[3])]


def finish_kernel(meta_ref, m0, m1, g0, g1, w_ref, out_ref, norm_ref, *rest, padded, links):
    step = pl.program_id(0)
    mine = (step < 2) == (meta_ref[2] == 0)
    first = step % 2 == 0
    down_refs, rows_ref = rest[:-1], rest[-1]
    for source, own, even in ((m0, True, True), (m1, True, False), (g0, False, True), (g1, False, False)):

        @pl.when((mine == own) & (first == even))
        def _(source=source):
            rows_ref[...] = source[...]

    value = rows_ref[...].astype(f32)
    hidden = out_ref.shape[1] // 2
    out_ref[:, :hidden] = value[:, :hidden]
    out_ref[:, hidden:] = value[:, padded : padded + hidden]
    sums = jnp.sum(out_ref[...] * w_ref[...].astype(f32), axis=1, keepdims=True)
    norm_ref[0] = jnp.broadcast_to(sums, (sums.shape[0], LANES)).T[:1]
    if down_refs:
        (down_ref,) = down_refs
        height = value.shape[0] // links
        tiles = (value.shape[1] - 2 * padded) // LANES

        def put(core, part):
            for link in range(links):
                for tile in range(tiles):
                    top = (part * tiles + tile) * height
                    if top < down_ref.shape[0]:
                        lane = (core * links + link) * LANES
                        start = 2 * padded + tile * LANES
                        down_ref[top : top + height, lane : lane + LANES] = value[
                            link * height : (link + 1) * height, start : start + LANES
                        ]

        for number in range(4):
            pl.when(step == number)(functools.partial(put, number // 2, number % 2))


def finish_call(meta, parts, w_in, padded, shard, model):
    rows, columns = w_in.shape
    quarter, width = parts[0].shape
    links = 1 << link_count()
    height = quarter // links
    fast = fits(shard, model // 2 // links, height)
    out = pl.pallas_call(
        functools.partial(finish_kernel, padded=padded, links=links),
        grid=(4,),
        in_specs=[SMEM_SPEC]
        + [once(quarter, width)] * 4
        + [pl.BlockSpec((quarter, columns), lambda i: (i, 0))],
        out_specs=[
            pl.BlockSpec((quarter, columns), lambda i: (i, 0)),
            pl.BlockSpec((1, 1, quarter), lambda i: (i, 0, 0)),
        ]
        + [fixed(shard, model)] * fast,
        out_shape=[jax.ShapeDtypeStruct((rows, columns), f32), jax.ShapeDtypeStruct((4, 1, quarter), f32)]
        + [jax.ShapeDtypeStruct((shard, model), f32)] * fast,
        scratch_shapes=[pltpu.VMEM((quarter, width), bf16)],
        compiler_params=params(30, "arbitrary"),
        cost_estimate=cost(4 * rows * columns, 10 * rows * columns),
        name="finish",
    )(meta, *far(*parts, w_in))
    if fast:
        return out
    mine, got = [
        jnp.stack([part[:, 2 * padded :] for part in pair]).reshape(1, 2, links, height, -1)
        for pair in (parts[:2], parts[2:])
    ]
    whole = jnp.moveaxis(in_order(mine, got, 0, 0), 2, 1).reshape(2 * links, shard, -1)
    return out[0], out[1], jnp.transpose(whole, (1, 0, 2)).reshape(shard, model).astype(f32)


def last_kernel(*refs):
    k0, g0, k1, g1, out_ref = refs
    cut = k0.shape[2]
    for place in range(k0.shape[0]):
        out_ref[place, :cut, :] = added(k0[place, 0], g0[place, 0])
        out_ref[place, cut:, :] = added(k1[place, 0], g1[place, 0])


def fold_last(parts, near_by=False):
    (k0, g0), (k1, g1) = parts
    size, _, cut, width = k0.shape
    rows = cut + k1.shape[2]
    if cut % 16 or k1.shape[2] % 16:
        return jnp.concatenate([added(k0, g0)[:, 0], added(k1, g1)[:, 0]], axis=1)
    return pl.pallas_call(
        last_kernel,
        grid=(1,),
        in_specs=[once(*array.shape) for array in (k0, g0, k1, g1)],
        out_specs=fixed(size, rows, width),
        out_shape=jax.ShapeDtypeStruct((size, rows, width), bf16),
        compiler_params=params(16, "arbitrary"),
        cost_estimate=cost(0, 6 * size * rows * width),
        name="fold_last",
    )(*((k0, g0, k1, g1) if near_by else far(k0, g0, k1, g1)))


def middle_back_kernel(
    meta_ref, gu_ref, own1_ref, p0, p1, p2, p3, own2_ref, q0, q1, q2, q3, out_own_ref, r0, r1, r2, r3,
    s0, s1, s2, s3, middle_ref, upstream_ref, valid_ref, gains_ref, grad_ref, branch_ref, att_ref,
    acc, first_ref, second_ref, out_ref,
):
    step = pl.program_id(0)
    assemble(meta_ref, first_ref, own1_ref, (p0, p1, p2, p3))
    assemble(meta_ref, second_ref, own2_ref, (q0, q1, q2, q3))
    total = dot_nt(gu_ref[0], first_ref[...]) + dot_nt(gu_ref[1], second_ref[...])

    @pl.when(step == 0)
    def _():
        acc[...] = total
        assemble_two(meta_ref, out_ref, out_own_ref, (r0, r1, r2, r3), (s0, s1, s2, s3))

    @pl.when(step > 0)
    def _():
        acc[...] += total

    @pl.when(step == pl.num_programs(0) - 1)
    def _():
        for top in range(0, acc.shape[0], 128):
            rows = slice(top, top + 128)
            scaled, inverse = normalized(middle_ref[rows, :])
            grad = upstream_ref[rows, :].astype(f32) + norm_back(
                acc[rows, :], gains_ref[1:2, :], scaled, inverse
            )
            grad_ref[rows, :] = grad
            branch = (grad * valid_ref[rows, :]).astype(bf16)
            branch_ref[rows, :] = branch
            att_ref[rows, :] = dot_nt(branch, out_ref[...]).astype(bf16)


def middle_back_call(
    meta, grad_hidden, owns, parts, out_own, middle, upstream, valid, gains, block
):
    rows, width = middle.shape
    slab = owns[0].shape[0]
    hidden = grad_hidden.shape[2]
    steps = hidden // block
    whole = fixed(rows, width)
    own = pl.BlockSpec((slab, block), lambda i: (0, i))
    flat_low = jax.ShapeDtypeStruct((rows, width), bf16)
    return pl.pallas_call(
        middle_back_kernel,
        grid=(hidden // block,),
        in_specs=[SMEM_SPEC, pl.BlockSpec((2, rows, block), lambda i: (0, 0, i)), own]
        + part_specs(parts, block, lambda i: i)
        + [own]
        + part_specs(parts, block, lambda i: i + steps)
        + [once(slab, width)]
        + stretch_specs(parts, 2 * hidden, block)
        + [whole, whole, once(rows, 1), once(8, width)],
        out_specs=[whole, whole, whole],
        out_shape=[pltpu.HBM((rows, width), f32), flat_low, flat_low],
        scratch_shapes=[
            pltpu.VMEM((rows, width), f32),
            pltpu.VMEM((width, block), bf16),
            pltpu.VMEM((width, block), bf16),
            pltpu.VMEM((width, width), bf16),
        ],
        compiler_params=params(38, "arbitrary"),
        cost_estimate=cost(4 * rows * width * hidden, 4 * width * hidden + 4 * rows * hidden + 12 * rows * width),
        name="middle_back",
    )(meta, grad_hidden, *far(owns[0], *parts, owns[1], *parts, out_own, *parts, *parts, middle, upstream), valid, gains)


def input_back_kernel(
    meta_ref, gqkv_ref, own_ref, p0, p1, p2, p3, x_ref, grad_ref, gains_ref, out_ref, acc, whole_ref
):
    step = pl.program_id(0)
    assemble(meta_ref, whole_ref, own_ref, (p0, p1, p2, p3))
    total = dot_nt(gqkv_ref[...], whole_ref[...])

    @pl.when(step == 0)
    def _():
        acc[...] = total

    @pl.when(step > 0)
    def _():
        acc[...] += total

    @pl.when(step == pl.num_programs(0) - 1)
    def _():
        for top in range(0, acc.shape[0], 128):
            rows = slice(top, top + 128)
            scaled, inverse = normalized(x_ref[rows, :].astype(f32))
            out_ref[rows, :] = (
                grad_ref[rows, :] + norm_back(acc[rows, :], gains_ref[0:1, :], scaled, inverse)
            ).astype(bf16)


def input_back_call(meta, grad_joint, own, parts, x, grad_middle, gains):
    rows, width = x.shape
    slab = own.shape[0]
    block = width
    whole = fixed(rows, width)
    return pl.pallas_call(
        input_back_kernel,
        grid=(3 * width // block,),
        in_specs=[
            SMEM_SPEC,
            pl.BlockSpec((rows, block), lambda i: (0, i)),
            pl.BlockSpec((slab, block), lambda i: (0, i)),
        ]
        + part_specs(parts, block, lambda i: i)
        + [whole, whole, once(8, width)],
        out_specs=whole,
        out_shape=jax.ShapeDtypeStruct((rows, width), bf16),
        scratch_shapes=[pltpu.VMEM((rows, width), f32), pltpu.VMEM((width, block), bf16)],
        compiler_params=params(24, "arbitrary"),
        cost_estimate=cost(6 * rows * width * width, 6 * width * width + 14 * rows * width),
        name="input_back",
    )(meta, *far(grad_joint, own, *parts, x, grad_middle), gains)


def rope_tables(positions):
    halfway = HEAD_DIM // 2
    frequency = 10000.0 ** (-(2.0 * jnp.arange(halfway, dtype=f32)) / HEAD_DIM)
    angles = positions.astype(f32)[:, None] * frequency[None, :]
    cosine, sine = jnp.cos(angles), jnp.sin(angles)
    return (
        jnp.concatenate([cosine] * (LANES // halfway), axis=1),
        jnp.concatenate([-sine, sine] * (LANES // HEAD_DIM), axis=1),
    )


def on_device(inputs, cotangent, lengths, norm_first, w_qkv, w_out, norm_second, w_in, w_down):
    seqs, shard_rows, width = inputs.shape
    rows = seqs * shard_rows
    size = lax.axis_size("fsdp")
    me = lax.axis_index("fsdp")
    hidden = w_in.shape[1] // 2
    block = 896
    hidden_pad = -(-hidden // block) * block
    pad = hidden_pad - hidden
    steps = link_orders()
    near, far, middle_way = runs()

    gains = jnp.pad(jnp.stack([norm_first, norm_second]).T, ((0, 0), (0, LANES - 2)))
    came_one = turned_before(row_piece([w_qkv, gains]), range(1, size))
    own_in = [jnp.pad(w_in[:, half * hidden :][:, :hidden], ((0, 0), (0, pad))) for half in range(2)]
    piece_two = row_piece([own_in[0], own_in[1], w_out])
    piece_three = column_piece(w_down)
    first_row = me * shard_rows
    query_pos = first_row + jnp.arange(shard_rows, dtype=jnp.int32)
    rim_pos = first_row - WIN + jnp.arange(shard_rows + 2 * WIN, dtype=jnp.int32)
    cosine, sine = rope_tables(rim_pos)
    valid = (query_pos[None, :] < lengths[:, None]).astype(f32).reshape(rows, 1)
    bits = [bit_value(bit) for pair in steps for bit in pair]
    meta = jnp.stack([first_row, me, bit_value(0)] + bits).astype(jnp.int32)
    meta_rows = jnp.concatenate([first_row.astype(jnp.int32)[None], lengths.astype(jnp.int32)])
    x = inputs.reshape(rows, width)
    upstream = cotangent.reshape(rows, width)
    grad_result = (upstream.astype(f32) * valid).astype(bf16)
    grad_give = lax.dynamic_slice_in_dim(grad_result, (1 - bit_value(0)) * (width // 2), width // 2, 1)
    grad_other = flip(grad_give, 0)
    own_rows = slice(WIN, WIN + shard_rows)
    own_cosine, own_sine = cosine[own_rows], sine[own_rows]
    (
        came_one, piece_two, piece_three, own_in, gains, cosine, sine, own_cosine, own_sine, grad_result, grad_other,
        valid,
    ) = after(
        (
            came_one, piece_two, piece_three, own_in, gains, cosine, sine, own_cosine, own_sine, grad_result,
            grad_other, valid,
        )
    )

    one = widen(row_states(came_one), steps[0], 1)
    came_two = turned_before(piece_two, near)
    one, came_two, piece_two = after((one, came_two, piece_two))

    for bits in steps[1:]:
        one = widen(one, bits, 1)
    came_two = came_two + turned_before(piece_two, far)
    one, came_two, piece_two = after((one, came_two, piece_two))

    parts_one = row_parts(one)
    came_two = came_two + turned_before(piece_two, middle_way)
    normed_first, qkv, gains_all = qkv_call(meta, x, w_qkv, parts_one, gains, own_cosine, own_sine)
    by_seq = qkv.reshape(3, seqs, shard_rows, width)[1:]
    edge = (2, seqs * WIN, width)
    edge_up, edge_down = by_seq[:, :, :WIN].reshape(edge), by_seq[:, :, shard_rows - WIN :].reshape(edge)
    qkv, edge_up, edge_down, came_two, piece_three = after((qkv, edge_up, edge_down, came_two, piece_three))

    rim_down, rim_up = neighbours(edge_up, edge_down)
    two = widen(in_turn(row_states, came_two), steps[0], 1)
    rim_down, rim_up, two, piece_three = after((rim_down, rim_up, two, piece_three))

    for bits in steps[1:]:
        two = widen(two, bits, 1)
    came_three = turned_before(piece_three, range(1, size))
    attended, saved = attend_call(meta_rows, qkv, rim_up, rim_down, seqs)
    two, came_three, attended, normed_first = after((two, came_three, attended, normed_first))

    parts_two = row_parts(two)
    three = widen(column_states(came_three), steps[0], 1)
    first_other = flip(half_of(normed_first, False), 0)
    parts_two, three, attended, first_other = after((parts_two, three, attended, first_other))

    for bits in steps[1:]:
        three = widen(three, bits, 1)
    middle, normed_second, attended_split = out_call(
        meta, attended, w_out, parts_two, 2 * hidden_pad, block, x, valid, gains_all
    )
    second_other = flip(half_of(normed_second, False), 0)
    attended_other = flip(half_of(attended_split, False), 0)
    mixed, slope, act = gate_call(meta, normed_second, own_in, parts_two, block)
    three, mixed, slope, act, second_other, attended_other = after(
        (three, mixed, slope, act, second_other, attended_other)
    )

    parts_three = column_parts(three)
    parts_three, mixed, slope, act = after((parts_three, mixed, slope, act))

    mixed_other = flip(mixed, 0)
    grad_hidden, whole_down = gate_back_call(meta, grad_result, w_down, parts_three, slope, act, block)
    grad_hidden, mixed, mixed_other = after((grad_hidden, mixed, mixed_other))

    hidden_other = flip(grad_hidden, 0)
    down = down_call(meta, mixed, mixed_other, grad_result, grad_other, hidden, block)
    down, hidden_other, grad_hidden = after((down, hidden_other, grad_hidden))

    down = swap(down, 0)
    one, two = sum_call(meta, normed_second, second_other, grad_hidden, hidden_other, block)
    down, one, two, grad_hidden = after((down, one, two, grad_hidden))

    one = swap(one, 0)
    for done in range(1, len(steps)):
        down = swap(fold_next(meta, [down], done), done)
    grad_middle, grad_branch, grad_att = middle_back_call(
        meta, grad_hidden, own_in, parts_two, w_out, middle, upstream, valid, gains_all, block
    )
    one, two, grad_branch, grad_att, down = after((one, two, grad_branch, grad_att, down))

    two = swap(two, 0)
    for done in range(1, len(steps)):
        one = swap(fold_next(meta, [one], done), done)
    down_slots = fold_last(down)
    down_came = turned_slots(down_slots, near)
    grad_q, grad_k, grad_v, edge_up, edge_down = attend_back_call(
        qkv, rim_up, rim_down, saved, grad_att, cosine, sine, seqs
    )
    one, two, edge_up, edge_down, grad_q, grad_branch, down_slots, down_came = after(
        (one, two, edge_up, edge_down, grad_q, grad_branch, down_slots, down_came)
    )

    def spread_start(owned):
        ones = (1,) * link_count()
        cut = owned.shape[0] // 2
        return [part.reshape(ones + part.shape) for part in (owned[:cut], owned[cut:])]

    def spread_end(states):
        mine = jnp.stack([state.reshape((-1,) + state.shape[-2:]) for state in states])
        return in_order(mine[None], flip(mine, 0)[None], 0, 0)

    from_next, from_before = neighbours(edge_up, edge_down)
    branch_other = flip(grad_branch, 0)
    two, branch_other = after((two, branch_other))
    for done in range(1, len(steps)):
        two = swap(fold_next(meta, [two], done), done)
    (outs,) = sum_call(meta, attended_split, attended_other, grad_branch[None], branch_other[None], width // 2)
    one_slots = fold_last(one)
    from_next, from_before, two, one_slots, outs = after((from_next, from_before, two, one_slots, outs))

    def with_edges(own, plane):
        own = own.reshape(seqs, shard_rows, width)
        before = from_before[plane].reshape(seqs, WIN, width).astype(f32)
        later = from_next[plane].reshape(seqs, WIN, width).astype(f32)
        rest = ((0, 0), (0, shard_rows - WIN), (0, 0))
        own = own + jnp.pad(before, rest) + jnp.pad(later, (rest[0], rest[1][::-1], rest[2]))
        return own.reshape(rows, width).astype(bf16)

    outs = swap(outs, 0)
    down_came = down_came + turned_slots(down_slots, far) + turned_slots(down_slots, middle_way)
    grad_joint = jnp.concatenate([grad_q, with_edges(grad_k, 0), with_edges(grad_v, 1)], axis=1)
    joint_other = flip(grad_joint, 0)
    (last,) = sum_call(meta, normed_first, first_other, grad_joint[None], joint_other[None], width, True)
    two_slots = fold_last(two)
    last, grad_joint, outs, one_slots, two_slots, down_came, down_slots = after(
        (last, grad_joint, outs, one_slots, two_slots, down_came, down_slots)
    )

    last = swap(last, 0)
    one_came = turned_slots(one_slots, range(1, size))
    grad_inputs = input_back_call(meta, grad_joint, w_qkv, parts_one, x, grad_middle, gains_all)
    last, grad_inputs, one_came, one_slots, two_slots, down_came, down_slots, mixed = after(
        (last, grad_inputs, one_came, one_slots, two_slots, down_came, down_slots, mixed)
    )

    last = [last, outs]
    for done in range(1, len(steps)):
        last = [swap(fold_next(meta, last, done, True), done)]
    two_came = turned_slots(two_slots, range(1, size))
    owned = [slot_sum(one_slots, one_came), slot_sum(down_slots, down_came)]
    result = jnp.dot(mixed, whole_down, preferred_element_type=f32)
    output = (middle + valid * result).astype(bf16)
    last, two_came, two_slots, owned, output = after((last, two_came, two_slots, owned, output))

    last_slots = fold_last(last[0], True)
    last_came = turned_slots(last_slots, near) + turned_slots(last_slots, far)
    spread_in = widen(
        spread_start(jnp.concatenate([owned[0], slot_sum(two_slots, two_came), owned[1]], axis=1)), steps[0], 0
    )
    last_came, spread_in, last_slots = after((last_came, spread_in, last_slots))

    last_came = last_came + turned_slots(last_slots, middle_way)
    for bits in steps[1:]:
        spread_in = widen(spread_in, bits, 0)
    last_came, spread_in, last_slots = after((last_came, spread_in, last_slots))

    spread_last = widen(spread_start(slot_sum(last_slots, last_came)), steps[0], 0)
    in_parts = [state.reshape((-1, state.shape[-1])) for state in spread_in]
    in_parts = in_parts + [flip(part, 0) for part in in_parts]
    spread_last, in_parts = after((spread_last, in_parts))

    for bits in steps[1:]:
        spread_last = widen(spread_last, bits, 0)
    grad_in, grad_second, grad_down = finish_call(meta, in_parts, w_in, hidden_pad, hidden // size, width)
    spread_last, grad_in, grad_second, grad_down = after((spread_last, grad_in, grad_second, grad_down))

    grad_second = grad_second.reshape(-1) / norm_second.astype(f32)
    grad_last = spread_end(spread_last)
    grad_last = grad_last.reshape(-1, grad_last.shape[-1])
    grad_qkv = grad_last[:, : 3 * width].astype(f32)
    grad_out = grad_last[:, 3 * width :].astype(f32)
    grad_first = jnp.sum(grad_qkv * w_qkv.astype(f32), axis=1) / norm_first.astype(f32)
    return (
        output.reshape(inputs.shape),
        grad_inputs.reshape(inputs.shape),
        grad_first,
        grad_qkv,
        grad_out,
        grad_second,
        grad_in,
        grad_down,
    )


def solution(mesh):
    in_specs = (
        P("rep", "fsdp", None),
        P("rep", "fsdp", None),
        P("rep"),
        P("fsdp"),
        P("fsdp", None),
        P("fsdp", None),
        P("fsdp"),
        P("fsdp", None),
        P("fsdp", None),
    )
    out_specs = (
        P("rep", "fsdp", None),
        P("rep", "fsdp", None),
        P("fsdp"),
        P("fsdp", None),
        P("fsdp", None),
        P("fsdp"),
        P("fsdp", None),
        P("fsdp", None),
    )
    return jax.shard_map(
        on_device, mesh=mesh, in_specs=in_specs, out_specs=out_specs, check_vma=False
    )
```
